32 devices in a mesh: rep: 4 (over x, core), shard: 8 (over z, y).
Axes of the slice: x: 2, y: 2, z: 4, core: 2. Of those that a mesh axis runs over, the one named last changes fastest.
Arguments:
- tokens: bfloat16 [32, 1024, 1152], P(('rep', 'shard')), may hold values from -6 to 6
- cotangent: bfloat16 [32, 1024, 1152], P(('rep', 'shard'))
- segments: int32 [32, 1024], P(('rep', 'shard')), may hold values from 0 to 4, as said below
- positions: int32 [32, 1024], P(('rep', 'shard')), may hold values from 0 to 783, as said below
- wide_master: float32 [3, 1152, 3072], P(None, 'shard'), may hold values from -0.1875 to 0.1875
- square_master: float32 [2, 1152, 1152], P(None, 'shard')
- key_value_master: float32 [2, 1152, 384], P(None, 'shard'), may hold values from -0.1875 to 0.1875
- wide_moment: float32 [3, 1152, 3072], P(None, 'shard'), may hold values from -16 to 16
- square_moment: float32 [2, 1152, 1152], P(None, 'shard'), may hold values from -10 to 10
- key_value_momentum: float32 [2, 1152, 384], P(None, 'shard'), may hold values from -28 to 28
- wide_error: float32 [4, 3, 1152, 3072], P('rep', None, 'shard'), may hold values from -256 to 256
- square_error: float32 [4, 2, 1152, 1152], P('rep', None, 'shard'), may hold values from -160 to 160
- key_value_error: float32 [4, 2, 1152, 384], P('rep', None, 'shard'), may hold values from -448 to 448
- wide_factor: float32 [3, 8, 3072], replicated, may hold values from -6 to 6
- square_factor: float32 [2, 8, 1152], replicated, may hold values from -6 to 6
- key_value_factor: float32 [2, 8, 384], replicated, may hold values from -6 to 6
- norm_gains: float32 [2, 1152], P(None, 'shard')
- gain_moment: float32 [2, 1152], P(None, 'shard'), may hold values from -256 to 256
Outputs:
- output: bfloat16 [32, 1024, 1152], P(('rep', 'shard'))
- input_grad: bfloat16 [32, 1024, 1152], P(('rep', 'shard'))
- wide_new: float32 [3, 1152, 3072], P(None, 'shard')
- square_new: float32 [2, 1152, 1152], P(None, 'shard')
- narrow_new: float32 [2, 1152, 384], P(None, 'shard')
- wide_moment_new: float32 [3, 1152, 3072], P(None, 'shard')
- square_moment_new: float32 [2, 1152, 1152], P(None, 'shard')
- narrow_moment_new: float32 [2, 1152, 384], P(None, 'shard')
- wide_error_new: float32 [4, 3, 1152, 3072], P('rep', None, 'shard')
- square_error_new: float32 [4, 2, 1152, 1152], P('rep', None, 'shard')
- narrow_error_new: float32 [4, 2, 1152, 384], P('rep', None, 'shard')
- wide_factor_new: float32 [3, 8, 3072], replicated
- square_factor_new: float32 [2, 8, 1152], replicated
- narrow_factor_new: float32 [2, 8, 384], replicated
- gains_new: float32 [2, 1152], P(None, 'shard')
- gain_moment_new: float32 [2, 1152], P(None, 'shard')
The draws below stay inside these ranges and needn't reach their ends.
Inputs may be any that keep to these rules, and one draw needn't show every extreme that they name: `segments`: within each row the number starts at 0 and rises by one at each new document; each row holds 5 documents of 60 or more tokens. `positions`: counts from 0 at the first token of each document; some row holds a document of 1024 - (5 - 1) * 60 tokens.
All inputs are finite; a program needn't handle non-finite values.
Results may differ from the reference program's by a relative error of at most 0.02.
The reference program's roundings to bfloat16 on the way count: a program that leaves them out, or rounds other values in their place, can miss the bound.
Values may be sent and summed in bfloat16 or wider, within the bound.
No kernel may reach another device: no remote copies, remote signals or barrier semaphores. Data moves between devices by JAX's collectives and lax.ppermute only.
A program may use at most 448 MiB of HBM per device.

```python
import jax
import jax.numpy as jnp
from jax import lax

MODEL_WIDTH = 1152
QUERY_HEADS = 18
KEY_VALUE_HEADS = 6
HEAD_SIZE = 64
FF = 3072
COMPRESS_RANK = 8
PACKED_ROW = 1024
DOCS = 5
MIN_DOC = 60
ROWS = 32
N_REP = 4
N_SHARD = 8


def document_layout(key):
    leftover = PACKED_ROW - DOCS * MIN_DOC
    cut_points = jnp.sort(jax.random.randint(key, (ROWS, DOCS - 1), 0, leftover + 1), axis=-1).astype(jnp.int32)
    chosen = jax.random.randint(jax.random.fold_in(key, 1), (), 0, ROWS).astype(jnp.int32)
    row_ids = jnp.arange(ROWS, dtype=jnp.int32)
    cut_points = jnp.where((row_ids == chosen)[:, None], jnp.zeros_like(cut_points), cut_points)
    boundary = jnp.concatenate([jnp.zeros((ROWS, 1), jnp.int32), cut_points, jnp.full((ROWS, 1), leftover, jnp.int32)], axis=-1)
    lengths = MIN_DOC + boundary[:, 1:] - boundary[:, :-1]
    doc_ends = jnp.cumsum(lengths, axis=-1)
    offsets = jnp.arange(PACKED_ROW, dtype=jnp.int32)
    passed = (offsets[None, :, None] >= doc_ends[:, None, :DOCS - 1]).astype(jnp.int32)
    segment = jnp.sum(passed, axis=-1).astype(jnp.int32)
    position = offsets[None, :] - jnp.sum(passed * lengths[:, None, :DOCS - 1], axis=-1)
    return (segment, position.astype(jnp.int32))


def draw_segments(key, part):
    segment, position = document_layout(key)
    return segment


def draw_positions(key, part):
    segment, position = document_layout(key)
    return position


def draw_cotangent(key, part):
    key = jax.random.fold_in(key, 7)
    ramp = jnp.arange(MODEL_WIDTH, dtype=jnp.float32) / (MODEL_WIDTH - 1)
    base = jax.random.normal(key, (ROWS, PACKED_ROW, MODEL_WIDTH), jnp.float32)
    scale = 0.6 + 1.2 * ramp
    return (base * scale).astype(jnp.bfloat16)


def draw_norm_gains(key, part):
    key = jax.random.fold_in(key, 5)
    ramp = jnp.arange(MODEL_WIDTH, dtype=jnp.float32) / (MODEL_WIDTH - 1)
    rough = jax.random.uniform(key, (2, MODEL_WIDTH), jnp.float32, 0.8, 1.25)
    return (0.6 + 1.2 * ramp) * rough


def draw_square_master(key, part):
    key = jax.random.fold_in(key, 11)
    base = jax.random.normal(key, (2, MODEL_WIDTH, QUERY_HEADS * HEAD_SIZE), jnp.float32)
    scale = jnp.array([MODEL_WIDTH ** (-0.5), max(QUERY_HEADS * HEAD_SIZE // 32, 1) ** (-0.5)], jnp.float32)
    return base * scale[:, None, None]


def steps_of(rng, dims, cuts, low, top_value):
    factor_of = 1.0
    for dim, shards_of in cuts:
        steps = jax.random.uniform(jax.random.fold_in(jax.random.fold_in(rng, 6), dim), (shards_of,), jnp.float32, low / len(cuts), top_value / len(cuts))
        factor_of = factor_of * jnp.repeat(jnp.exp(steps), dims[dim] // shards_of).reshape((-1,) + (1,) * (len(dims) - 1 - dim))
    return factor_of


def normal_values(own_key, extent, spread, limit, pieces=(), held_as=jnp.bfloat16):
    loudness = steps_of(own_key, extent, pieces, -0.22, 0.18) if pieces else 1.0
    entries = jax.random.normal(own_key, extent, jnp.float32) * spread * loudness
    return jnp.minimum(jnp.maximum(entries, -limit), limit).astype(held_as)


def setup_inputs(seed: int = 0) -> dict:
    seeds = jax.random.split(jax.random.key(seed), 19)
    return {
        "tokens": normal_values(seeds[0], (ROWS, PACKED_ROW, MODEL_WIDTH), 1.0, 6.0, ((0, 32),)),
        "cotangent": draw_cotangent(jax.random.fold_in(seeds[18], 71), 0),
        "segments": draw_segments(jax.random.fold_in(seeds[18], 71), 0),
        "positions": draw_positions(jax.random.fold_in(seeds[18], 71), 0),
        "wide_master": normal_values(seeds[4], (3, MODEL_WIDTH, FF), MODEL_WIDTH ** -0.5, 0.1875, ((1, 8),), jnp.float32),
        "square_master": draw_square_master(jax.random.fold_in(seeds[18], 71), 0),
        "key_value_master": normal_values(seeds[6], (2, MODEL_WIDTH, KEY_VALUE_HEADS * HEAD_SIZE), MODEL_WIDTH ** -0.5, 0.1875, ((1, 8),), jnp.float32),
        "wide_moment": normal_values(seeds[7], (3, MODEL_WIDTH, FF), (0.75 * (PACKED_ROW * N_SHARD * COMPRESS_RANK) ** 0.5 * (MODEL_WIDTH * N_REP) ** -0.5), 16.0, ((1, 8),), jnp.float32),
        "square_moment": normal_values(seeds[8], (2, MODEL_WIDTH, QUERY_HEADS * HEAD_SIZE), (0.45 * (PACKED_ROW * N_SHARD * COMPRESS_RANK) ** 0.5 * (MODEL_WIDTH * N_REP) ** -0.5), 10.0, ((1, 8),), jnp.float32),
        "key_value_momentum": normal_values(seeds[9], (2, MODEL_WIDTH, KEY_VALUE_HEADS * HEAD_SIZE), (1.2 * (PACKED_ROW * N_SHARD * COMPRESS_RANK) ** 0.5 * (MODEL_WIDTH * N_REP) ** -0.5), 28.0, ((1, 8),), jnp.float32),
        "wide_error": normal_values(seeds[10], (N_REP, 3, MODEL_WIDTH, FF), (0.5 * (PACKED_ROW * N_SHARD) ** 0.5), 256.0, ((0, 4), (2, 8)), jnp.float32),
        "square_error": normal_values(seeds[11], (N_REP, 2, MODEL_WIDTH, QUERY_HEADS * HEAD_SIZE), (0.3 * (PACKED_ROW * N_SHARD) ** 0.5), 160.0, ((0, 4), (2, 8)), jnp.float32),
        "key_value_error": normal_values(seeds[12], (N_REP, 2, MODEL_WIDTH, KEY_VALUE_HEADS * HEAD_SIZE), (0.8 * (PACKED_ROW * N_SHARD) ** 0.5), 448.0, ((0, 4), (2, 8)), jnp.float32),
        "wide_factor": normal_values(seeds[13], (3, COMPRESS_RANK, FF), 1.0, 6.0, (), jnp.float32),
        "square_factor": normal_values(seeds[14], (2, COMPRESS_RANK, QUERY_HEADS * HEAD_SIZE), 1.0, 6.0, (), jnp.float32),
        "key_value_factor": normal_values(seeds[15], (2, COMPRESS_RANK, KEY_VALUE_HEADS * HEAD_SIZE), 1.0, 6.0, (), jnp.float32),
        "norm_gains": draw_norm_gains(jax.random.fold_in(seeds[18], 71), 0),
        "gain_moment": normal_values(seeds[17], (2, MODEL_WIDTH), ((PACKED_ROW * N_SHARD) ** 0.5 * N_REP ** -0.5), 256.0, ((1, 8),), jnp.float32),
    }


eps_norm = 1e-05
theta_base = 10000.0
decay_rate = 0.9
rate_wide = 0.03
rate_square = 0.1
rate_narrow = 0.02
rate_gains = 0.01
mask_fill = -1e+30
highest = lax.Precision.HIGHEST

@jax.custom_vjp
def lowered_precision(v):
    return lax.optimization_barrier(v.astype(jnp.bfloat16)).astype(jnp.float32)

@jax.custom_vjp
def lowered_pullback(v):
    return v

def low_keep(v):
    return (lowered_precision(v), None)

def low_pass(kept, grad):
    return (grad,)

def back_keep(v):
    return (v, None)

def back_low(kept, grad):
    return (lowered_precision(grad),)
lowered_precision.defvjp(low_keep, low_pass)
lowered_pullback.defvjp(back_keep, back_low)

def normed(value_heads, gain):
    return value_heads * lax.rsqrt(lax.optimization_barrier(jnp.mean(value_heads * value_heads, axis=-1, keepdims=True)) + eps_norm) * gain

def rotary_tables(position, width):
    halfway = width // 2
    inverse = theta_base ** (-2.0 * jnp.arange(halfway, dtype=jnp.float32) / width)
    angles = position.astype(jnp.float32)[:, None] * inverse[None, :]
    return (jnp.cos(angles), jnp.sin(angles))

def apply_rotation(value_heads, cosine_table, sine_table):
    halfway = value_heads.shape[-1] // 2
    first_half = value_heads[..., :halfway]
    second_half = value_heads[..., halfway:]
    cos_wide = cosine_table[:, None, :]
    sin_wide = sine_table[:, None, :]
    return jnp.concatenate([first_half * cos_wide - second_half * sin_wide, second_half * cos_wide + first_half * sin_wide], axis=-1)

def matrix_product(left_side, right_side):
    return jnp.dot(left_side, right_side, precision=highest)

def layer(hidden_in, weights, segment, position):
    wide_w, square_w, key_value_weight, gain_w = weights
    packed_row_count = hidden_in.shape[0]
    query_groups = QUERY_HEADS // KEY_VALUE_HEADS
    cosine_table, sine_table = rotary_tables(position, HEAD_SIZE)
    normalized_input = lowered_precision(normed(hidden_in, gain_w[0]))
    query_heads = lowered_pullback(matrix_product(normalized_input, square_w[0])).reshape(packed_row_count, QUERY_HEADS, HEAD_SIZE)
    query_heads = lowered_precision(apply_rotation(query_heads, cosine_table, sine_table)).reshape(packed_row_count, KEY_VALUE_HEADS, query_groups, HEAD_SIZE)
    rotated_keys = lowered_pullback(matrix_product(normalized_input, key_value_weight[0])).reshape(packed_row_count, KEY_VALUE_HEADS, HEAD_SIZE)
    rotated_keys = lowered_precision(apply_rotation(rotated_keys, cosine_table, sine_table))
    value_heads = lowered_precision(lowered_pullback(matrix_product(normalized_input, key_value_weight[1]))).reshape(packed_row_count, KEY_VALUE_HEADS, HEAD_SIZE)
    scores = lowered_pullback(jnp.einsum('qagd,kad->agqk', query_heads, rotated_keys, precision=highest) * 0.125)
    places = jnp.arange(packed_row_count)
    allowed = (segment[:, None] == segment[None, :]) & (places[:, None] >= places[None, :])
    scores = jnp.where(allowed, scores, mask_fill)
    prob_low = lowered_precision(jax.nn.softmax(scores, axis=-1))
    attended = jnp.einsum('agqk,kad->qagd', prob_low, value_heads, precision=highest).reshape(packed_row_count, QUERY_HEADS * HEAD_SIZE)
    attended = lowered_precision(lowered_pullback(attended))
    residual = hidden_in + lowered_pullback(jnp.einsum('tn,dn->td', attended, square_w[1], precision=highest))
    normed_mid = lowered_precision(normed(residual, gain_w[1]))
    gate = lowered_pullback(matrix_product(normed_mid, wide_w[0]))
    upward = lowered_pullback(matrix_product(normed_mid, wide_w[1]))
    hidden = lowered_precision(jax.nn.silu(gate) * upward)
    return residual + lowered_pullback(jnp.einsum('tf,df->td', hidden, wide_w[2], precision=highest))

def compress(group_mats, errors, factor, master, moment, rate):
    mixed = group_mats + errors
    left_factor = jnp.einsum('ekdn,krn->kdr', mixed, factor, precision=highest)
    gram = jnp.einsum('kdr,kds->krs', left_factor, left_factor, precision=highest)
    chol = jnp.linalg.cholesky(gram)
    basis = lax.linalg.triangular_solve(chol, left_factor, left_side=False, lower=True, transpose_a=True)
    factor_new = jnp.einsum('kdr,ekdn->krn', basis, mixed, precision=highest) / N_REP
    approx = jnp.einsum('kdr,krn->kdn', basis, factor_new, precision=highest)
    error_new = mixed - approx[None]
    moment_new = decay_rate * moment + approx
    master_new = master - rate * moment_new
    return (master_new, moment_new, error_new, factor_new)

def reference(tokens, cotangent, segments, positions, wide_master, square_master, key_value_master, wide_moment, square_moment, key_value_momentum, wide_error, square_error, key_value_error, wide_factor, square_factor, key_value_factor, norm_gains, gain_moment):
    weights = (lowered_precision(wide_master), lowered_precision(square_master), lowered_precision(key_value_master), lowered_precision(norm_gains))
    zero_grads = jax.tree.map(jnp.zeros_like, weights)
    grouped = (tokens.reshape(N_REP, N_SHARD, PACKED_ROW, MODEL_WIDTH), cotangent.reshape(N_REP, N_SHARD, PACKED_ROW, MODEL_WIDTH), segments.reshape(N_REP, N_SHARD, PACKED_ROW), positions.reshape(N_REP, N_SHARD, PACKED_ROW))

    def row_step(totals, row_data):
        row_tokens, row_cot, row_seg, row_pos = row_data

        def forward(hidden_in, params):
            return layer(hidden_in, params, row_seg, row_pos)
        result, pullback = jax.vjp(forward, row_tokens.astype(jnp.float32), weights)
        grad_in, grad_weights = pullback(row_cot.astype(jnp.float32))
        totals = jax.tree.map(jnp.add, totals, grad_weights)
        return (totals, (result.astype(jnp.bfloat16), grad_in.astype(jnp.bfloat16)))

    def group_step(carry_none, group_data):
        totals, row_outs = lax.scan(row_step, zero_grads, group_data)
        return (carry_none, (totals, row_outs))
    _, (group_grads, row_results) = lax.scan(group_step, jnp.zeros((), jnp.float32), grouped)
    output = row_results[0].reshape(ROWS, PACKED_ROW, MODEL_WIDTH)
    input_grad = row_results[1].reshape(ROWS, PACKED_ROW, MODEL_WIDTH)
    wide_new, wide_moment_new, wide_error_new, wide_factor_new = compress(group_grads[0], wide_error, wide_factor, wide_master, wide_moment, rate_wide)
    square_new, square_moment_new, square_error_new, square_factor_new = compress(group_grads[1], square_error, square_factor, square_master, square_moment, rate_square)
    narrow_new, narrow_moment_new, narrow_error_new, narrow_factor_new = compress(group_grads[2], key_value_error, key_value_factor, key_value_master, key_value_momentum, rate_narrow)
    gain_grad = lax.optimization_barrier(jnp.sum(group_grads[3], axis=0)) / N_REP
    gain_moment_new = decay_rate * gain_moment + gain_grad
    gains_new = norm_gains - rate_gains * gain_moment_new
    return (output, input_grad, wide_new, square_new, narrow_new, wide_moment_new, square_moment_new, narrow_moment_new, wide_error_new, square_error_new, narrow_error_new, wide_factor_new, square_factor_new, narrow_factor_new, gains_new, gain_moment_new)
```

```python
import functools

import jax
import jax.numpy as jnp
from jax import lax
from jax.experimental import pallas as pl
from jax.experimental.pallas import tpu as pltpu
from jax.sharding import PartitionSpec as P

QUERY_HEADS = 18
KEY_VALUE_HEADS = 6
HEAD_SIZE = 64
PAIRS = KEY_VALUE_HEADS // 2


eps_norm = 1e-05
theta_base = 10000.0
decay_rate = 0.9
rate_wide = 0.03
rate_square = 0.1
rate_narrow = 0.02
rate_gains = 0.01
mask_fill = -1e30
highest = lax.Precision.HIGHEST


def normed(value_heads, gain):
    return (
        value_heads
        * lax.rsqrt(jnp.mean(value_heads * value_heads, axis=-1, keepdims=True) + eps_norm)
        * gain
    )


def rotary_tables(position, width):
    halfway = width // 2
    inverse = theta_base ** (-2.0 * jnp.arange(halfway, dtype=jnp.float32) / width)
    angles = position.astype(jnp.float32)[:, None] * inverse[None, :]
    return (jnp.cos(angles), jnp.sin(angles))


BLOCK_ROWS = 256
VMEM_BYTES = 56 * 1024 * 1024


def partner_lanes(values):
    lane = lax.broadcasted_iota(jnp.int32, values.shape, 1)
    return jnp.where(
        lane % HEAD_SIZE < HEAD_SIZE // 2,
        pltpu.roll(values, 128 - HEAD_SIZE // 2, 1),
        pltpu.roll(values, HEAD_SIZE // 2, 1),
    )


def project_kernel(
    order_ref, x_ref, gain_ref, w_ref, cos_ref, sin_ref, out_ref, turned_ref, scratch_ref
):
    x = x_ref[...].astype(jnp.float32)
    scale = lax.rsqrt(jnp.mean(x * x, axis=-1, keepdims=True) + eps_norm)
    low = (x * scale * gain_ref[...]).astype(jnp.bfloat16)
    scratch_ref[...] = low.astype(jnp.float32).T
    share = scratch_ref.shape[0] // order_ref.shape[0]
    parts = [
        scratch_ref[pl.ds(pl.multiple_of(order_ref[p] * share, 8), share), :]
        for p in range(order_ref.shape[0])
    ]
    turned_ref[...] = jnp.concatenate(parts, axis=0).astype(jnp.bfloat16)
    cos, sin = cos_ref[...], sin_ref[...]
    for first in range(0, out_ref.shape[1], 640):
        got = jnp.dot(low, w_ref[:, first : first + 640], preferred_element_type=jnp.float32)
        for at in range(0, 640, 128):
            piece = got[:, at : at + 128]
            if at < 512:
                piece = piece * cos + partner_lanes(piece) * sin
            out_ref[:, first + at : first + at + 128] = piece.astype(jnp.bfloat16)


def project_qkv(order, x, gain, weights, cos, sin):
    rows, width = x.shape
    columns = weights.shape[1]
    block = min(BLOCK_ROWS, rows)
    return pl.pallas_call(
        project_kernel,
        grid_spec=pltpu.PrefetchScalarGridSpec(
            num_scalar_prefetch=1,
            grid=(rows // block,),
            in_specs=[
                pl.BlockSpec((block, width), lambda i, order: (i, 0)),
                pl.BlockSpec((1, width), lambda i, order: (0, 0)),
                pl.BlockSpec((width, columns), lambda i, order: (0, 0)),
                pl.BlockSpec((block, 128), lambda i, order: (i, 0)),
                pl.BlockSpec((block, 128), lambda i, order: (i, 0)),
            ],
            out_specs=[
                pl.BlockSpec((block, columns), lambda i, order: (i, 0)),
                pl.BlockSpec((width, block), lambda i, order: (0, i)),
            ],
            scratch_shapes=[pltpu.VMEM((width, block), jnp.float32)],
        ),
        out_shape=[
            jax.ShapeDtypeStruct((rows, columns), jnp.bfloat16),
            jax.ShapeDtypeStruct((width, rows), jnp.bfloat16),
        ],
        compiler_params=pltpu.CompilerParams(vmem_limit_bytes=VMEM_BYTES),
        cost_estimate=pl.CostEstimate(
            flops=2 * rows * width * columns,
            bytes_accessed=2 * (rows * width * 2 + rows * columns + width * columns),
            transcendentals=0,
        ),
    )(order, x, gain, weights, cos, sin)


def spread_heads(pair, spread_ref):
    wide = pair.astype(jnp.float32)
    turned = pltpu.roll(wide, HEAD_SIZE, 1)
    low_half = lax.broadcasted_iota(jnp.int32, wide.shape, 1) < HEAD_SIZE
    zero = jnp.zeros_like(wide)
    spread_ref[0] = jnp.where(low_half, wide, zero).astype(jnp.bfloat16)
    spread_ref[1] = jnp.where(low_half, zero, turned).astype(jnp.bfloat16)
    spread_ref[2] = jnp.where(low_half, turned, zero).astype(jnp.bfloat16)
    spread_ref[3] = jnp.where(low_half, zero, wide).astype(jnp.bfloat16)


def mask_bias(position, start, keys):
    rows = position.shape[0]
    row = lax.broadcasted_iota(jnp.int32, (rows, keys), 0) + start
    column = lax.broadcasted_iota(jnp.int32, (rows, keys), 1)
    allowed = (column <= row) & (column >= row - position)
    return jnp.where(allowed, 0.0, mask_fill)


def across(left, right):
    return lax.dot_general(
        left, right, (((1,), (1,)), ((), ())), preferred_element_type=jnp.float32
    )


def forward_kernel(qkv_ref, pos_ref, out_ref, log_ref, key_ref, value_ref):
    step = pl.program_id(1)
    block = out_ref.shape[0]

    @pl.when(step == 0)
    def _():
        spread_heads(qkv_ref[:, 384:512], key_ref)
        spread_heads(qkv_ref[:, 512:640], value_ref)

    for place in range(qkv_ref.shape[0] // block):

        @pl.when(step == place)
        def _(place=place):
            start = place * block
            keys = start + block
            bias = mask_bias(pos_ref[...], start, keys)
            lane = lax.broadcasted_iota(jnp.int32, (block, 128), 1)
            logs = jnp.zeros((block, 128), jnp.float32)
            for g in range(3):
                query = qkv_ref[start:keys, 128 * g : 128 * g + 128] * 0.125
                total = jnp.zeros((block, 128), jnp.float32)
                for e in range(2):
                    head = 2 * g + e
                    which = 2 * (head // 3) + e
                    scores = across(query, key_ref[which, :keys, :]) + bias
                    top = jnp.max(scores, axis=-1, keepdims=True)
                    raised = jnp.exp(scores - top)
                    row_total = jnp.sum(raised, axis=-1, keepdims=True)
                    low = (raised * (1.0 / row_total)).astype(jnp.bfloat16)
                    total += jnp.dot(
                        low, value_ref[which, :keys, :], preferred_element_type=jnp.float32
                    )
                    logs = jnp.where(lane == head, top + jnp.log(row_total), logs)
                out_ref[:, 128 * g : 128 * g + 128] = total.astype(jnp.bfloat16)
            log_ref[0] = logs


def attend_forward(qkv, position):
    rows = qkv.shape[0]
    pairs = qkv.shape[1] // 640
    block = min(BLOCK_ROWS, rows)
    return pl.pallas_call(
        forward_kernel,
        grid=(pairs, rows // block),
        in_specs=[
            pl.BlockSpec((rows, 640), lambda j, i: (0, j)),
            pl.BlockSpec((block, 1), lambda j, i: (i, 0)),
        ],
        out_specs=[
            pl.BlockSpec((block, 384), lambda j, i: (i, j)),
            pl.BlockSpec((1, block, 128), lambda j, i: (j, i, 0)),
        ],
        out_shape=[
            jax.ShapeDtypeStruct((rows, 384 * pairs), jnp.bfloat16),
            jax.ShapeDtypeStruct((pairs, rows, 128), jnp.float32),
        ],
        scratch_shapes=[
            pltpu.VMEM((4, rows, 128), jnp.bfloat16),
            pltpu.VMEM((4, rows, 128), jnp.bfloat16),
        ],
        compiler_params=pltpu.CompilerParams(vmem_limit_bytes=VMEM_BYTES),
        cost_estimate=pl.CostEstimate(
            flops=20 * pairs * rows * rows * 128,
            bytes_accessed=8 * rows * 640 * pairs,
            transcendentals=6 * pairs * rows * rows,
        ),
    )(qkv, position)


def backward_kernel(
    qkv_ref, d_ref, log_ref, pos_ref, cos_ref, sin_ref, out_ref, key_ref, value_ref, dk_ref, dv_ref
):
    step = pl.program_id(0)
    block = d_ref.shape[0]
    blocks = qkv_ref.shape[0] // block

    @pl.when(step == 0)
    def _():
        spread_heads(qkv_ref[:, 384:512], key_ref)
        spread_heads(qkv_ref[:, 512:640], value_ref)
        dk_ref[...] = jnp.zeros_like(dk_ref)
        dv_ref[...] = jnp.zeros_like(dv_ref)

    for place in range(blocks):

        @pl.when(step == place)
        def _(place=place):
            start = place * block
            keys = start + block
            bias = mask_bias(pos_ref[...], start, keys)
            logs = log_ref[0]
            cos, sin = cos_ref[start:keys, :], sin_ref[start:keys, :]
            for g in range(3):
                query = qkv_ref[start:keys, 128 * g : 128 * g + 128] * 0.125
                d_out = d_ref[:, 128 * g : 128 * g + 128]
                query_turned = query.astype(jnp.float32).T.astype(jnp.bfloat16)
                d_turned = d_out.astype(jnp.float32).T.astype(jnp.bfloat16)
                total = jnp.zeros((block, 128), jnp.float32)
                for e in range(2):
                    head = 2 * g + e
                    which = 2 * (head // 3) + e
                    at = HEAD_SIZE * (head // 3)
                    key = key_ref[which, :keys, :]
                    scores = across(query, key) + bias
                    prob = jnp.exp(scores - logs[:, head : head + 1])
                    d_prob = across(d_out, value_ref[which, :keys, :])
                    delta = jnp.sum(prob * d_prob, axis=-1, keepdims=True)
                    d_scores = (prob * (d_prob - delta)).astype(jnp.bfloat16)
                    half = slice(HEAD_SIZE * e, HEAD_SIZE * e + HEAD_SIZE)
                    dv_ref[at : at + HEAD_SIZE, :keys] += jnp.dot(
                        d_turned[half], prob.astype(jnp.bfloat16), preferred_element_type=jnp.float32
                    )
                    dk_ref[at : at + HEAD_SIZE, :keys] += jnp.dot(
                        query_turned[half], d_scores, preferred_element_type=jnp.float32
                    )
                    total += jnp.dot(d_scores, key, preferred_element_type=jnp.float32)
                total = total * 0.125
                total = total * cos - partner_lanes(total) * sin
                out_ref[start:keys, 128 * g : 128 * g + 128] = total.astype(jnp.bfloat16)

    @pl.when(step == blocks - 1)
    def _():
        d_key = dk_ref[...].T
        d_key = d_key * cos_ref[...] - partner_lanes(d_key) * sin_ref[...]
        out_ref[:, 384:512] = d_key.astype(jnp.bfloat16)
        out_ref[:, 512:640] = dv_ref[...].T.astype(jnp.bfloat16)


def attend_backward(qkv, d_attended, logs, position, cos, sin, pair):
    rows = qkv.shape[0]
    block = min(BLOCK_ROWS, rows)
    return pl.pallas_call(
        backward_kernel,
        grid=(rows // block,),
        in_specs=[
            pl.BlockSpec((rows, 640), lambda i: (0, pair)),
            pl.BlockSpec((block, 384), lambda i: (i, pair)),
            pl.BlockSpec((1, block, 128), lambda i: (pair, i, 0)),
            pl.BlockSpec((block, 1), lambda i: (i, 0)),
            pl.BlockSpec((rows, 128), lambda i: (0, 0)),
            pl.BlockSpec((rows, 128), lambda i: (0, 0)),
        ],
        out_specs=pl.BlockSpec((rows, 640), lambda i: (0, 0)),
        out_shape=jax.ShapeDtypeStruct((rows, 640), jnp.bfloat16),
        scratch_shapes=[
            pltpu.VMEM((4, rows, 128), jnp.bfloat16),
            pltpu.VMEM((4, rows, 128), jnp.bfloat16),
            pltpu.VMEM((128, rows), jnp.float32),
            pltpu.VMEM((128, rows), jnp.float32),
        ],
        compiler_params=pltpu.CompilerParams(vmem_limit_bytes=VMEM_BYTES),
        cost_estimate=pl.CostEstimate(
            flops=50 * rows * rows * 128,
            bytes_accessed=8 * rows * 640,
            transcendentals=6 * rows * rows,
        ),
    )(qkv, d_attended, logs, position, cos, sin)


def turn_kernel(order_ref, rows_ref, out_ref, turned_ref):
    turned_ref[...] = rows_ref[...].astype(jnp.float32).T
    owners = order_ref.shape[0]
    share = turned_ref.shape[0] // owners
    parts = [
        turned_ref[pl.ds(pl.multiple_of(order_ref[p] * share, 8), share), :] for p in range(owners)
    ]
    out_ref[...] = jnp.concatenate(parts, axis=0).astype(jnp.bfloat16)


def turn_rows(rows, order):
    count, model = rows.shape
    block = min(BLOCK_ROWS, count)
    return pl.pallas_call(
        turn_kernel,
        grid_spec=pltpu.PrefetchScalarGridSpec(
            num_scalar_prefetch=1,
            grid=(count // block,),
            in_specs=[pl.BlockSpec((block, model), lambda i, order: (i, 0))],
            out_specs=pl.BlockSpec((model, block), lambda i, order: (0, i)),
            scratch_shapes=[pltpu.VMEM((model, block), jnp.float32)],
        ),
        out_shape=jax.ShapeDtypeStruct((model, count), jnp.bfloat16),
        compiler_params=pltpu.CompilerParams(vmem_limit_bytes=VMEM_BYTES),
        cost_estimate=pl.CostEstimate(
            flops=0, bytes_accessed=4 * count * model, transcendentals=0
        ),
    )(order, rows)


def mlp_kernel(reps, first, slot_ref, place_ref, mid_ref, d_ref, *refs):
    del slot_ref
    mid_hbm, d_hbm = refs[:2]
    befores = refs[2 : 3 if first else 4]
    refs = refs[2 + len(befores) :]
    weight_hbm, refs = (refs[:1], refs[1:]) if place_ref.shape[0] == 1 else (refs[:2], refs[2:])
    away_ref, home_ref, result_ref, back_ref = refs[:4]
    weight_ref, mid_turned_ref, d_turned_ref, d_pair_ref, hidden_ref, weight_sem, sem = refs[4:]
    step = pl.program_id(0)
    count = mid_ref.shape[0]
    part = min(512, count)
    tile = hidden_ref.shape[1]
    half = away_ref.shape[1]

    wide = 3 * tile

    def load(i):
        if len(weight_hbm) == 1:
            pltpu.make_async_copy(
                weight_hbm[0].at[i], weight_ref.at[i], weight_sem.at[i]
            ).start()
            return
        ref, at = weight_hbm[2 * i // reps], i % (reps // 2)
        owners, share = ref.shape[:2]
        for a in range(owners):
            pltpu.make_async_copy(
                ref.at[place_ref[a], :, wide * at : wide * at + wide],
                weight_ref.at[i, share * a : share * a + share, :],
                weight_sem.at[i],
            ).start()

    sums = [pltpu.make_async_copy(befores[0], result_ref, sem.at[0])]
    if not first:
        sums.append(pltpu.make_async_copy(befores[1], back_ref, sem.at[1]))
    turned = [
        pltpu.make_async_copy(mid_hbm, mid_turned_ref, sem.at[2]),
        pltpu.make_async_copy(d_hbm, d_turned_ref, sem.at[3]),
    ]

    @pl.when(step == 0)
    def _():
        load(0)
        for copy in sums + turned:
            copy.start()
        for i in range(1, reps):
            load(i)
        if first:
            back_ref[...] = jnp.zeros_like(back_ref)

    for i in range(reps):

        @pl.when(step == i)
        def _(i=i):
            pltpu.make_async_copy(weight_ref.at[i], weight_ref.at[i], weight_sem.at[i]).wait()

    @pl.when(step == 0)
    def _():
        for copy in sums:
            copy.wait()

    @pl.loop(0, count // part)
    def _(t):
        rows = pl.ds(pl.multiple_of(t * part, part), part)
        pair_w = weight_ref[step, :, : 2 * tile]
        down_w = weight_ref[step, :, 2 * tile :]
        pair = jnp.dot(mid_ref[rows, :], pair_w, preferred_element_type=jnp.float32)
        d_hidden = jnp.dot(d_ref[rows, :], down_w, preferred_element_type=jnp.float32)
        gate, up = pair[:, :tile], pair[:, tile:]
        sig = jax.nn.sigmoid(gate)
        silu = gate * sig
        hidden = (silu * up).astype(jnp.bfloat16)
        hidden_ref[rows, :] = hidden
        d_gate = d_hidden * up * (sig * (1.0 + gate * (1.0 - sig)))
        d_pair_ref[rows, :tile] = d_gate.astype(jnp.bfloat16)
        d_pair_ref[rows, tile:] = (d_hidden * silu).astype(jnp.bfloat16)
        back_ref[rows, :] += across(d_pair_ref[rows, :], pair_w)
        result_ref[rows, :] += across(hidden, down_w)

    @pl.when(step == 0)
    def _():
        for copy in turned:
            copy.wait()

    for at, out_ref in ((0, away_ref), (half, home_ref)):
        pair = jnp.dot(
            mid_turned_ref[at : at + half, :], d_pair_ref[...], preferred_element_type=jnp.float32
        )
        out_ref[0] = pair[:, :tile].astype(jnp.bfloat16)
        out_ref[1] = pair[:, tile:].astype(jnp.bfloat16)
        out_ref[2] = jnp.dot(
            d_turned_ref[at : at + half, :], hidden_ref[...], preferred_element_type=jnp.float32
        ).astype(jnp.bfloat16)


def mlp_part(reps, slots, places, mid, d_out, mid_turned, d_turned, weights, result, back):
    count, model = mid.shape
    tile = weights[0].shape[2] // (3 if len(weights) == 1 else 3 * (reps // 2))
    units = tile * reps
    half = model // 2
    first = back is None
    befores = [result] if first else [result, back]

    def once(shape):
        return pl.BlockSpec(shape, lambda i, slots, places: (0, 0), pipeline_mode=pl.Buffered(1))

    anywhere = pl.BlockSpec(memory_space=pl.ANY)
    return pl.pallas_call(
        functools.partial(mlp_kernel, reps, first),
        grid_spec=pltpu.PrefetchScalarGridSpec(
            num_scalar_prefetch=2,
            grid=(reps,),
            in_specs=[once((count, model))] * 2 + [anywhere] * (2 + len(befores) + len(weights)),
            out_specs=[
                pl.BlockSpec((3, half, tile), lambda i, slots, places: (0, 0, slots[i])),
                pl.BlockSpec((3, half, tile), lambda i, slots, places: (0, 0, slots[i])),
                once((count, model)),
                once((count, model)),
            ],
            scratch_shapes=[
                pltpu.VMEM((reps, model, 3 * tile), jnp.bfloat16),
                pltpu.VMEM((model, count), jnp.bfloat16),
                pltpu.VMEM((model, count), jnp.bfloat16),
                pltpu.VMEM((count, 2 * tile), jnp.bfloat16),
                pltpu.VMEM((count, tile), jnp.bfloat16),
                pltpu.SemaphoreType.DMA((reps,)),
                pltpu.SemaphoreType.DMA((4,)),
            ],
        ),
        out_shape=[
            jax.ShapeDtypeStruct((3, half, units), jnp.bfloat16),
            jax.ShapeDtypeStruct((3, half, units), jnp.bfloat16),
            jax.ShapeDtypeStruct((count, model), jnp.float32),
            jax.ShapeDtypeStruct((count, model), jnp.float32),
        ],
        compiler_params=pltpu.CompilerParams(vmem_limit_bytes=VMEM_BYTES),
        cost_estimate=pl.CostEstimate(
            flops=18 * count * model * units,
            bytes_accessed=2 * (4 * count * model + 6 * model * units) + 16 * count * model,
            transcendentals=count * units,
        ),
    )(slots, places, mid, d_out, mid_turned, d_turned, *befores, *weights)


def assemble(rows, mine, other, places, core, low, high):
    owners = mine[0].shape[0]
    widths = [m.shape[2] for m in mine]
    count = len(mine)

    def kernel(place_ref, core_ref, *refs):
        del place_ref
        out_ref = refs[-1]
        for own in range(2):

            @pl.when(core_ref[0] == own)
            def _(own=own):
                at = 0
                for i in range(count):
                    for half in range(2):
                        ref = refs[i] if half == own else refs[count + i]
                        first, last = max(low, at), min(high, at + widths[i])
                        if first < last:
                            out_ref[0, :, first - low : last - low] = ref[
                                0, :, first - at : last - at
                            ]
                        at += widths[i]

    def spec(width):
        return pl.BlockSpec((1, rows, width), lambda a, place, core: (place[a], 0, 0))

    out = pl.pallas_call(
        kernel,
        grid_spec=pltpu.PrefetchScalarGridSpec(
            num_scalar_prefetch=2,
            grid=(owners,),
            in_specs=[spec(w) for w in widths] * 2,
            out_specs=pl.BlockSpec((1, rows, high - low), lambda a, place, core: (a, 0, 0)),
        ),
        out_shape=jax.ShapeDtypeStruct((owners, rows, high - low), jnp.bfloat16),
        compiler_params=pltpu.CompilerParams(vmem_limit_bytes=VMEM_BYTES),
        cost_estimate=pl.CostEstimate(
            flops=0, bytes_accessed=8 * owners * rows * sum(widths), transcendentals=0
        ),
    )(places, core, *mine, *other)
    return out.reshape(owners * rows, high - low)


def exact_dot(left, right, contract):
    return lax.dot_general(
        left, right, (contract, ((), ())), precision=highest, preferred_element_type=jnp.float32
    )


def mix_kernel(layout, count, flag_ref, *refs):
    sums, refs = refs[: 3 * count], refs[3 * count :]
    errors, refs = refs[: len(layout)], refs[len(layout) :]
    factors, refs = refs[: len(layout)], refs[len(layout) :]
    mixed, left_ref = refs[: len(layout)], refs[len(layout)]
    stays = flag_ref[0] == 1
    for m, pieces in enumerate(layout):
        at = 0
        for which, first, last in pieces:
            away, home, moved = (
                sums[3 * which + k][..., first:last].astype(jnp.float32) for k in range(3)
            )
            width = last - first
            where = (..., slice(at, at + width))
            total = away + jnp.where(stays, home, moved)
            total = total.reshape(total.shape[-2:])
            error = errors[m][where]
            error = error.reshape(error.shape[-2:])
            mixed[m][where] = (total + error).reshape(mixed[m].shape[:-1] + (width,))
            at += width
        rows = mixed[m][...].reshape(mixed[m].shape[-2:])
        factor = factors[m][...].reshape(factors[m].shape[-2:])
        left = exact_dot(factor, rows, ((1,), (1,)))
        left_ref[8 * m : 8 * m + 8, :] = left


def mix_wide(flag, parts, error, factor):
    count, rows, third = parts[0][0].shape
    number = len(parts)
    columns = third * number
    arrays = [a for part in parts for a in part]

    def kernel(flag_ref, *refs):
        error_ref, factor_ref, mixed_ref, left_ref = refs[3 * number :]
        step = pl.program_id(1)

        @pl.when(step == 0)
        def _():
            left_ref[...] = jnp.zeros_like(left_ref)

        for p in range(number):

            @pl.when(step == p)
            def _(p=p):
                away, home, moved = (refs[3 * p + k][0].astype(jnp.float32) for k in range(3))
                mixed = away + jnp.where(flag_ref[0] == 1, home, moved) + error_ref[0, 0]
                mixed_ref[0] = mixed
                left_ref[...] += exact_dot(factor_ref[0], mixed, ((1,), (1,)))

    return pl.pallas_call(
        kernel,
        grid_spec=pltpu.PrefetchScalarGridSpec(
            num_scalar_prefetch=1,
            grid=(count, number),
            in_specs=[pl.BlockSpec((1, rows, third), lambda i, k, flag: (i, 0, 0))] * len(arrays)
            + [
                pl.BlockSpec((1, 1, rows, third), lambda i, k, flag: (0, i, 0, k)),
                pl.BlockSpec((1, 8, third), lambda i, k, flag: (i, 0, k)),
            ],
            out_specs=[
                pl.BlockSpec((1, rows, third), lambda i, k, flag: (i, 0, k)),
                pl.BlockSpec((8, rows), lambda i, k, flag: (i, 0)),
            ],
        ),
        out_shape=[
            jax.ShapeDtypeStruct((count, rows, columns), jnp.float32),
            jax.ShapeDtypeStruct((8 * count, rows), jnp.float32),
        ],
        compiler_params=pltpu.CompilerParams(vmem_limit_bytes=VMEM_BYTES),
        cost_estimate=pl.CostEstimate(
            flops=96 * count * rows * columns,
            bytes_accessed=14 * count * rows * columns,
            transcendentals=0,
        ),
    )(flag, *arrays, error, factor)


def in_vmem(count):
    return [pl.BlockSpec(memory_space=pltpu.VMEM)] * count


def mix_rest(flag, parts, layout, errors, factors):
    rows = errors[0].shape[0]
    arrays = [a for part in parts for a in part]
    return pl.pallas_call(
        functools.partial(mix_kernel, layout, len(parts)),
        in_specs=[pl.BlockSpec(memory_space=pltpu.SMEM)]
        + in_vmem(len(arrays) + len(errors) + len(factors)),
        out_specs=in_vmem(len(errors) + 1),
        out_shape=[jax.ShapeDtypeStruct(e.shape, jnp.float32) for e in errors]
        + [jax.ShapeDtypeStruct((8 * len(errors), rows), jnp.float32)],
        compiler_params=pltpu.CompilerParams(vmem_limit_bytes=VMEM_BYTES),
        cost_estimate=pl.CostEstimate(
            flops=96 * sum(e.size for e in errors),
            bytes_accessed=14 * sum(e.size for e in errors),
            transcendentals=0,
        ),
    )(flag, *arrays, *errors, *factors)


def contract_all(left, mixed, width, extra=None):
    def kernel(*refs):
        left_ref, out_ref = refs[0], refs[-1]
        out_ref[...] = jnp.zeros_like(out_ref)
        at, m = 0, 0
        for ref in refs[1 : 1 + len(mixed)]:
            for k in range(ref.shape[0] if len(ref.shape) == 3 else 1):
                rows = ref[k] if len(ref.shape) == 3 else ref[...]
                own = left_ref[8 * m : 8 * m + 8, :]
                out_ref[:, at : at + rows.shape[1]] = exact_dot(own, rows, ((1,), (0,)))
                at += rows.shape[1]
                m += 1
        for k in range(m):
            own = left_ref[8 * k : 8 * k + 8, :]
            out_ref[:, at : at + 8] = exact_dot(own, own, ((1,), (1,)))
            at += 128
        if extra is not None:
            out_ref[: extra.shape[0], at : at + extra.shape[1]] = refs[-2][...]

    more = [] if extra is None else [extra]
    return pl.pallas_call(
        kernel,
        in_specs=in_vmem(1 + len(mixed) + len(more)),
        out_specs=pl.BlockSpec(memory_space=pltpu.VMEM),
        out_shape=jax.ShapeDtypeStruct((8, width), jnp.float32),
        compiler_params=pltpu.CompilerParams(vmem_limit_bytes=VMEM_BYTES),
        cost_estimate=pl.CostEstimate(
            flops=96 * sum(m.size for m in mixed),
            bytes_accessed=4 * sum(m.size for m in mixed),
            transcendentals=0,
        ),
    )(left, *mixed, *more)


def eliminate(gram, rights):
    row = lax.broadcasted_iota(jnp.int32, (8, 1), 0)
    for j in range(8):
        scale = 1.0 / jnp.sqrt(gram[j : j + 1, j : j + 1])
        below = jnp.where(row > j, gram[:, j : j + 1] * scale, 0.0)
        done = []
        for right in [gram] + list(rights):
            top = right[j : j + 1, :] * scale
            done.append(jnp.where(row == j, top, right - below * top))
        gram, rights = done[0], done[1:]
    return rights


def finish_matrix(reps, rate, row, gram, left, mixed, moment, master):
    factor, basis = eliminate(gram[:, :8] * (1.0 / reps), [row, left])
    factor = factor * (1.0 / reps)
    approx = exact_dot(basis, factor, ((0,), (0,)))
    moment_new = decay_rate * moment + approx
    return factor, moment_new, master - rate * moment_new, mixed - approx


def finish_wide(reps, packed, gram_at, left, mixed, moment, master):
    count, rows, columns = mixed.shape

    def kernel(row_ref, gram_ref, left_ref, mixed_ref, moment_ref, master_ref, *outs):
        new_ref, moment_new_ref, error_ref, factor_ref = outs
        factor_ref[0], moment_new_ref[0], new_ref[0], error_ref[0, 0] = finish_matrix(
            reps,
            rate_wide,
            row_ref[...],
            gram_ref[...],
            left_ref[...],
            mixed_ref[0],
            moment_ref[0],
            master_ref[0],
        )

    third = columns // 3
    whole = pl.BlockSpec((1, rows, third), lambda i, k: (i, 0, k))
    shape = jax.ShapeDtypeStruct((count, rows, columns), jnp.float32)
    return pl.pallas_call(
        kernel,
        grid=(count, 3),
        in_specs=[
            pl.BlockSpec((8, third), lambda i, k: (0, 3 * i + k)),
            pl.BlockSpec((8, 128), lambda i, k: (0, gram_at // 128 + i)),
            pl.BlockSpec((8, rows), lambda i, k: (i, 0)),
            whole,
            whole,
            whole,
        ],
        out_specs=[
            whole,
            whole,
            pl.BlockSpec((1, 1, rows, third), lambda i, k: (0, i, 0, k)),
            pl.BlockSpec((1, 8, third), lambda i, k: (i, 0, k)),
        ],
        out_shape=[
            shape,
            shape,
            jax.ShapeDtypeStruct((1, count, rows, columns), jnp.float32),
            jax.ShapeDtypeStruct((count, 8, columns), jnp.float32),
        ],
        compiler_params=pltpu.CompilerParams(vmem_limit_bytes=VMEM_BYTES),
        cost_estimate=pl.CostEstimate(
            flops=96 * count * rows * columns,
            bytes_accessed=24 * count * rows * columns,
            transcendentals=0,
        ),
    )(packed, packed, left, mixed, moment, master)


def finish_rest(reps, packs, lefts, mixed, where, states):
    groups = []
    at = 0
    for moment, _, rate in states:
        groups.append((at, moment.shape[0], rate))
        at += moment.shape[0]

    def kernel(*refs):
        pack_refs, refs = refs[: len(packs)], refs[len(packs) :]
        left_refs, refs = refs[: len(lefts)], refs[len(lefts) :]
        mixed_refs, refs = refs[: len(mixed)], refs[len(mixed) :]
        state_refs, outs = refs[: 2 * len(states)], refs[2 * len(states) :]
        for g, (first, count, rate) in enumerate(groups):
            new_ref, moment_new_ref, error_ref, factor_ref = outs[4 * g : 4 * g + 4]
            for k in range(count):
                pack, row_at, gram_at, left_at = where[first + k]
                rows = mixed_refs[first + k][...]
                (
                    factor_ref[k],
                    moment_new_ref[k],
                    new_ref[k],
                    error_ref[0, k],
                ) = finish_matrix(
                    reps,
                    rate,
                    pack_refs[pack][:, row_at : row_at + rows.shape[1]],
                    pack_refs[pack][:, gram_at : gram_at + 128],
                    left_refs[pack][left_at : left_at + 8, :],
                    rows,
                    state_refs[2 * g][k],
                    state_refs[2 * g + 1][k],
                )

    shapes = []
    for moment, _, _ in states:
        count, rows, columns = moment.shape
        shapes += [
            jax.ShapeDtypeStruct(moment.shape, jnp.float32),
            jax.ShapeDtypeStruct(moment.shape, jnp.float32),
            jax.ShapeDtypeStruct((1,) + moment.shape, jnp.float32),
            jax.ShapeDtypeStruct((count, 8, columns), jnp.float32),
        ]
    arrays = [a for state in states for a in state[:2]]
    return pl.pallas_call(
        kernel,
        in_specs=in_vmem(len(packs) + len(lefts) + len(mixed) + len(arrays)),
        out_specs=in_vmem(len(shapes)),
        out_shape=shapes,
        compiler_params=pltpu.CompilerParams(vmem_limit_bytes=VMEM_BYTES),
        cost_estimate=pl.CostEstimate(
            flops=96 * sum(m.size for m in mixed),
            bytes_accessed=24 * sum(m.size for m in mixed),
            transcendentals=0,
        ),
    )(*packs, *lefts, *mixed, *arrays)


def pack_wide(master, picks, groups, tile):
    count, rows, _ = master.shape
    number = picks.shape[0]

    def kernel(pick_ref, *refs):
        del pick_ref
        for group, out_ref in zip(groups, refs[number:]):
            at = 0
            for pick in group:
                for i in range(count):
                    out_ref[:, at : at + tile] = refs[pick][i].astype(jnp.bfloat16)
                    at += tile

    def spec(n):
        return pl.BlockSpec((count, rows, tile), lambda i, picks: (0, 0, picks[n]))

    shapes = [
        jax.ShapeDtypeStruct((rows, count * tile * len(group)), jnp.bfloat16) for group in groups
    ]
    return pl.pallas_call(
        kernel,
        grid_spec=pltpu.PrefetchScalarGridSpec(
            num_scalar_prefetch=1,
            grid=(1,),
            in_specs=[spec(n) for n in range(number)],
            out_specs=[pl.BlockSpec(s.shape, lambda i, picks: (0, 0)) for s in shapes],
        ),
        out_shape=shapes,
        compiler_params=pltpu.CompilerParams(vmem_limit_bytes=VMEM_BYTES),
        cost_estimate=pl.CostEstimate(
            flops=0, bytes_accessed=6 * number * count * rows * tile, transcendentals=0
        ),
    )(picks, *[master] * number)


def split_sum(home, got):
    shape = home.shape
    rows, columns = shape[-2:]
    lead = home.size // (rows * columns)
    half = rows // 2

    def kernel(home_ref, got_ref, away_ref, kept_ref):
        total = home_ref[0].astype(jnp.float32) + got_ref[0].astype(jnp.float32)
        away_ref[0] = total[:half].astype(jnp.bfloat16)
        kept_ref[0] = total[half:].astype(jnp.bfloat16)

    block = columns // 2 if columns % 256 == 0 else columns
    whole = pl.BlockSpec((1, rows, block), lambda i, j: (i, 0, j))
    part = pl.BlockSpec((1, half, block), lambda i, j: (i, 0, j))
    out = jax.ShapeDtypeStruct((lead, half, columns), jnp.bfloat16)
    away, kept = pl.pallas_call(
        kernel,
        grid=(lead, columns // block),
        in_specs=[whole, whole],
        out_specs=[part, part],
        out_shape=[out, out],
        compiler_params=pltpu.CompilerParams(vmem_limit_bytes=VMEM_BYTES),
        cost_estimate=pl.CostEstimate(
            flops=home.size, bytes_accessed=6 * home.size, transcendentals=0
        ),
    )(home.reshape(lead, rows, columns), got.reshape(lead, rows, columns))
    tail = (half, columns)
    return away.reshape(shape[:-2] + tail), kept.reshape(shape[:-2] + tail)


def out_kernel(owners, place_ref, core_ref, order_ref, att_ref, x_ref, gain_ref, *refs):
    halves, refs = refs[:4], refs[4:]
    residual_ref, mid_ref, mid_turned_ref, w_ref, turned_ref, sem = refs
    share = w_ref.shape[0] // owners

    @pl.when(pl.program_id(0) == 0)
    def _():
        for own in range(2):

            @pl.when(core_ref[0] == own)
            def _(own=own):
                spans = (
                    (halves[0 if own == 1 else 1], 384, 0, 128),
                    (halves[2 if own == 0 else 3], 0, 128, 512),
                    (halves[2 if own == 1 else 3], 0, 640, 512),
                )
                for ref, first, at, width in spans:
                    for a in range(owners):
                        pltpu.make_async_copy(
                            ref.at[place_ref[a], :, first : first + width],
                            w_ref.at[share * a : share * a + share, at : at + width],
                            sem.at[0],
                        ).start()

        pltpu.make_async_copy(w_ref, w_ref, sem.at[0]).wait()

    residual = x_ref[...].astype(jnp.float32) + across(att_ref[...], w_ref[...])
    residual_ref[...] = residual
    scale = lax.rsqrt(jnp.mean(residual * residual, axis=-1, keepdims=True) + eps_norm)
    mid = (residual * scale * gain_ref[...]).astype(jnp.bfloat16)
    mid_ref[...] = mid
    turned_ref[...] = mid.astype(jnp.float32).T
    parts = [
        turned_ref[pl.ds(pl.multiple_of(order_ref[p] * share, 8), share), :] for p in range(owners)
    ]
    mid_turned_ref[...] = jnp.concatenate(parts, axis=0).astype(jnp.bfloat16)


def project_out(places, core, order, attended, x, gain, halves):
    count, model = x.shape
    owners = order.shape[0]
    block = min(BLOCK_ROWS, count)
    rows = pl.BlockSpec((block, model), lambda i, *_: (i, 0))
    return pl.pallas_call(
        functools.partial(out_kernel, owners),
        grid_spec=pltpu.PrefetchScalarGridSpec(
            num_scalar_prefetch=3,
            grid=(count // block,),
            in_specs=[rows, rows, pl.BlockSpec((1, model), lambda i, *_: (0, 0))]
            + [pl.BlockSpec(memory_space=pl.ANY)] * 4,
            out_specs=[
                rows,
                rows,
                pl.BlockSpec((model, block), lambda i, *_: (0, i)),
                pl.BlockSpec((model, model), lambda i, *_: (0, 0)),
            ],
            scratch_shapes=[
                pltpu.VMEM((model, block), jnp.float32),
                pltpu.SemaphoreType.DMA((1,)),
            ],
        ),
        out_shape=[
            jax.ShapeDtypeStruct((count, model), jnp.float32),
            jax.ShapeDtypeStruct((count, model), jnp.bfloat16),
            jax.ShapeDtypeStruct((model, count), jnp.bfloat16),
            jax.ShapeDtypeStruct((model, model), jnp.bfloat16),
        ],
        compiler_params=pltpu.CompilerParams(vmem_limit_bytes=VMEM_BYTES),
        cost_estimate=pl.CostEstimate(
            flops=2 * count * model * model,
            bytes_accessed=12 * count * model + 4 * model * model,
            transcendentals=count,
        ),
    )(places, core, order, attended, x, gain, *halves)


class Grid:
    def __init__(self, mesh):
        self.reps = mesh.shape["rep"]
        self.shards = mesh.shape["shard"]
        self.core_bit = self.shards.bit_length() - 3
        stages = self.shards.bit_length() - 1
        self.order = [self.core_bit] + [b for b in range(stages) if b != self.core_bit]

    def swapped(self, rep, shard):
        bit = self.core_bit
        core = rep & 1
        turn = (shard >> bit) & 1
        return (rep - core + turn, shard - (turn << bit) + (core << bit))

    def flat(self, pair):
        return pair[0] * self.shards + pair[1]

    def every(self):
        return [(r, s) for r in range(self.reps) for s in range(self.shards)]

    def move(self, value, target):
        pairs = [(self.flat(p), self.flat(target(*p))) for p in self.every() if target(*p) != p]
        return lax.ppermute(value, ("rep", "shard"), pairs)

    def stays(self):
        return lax.axis_index("rep") % 2 == (lax.axis_index("shard") >> self.core_bit) % 2

    def swap_rows(self, value):
        return jnp.where(self.stays(), value, self.move(value, self.swapped))

    def partner(self, bit):
        def target(rep, shard):
            lr, ls = self.swapped(rep, shard)
            return self.swapped(lr, ls ^ (1 << bit))

        return target

    def last(self, bit):
        def target(rep, shard):
            lr, ls = self.swapped(rep, shard)
            return (lr, ls ^ (1 << bit))

        return target

    def flip_rep(self, bit):
        return lambda rep, shard: (rep ^ (1 << bit), shard)

    def flip_shard(self, bit):
        return lambda rep, shard: (rep, shard ^ (1 << bit))

    def doubling(self):
        return list(range(len(self.order)))[::-1]

    def places(self):
        out = [0] * self.shards
        for place in range(self.shards):
            distance = 0
            for k, bit in enumerate(self.doubling()):
                if (place >> k) & 1:
                    distance |= 1 << bit
            out[distance] = place
        return out

    def masks(self):
        count = len(self.order)
        out = []
        for place in range(self.shards):
            mask = 0
            for k, bit in enumerate(self.order):
                if not (place >> (count - 1 - k)) & 1:
                    mask |= 1 << bit
            out.append(mask)
        return out


def after(value, *others):
    return lax.optimization_barrier((value, others))[0]


def gather_pieces(grid, blocks):
    mine = []
    before = [None] * len(grid.order)
    for number, block in enumerate(blocks):
        held = block[None]
        for k, bit in enumerate(grid.doubling()):
            last = k == len(before) - 1
            if before[k] is not None:
                held = after(held, before[k])
            before[k] = grid.move(held, grid.flip_shard(bit))
            if not (last and number == len(blocks) - 1):
                held = jnp.concatenate([held, before[k]], axis=0)
        mine.append(held)
    return mine, before


class Sums:
    def __init__(self, grid, away, home):
        self.grid = grid
        self.stage = 0
        self.away, self.home = away, home
        self.send()

    def send(self):
        grid, bit = self.grid, self.grid.order[self.stage]
        if self.stage == len(grid.order) - 1:
            self.got = (grid.move(self.away, grid.last(bit)), grid.move(self.home, grid.swapped))
        else:
            self.got = grid.move(self.away, grid.partner(bit))

    def step(self, late, hold=False):
        self.got = after(self.got, late)
        self.away, self.home = split_sum(self.home, self.got)
        self.stage += 1
        if not hold:
            self.send()
        return (self.away, self.home)

    def join(self, other):
        self.away = jnp.concatenate([self.away, other.away], axis=-1)
        self.home = jnp.concatenate([self.home, other.home], axis=-1)
        self.send()

    def result(self, late):
        while self.stage < len(self.grid.order) - 1:
            self.step(late)
        return (self.got[0], self.home, self.got[1])


def butterfly(grid, value, moves):
    for move in moves:
        value = jax.tree.map(lambda v: v + grid.move(v, move), value)
    return value


def sum_all(grid, value, beside=None):
    rep = lax.axis_index("rep")
    bits = range(grid.reps.bit_length() - 1)
    pad = -value.shape[1] % (128 * grid.reps)
    columns = value.shape[1]
    value = jnp.pad(value, ((0, 0), (0, pad)))
    for bit in bits:
        half = value.shape[1] // 2
        upper = (rep >> bit) % 2 == 1
        low, high = value[:, :half], value[:, half:]
        got = grid.move(jnp.where(upper, low, high), grid.flip_rep(bit))
        value = jnp.where(upper, high, low) + got
    for bit in range(grid.shards.bit_length() - 1):
        value = value + grid.move(value, grid.flip_shard(bit))
    if beside is not None:
        value = after(value, beside)
    for bit in reversed(bits):
        got = grid.move(value, grid.flip_rep(bit))
        upper = (rep >> bit) % 2 == 1
        value = jnp.concatenate(
            [jnp.where(upper, got, value), jnp.where(upper, value, got)], axis=1
        )
    return value[:, :columns]


def shards(
    grid,
    tokens,
    cotangent,
    segments,
    positions,
    wide_master,
    square_master,
    key_value_master,
    wide_moment,
    square_moment,
    key_value_momentum,
    wide_error,
    square_error,
    key_value_error,
    wide_factor,
    square_factor,
    key_value_factor,
    norm_gains,
    gain_moment,
):
    reps, owners = grid.reps, grid.shards
    rep = lax.axis_index("rep")
    shard = lax.axis_index("shard")
    core = rep % 2
    turn = (shard >> grid.core_bit) % 2
    logical_shard = shard + (core - turn) * (1 << grid.core_bit)

    low_square = square_master.astype(jnp.bfloat16)
    low_narrow = key_value_master.astype(jnp.bfloat16)
    pieces = []
    for j in range(PAIRS):
        pieces.append(low_square[0, :, 384 * j : 384 * j + 384])
        pieces.append(low_narrow[0, :, 128 * j : 128 * j + 128])
        pieces.append(low_narrow[1, :, 128 * j : 128 * j + 128])
    low_attn = jnp.concatenate(pieces + [low_square[1]], axis=1)
    units = wide_master.shape[2] // 3

    position = grid.swap_rows(positions)[0]
    rows = low_attn.shape[0]
    tile = units // reps
    chained = 1 if rows % 16 == 0 else 0
    blocks = [low_attn[:, 1024 * i : 1024 * i + 1024] for i in range(3)]
    gain_row = norm_gains.astype(jnp.bfloat16).reshape(1, 2 * rows)
    gain_row = jnp.pad(gain_row, ((0, 15), (0, 512 - 2 * rows)))
    blocks[0] = jnp.concatenate([blocks[0], jnp.concatenate([gain_row] * 2, axis=1)], axis=0)
    blocks = [lax.dynamic_slice_in_dim(b, core * 512, 512, axis=1) for b in blocks]
    picks = [core * (reps // 2) + i for i in range(reps // 2)] if chained else []
    groups = [tuple(range(len(picks)))] if chained else []
    for k in range(chained, 3):
        groups.append((len(picks),))
        picks.append(reps * k + rep)
    cuts = list(pack_wide(wide_master, jnp.stack(picks).astype(jnp.int32), groups, tile))
    mine, gathering = gather_pieces(grid, blocks + cuts[:chained])
    other = [grid.move(held, grid.flip_rep(0)) for held in mine[:2]]
    places = jnp.array(grid.places(), jnp.int32)[jnp.arange(owners) ^ shard]
    cores = core[None]
    gain_w = mine[0][:, rows, : 2 * rows].reshape(owners, 2, rows)
    gain_w = jnp.take(gain_w, places, axis=0).transpose(1, 0, 2).reshape(2, -1).astype(jnp.float32)
    natural = jnp.arange(reps, dtype=jnp.int32)
    whole = jnp.zeros((1,), jnp.int32)
    moved_tokens = grid.move(after(tokens, gathering[1]), grid.swapped)
    tokens = jnp.where(grid.stays(), tokens, moved_tokens)[0]
    moved_out = grid.move(after(cotangent, moved_tokens), grid.swapped)
    model = gain_w.shape[1]
    columns = 640 * PAIRS
    qkv_w = assemble(rows, mine[:2], other[:2], places, cores, 0, columns)

    count = tokens.shape[0]
    hidden_in = tokens.astype(jnp.float32)
    gain_attn, gain_mlp = gain_w[0], gain_w[1]
    cos, sin = rotary_tables(position, HEAD_SIZE)
    cos = jnp.concatenate([cos] * 4, axis=1)
    sin = jnp.concatenate([-sin, sin] * 2, axis=1)
    place = position[:, None]
    order = jnp.array(grid.masks(), jnp.int32) ^ logical_shard

    tokens = after(tokens, mine[2])
    qkv, turned_in = project_qkv(order, tokens, gain_attn[None], qkv_w, cos, sin)
    if chained:
        held, got = after((mine[3], gathering[-1]), qkv)
        mine[3] = jnp.concatenate([held, got], axis=0)
        qkv = after(qkv, mine[3])
    else:
        mine[2] = jnp.concatenate([mine[2], gathering[-1]], axis=0)
    wide_parts = [None] * chained
    for k in range(chained, 3):
        part = after(cuts[k], mine[2:])
        part = lax.all_gather(part, ("rep", "shard"), axis=0, tiled=True)
        wide_parts.append((natural, whole, [part.reshape(reps, owners * rows, 3 * tile)]))
    mine[2] = after(mine[2], qkv)
    other += [grid.move(held, grid.flip_rep(0)) for held in mine[2:]]
    attended, logs = attend_forward(qkv, place)
    other[2:] = after(other[2:], attended)
    d_out = jnp.where(grid.stays(), cotangent, after(moved_out, attended))[0]
    if chained:
        slots = (natural + core * (reps // 2)) % reps
        wide_parts[0] = (slots, places, mine[3:] + other[3:])
        residual, normed_mid, turned_mid, out_w = project_out(
            places,
            cores,
            order,
            attended,
            tokens,
            gain_mlp[None],
            [mine[1], other[1], mine[2], other[2]],
        )
    else:
        out_w = assemble(rows, mine[1:3], other[1:3], places, cores, columns - 1024, 2048)
        residual = hidden_in + jnp.einsum(
            "tn,dn->td", attended, out_w, preferred_element_type=jnp.float32
        )
        normed_mid = normed(residual, gain_mlp).astype(jnp.bfloat16)
        turned_mid = turn_rows(normed_mid, order)
    turned_out = turn_rows(d_out, order)

    half = model // 2

    def weight_grad(turned, right):
        return Sums(
            grid,
            jnp.dot(turned[:half], right, preferred_element_type=jnp.float32).astype(jnp.bfloat16),
            jnp.dot(turned[half:], right, preferred_element_type=jnp.float32).astype(jnp.bfloat16),
        )

    wide_sums = []
    result, d_mid = residual, None
    for k in range(3):
        slots, where, weights = wide_parts[k]
        away, home, result, d_mid = mlp_part(
            reps, slots, where, normed_mid, d_out, turned_mid, turned_out, weights, result, d_mid
        )
        wide_sums.append(Sums(grid, away, home))
        for earlier in wide_sums[max(0, k - 2) : k]:
            d_mid, result = after((d_mid, result), earlier.step(away))
    result = grid.swap_rows(result.astype(jnp.bfloat16)[None])

    _, mid_back = jax.vjp(normed, residual, gain_mlp)
    d_residual, grad_gain_mlp = mid_back(d_mid)
    d_residual = d_residual + d_out.astype(jnp.float32)
    d_branch = d_residual.astype(jnp.bfloat16)
    d_attended = jnp.einsum(
        "td,dn->tn", d_branch, out_w, preferred_element_type=jnp.float32
    ).astype(jnp.bfloat16)
    out_sums = weight_grad(turn_rows(d_branch, order), attended)

    d_attended = after(d_attended, wide_sums[2].step(out_sums.away), wide_sums[0].got)
    d_stacks, pair_sums = [], []
    hold = len(grid.order) == 3
    for j in range(PAIRS):
        d_stack = attend_backward(qkv, d_attended, logs, place, cos, sin, j)
        d_stacks.append(d_stack)
        pair_sums.append(weight_grad(turned_in, d_stack))
        if j == 0:
            done = (wide_sums[1].step(d_stack), out_sums.step(d_stack), result)
        elif j == 1:
            done = (
                wide_sums[2].step(d_stack),
                out_sums.step(d_stack),
                pair_sums[0].step(d_stack),
                wide_sums[1].got,
            )
        else:
            done = (pair_sums[0].step(d_stack, hold), pair_sums[1].step(d_stack), out_sums.got)
        d_attended = after(d_attended, done, pair_sums[j].away)
        d_stacks = after(d_stacks, done, pair_sums[j].away)
    def back(j):
        return jnp.einsum(
            "tn,dn->td",
            d_stacks[j],
            qkv_w[:, 640 * j : 640 * j + 640],
            preferred_element_type=jnp.float32,
        )

    flag = grid.stays().astype(jnp.int32)[None]
    d_first = back(0) + back(1)
    d_stacks, wide_got = after(
        (d_stacks, wide_sums[2].got), pair_sums[2].step(d_first), pair_sums[1].step(d_first, hold)
    )
    wide_sums[2].got = wide_got
    spans = [(j, 0) for j in range(PAIRS)]
    late_sums = pair_sums
    if hold:
        pair_sums[0].join(pair_sums[1])
        spans = [(0, 0), (0, 640), (1, 0)]
        late_sums = [pair_sums[0], pair_sums[2]]
    mixed_wide, left_wide = mix_wide(
        flag, [part.result(d_first) for part in wide_sums], wide_error, wide_factor
    )
    mixed_out, left_out = mix_rest(
        flag,
        [out_sums.result(d_first)],
        [[(0, 0, model)]],
        [square_error[0, 1]],
        [square_factor[1]],
    )
    last_step = pair_sums[2].step(left_wide)
    d_stacks = after(d_stacks, last_step, left_out)
    d_normed_in = d_first + back(2)
    rep_moves = [grid.flip_rep(b) for b in range(reps.bit_length() - 1)]
    unit = 128 * reps
    left_early = butterfly(grid, jnp.concatenate([left_wide, left_out], axis=0), rep_moves)
    left_early = after(left_early, last_step)
    gram_early = 9 * units + model
    width = -(-(gram_early + 512) // unit) * unit
    early = contract_all(left_early, [mixed_wide, mixed_out], width)
    d_normed_in = after(d_normed_in, early)
    _, in_back = jax.vjp(normed, hidden_in, gain_attn)
    d_input, grad_gain_attn = in_back(d_normed_in)
    d_input = (d_input + d_residual).astype(jnp.bfloat16)
    early = sum_all(grid, early)
    late = d_input
    d_input = grid.swap_rows(d_input[None])
    narrow = 128 * PAIRS

    mixed_query, mixed_key, mixed_value, left_late = mix_rest(
        flag,
        [part.result(late) for part in late_sums],
        [
            [(which, at + first, at + last) for which, at in spans]
            for first, last in ((0, 384), (384, 512), (512, 640))
        ],
        [square_error[0, 0], key_value_error[0, 0], key_value_error[0, 1]],
        [square_factor[0], key_value_factor[0], key_value_factor[1]],
    )
    left_late = butterfly(grid, left_late, rep_moves)
    gram_late = columns
    gain_at = gram_late + 384
    width = -(-(gain_at + model) // unit) * unit
    gain_grad = jnp.stack([grad_gain_attn, grad_gain_mlp])
    mixed_late = [mixed_query, mixed_key, mixed_value]
    left_late = after(left_late, late)
    summed = contract_all(left_late, mixed_late, width, gain_grad)
    wide_new, wide_moment_new, wide_error_new, factor_wide = finish_wide(
        reps, early, gram_early, left_early, mixed_wide, wide_moment, wide_master
    )
    summed = butterfly(grid, summed, rep_moves + [grid.flip_shard(0)])
    summed = after(summed, wide_new)
    shard_moves = [grid.flip_shard(b) for b in range(1, owners.bit_length() - 1)]
    summed = butterfly(grid, summed, shard_moves)
    (
        square_new,
        square_moment_new,
        square_error_new,
        factor_square,
        narrow_new,
        narrow_moment_new,
        narrow_error_new,
        factor_narrow,
    ) = finish_rest(
        reps,
        [summed, early],
        [left_late, left_early],
        [mixed_query, mixed_out, mixed_key, mixed_value],
        [
            (0, 0, gram_late, 0),
            (1, 9 * units, gram_early + 384, 24),
            (0, model, gram_late + 128, 8),
            (0, model + narrow, gram_late + 256, 16),
        ],
        [
            (square_moment, square_master, rate_square),
            (key_value_momentum, key_value_master, rate_narrow),
        ],
    )
    gain_total = lax.dynamic_slice_in_dim(
        summed[:2, gain_at : gain_at + model], shard * (model // owners), model // owners, axis=1
    )
    gain_moment_new = decay_rate * gain_moment + gain_total / reps
    gains_new = norm_gains - rate_gains * gain_moment_new
    return (
        result,
        d_input,
        wide_new,
        square_new,
        narrow_new,
        wide_moment_new,
        square_moment_new,
        narrow_moment_new,
        wide_error_new,
        square_error_new,
        narrow_error_new,
        factor_wide,
        factor_square,
        factor_narrow,
        gains_new,
        gain_moment_new,
    )


def solution(mesh):
    return jax.shard_map(
        functools.partial(shards, Grid(mesh)),
        mesh=mesh,
        in_specs=(
            P(("rep", "shard"), None, None),
            P(("rep", "shard"), None, None),
            P(("rep", "shard"), None),
            P(("rep", "shard"), None),
            P(None, "shard", None),
            P(None, "shard", None),
            P(None, "shard", None),
            P(None, "shard", None),
            P(None, "shard", None),
            P(None, "shard", None),
            P("rep", None, "shard", None),
            P("rep", None, "shard", None),
            P("rep", None, "shard", None),
            P(),
            P(),
            P(),
            P(None, "shard"),
            P(None, "shard"),
        ),
        out_specs=(
            P(("rep", "shard"), None, None),
            P(("rep", "shard"), None, None),
            P(None, "shard", None),
            P(None, "shard", None),
            P(None, "shard", None),
            P(None, "shard", None),
            P(None, "shard", None),
            P(None, "shard", None),
            P("rep", None, "shard", None),
            P("rep", None, "shard", None),
            P("rep", None, "shard", None),
            P(),
            P(),
            P(),
            P(None, "shard"),
            P(None, "shard"),
        ),
        check_vma=False,
    )
```

```python
import functools

import jax
import jax.numpy as jnp
from jax import lax
from jax.experimental import pallas as pl
from jax.experimental.pallas import tpu as pltpu
from jax.sharding import PartitionSpec as P

QUERY_HEADS = 18
KEY_VALUE_HEADS = 6
HEAD_SIZE = 64
PAIRS = KEY_VALUE_HEADS // 2


eps_norm = 1e-05
theta_base = 10000.0
decay_rate = 0.9
rate_wide = 0.03
rate_square = 0.1
rate_narrow = 0.02
rate_gains = 0.01
mask_fill = -1e30
highest = lax.Precision.HIGHEST


def normed(value_heads, gain):
    return (
        value_heads
        * lax.rsqrt(jnp.mean(value_heads * value_heads, axis=-1, keepdims=True) + eps_norm)
        * gain
    )


def rotary_tables(position, width):
    halfway = width // 2
    inverse = theta_base ** (-2.0 * jnp.arange(halfway, dtype=jnp.float32) / width)
    angles = position.astype(jnp.float32)[:, None] * inverse[None, :]
    return (jnp.cos(angles), jnp.sin(angles))


BLOCK_ROWS = 256
VMEM_BYTES = 56 * 1024 * 1024


def partner_lanes(values):
    lane = lax.broadcasted_iota(jnp.int32, values.shape, 1)
    return jnp.where(
        lane % HEAD_SIZE < HEAD_SIZE // 2,
        pltpu.roll(values, 128 - HEAD_SIZE // 2, 1),
        pltpu.roll(values, HEAD_SIZE // 2, 1),
    )


def project_kernel(
    order_ref, x_ref, gain_ref, w_ref, cos_ref, sin_ref, out_ref, turned_ref, scratch_ref
):
    x = x_ref[...].astype(jnp.float32)
    scale = lax.rsqrt(jnp.mean(x * x, axis=-1, keepdims=True) + eps_norm)
    low = (x * scale * gain_ref[...]).astype(jnp.bfloat16)
    scratch_ref[...] = low.astype(jnp.float32).T
    share = scratch_ref.shape[0] // order_ref.shape[0]
    parts = [
        scratch_ref[pl.ds(pl.multiple_of(order_ref[p] * share, 8), share), :]
        for p in range(order_ref.shape[0])
    ]
    turned_ref[...] = jnp.concatenate(parts, axis=0).astype(jnp.bfloat16)
    cos, sin = cos_ref[...], sin_ref[...]
    for first in range(0, out_ref.shape[1], 640):
        got = jnp.dot(low, w_ref[:, first : first + 640], preferred_element_type=jnp.float32)
        for at in range(0, 640, 128):
            piece = got[:, at : at + 128]
            if at < 512:
                piece = piece * cos + partner_lanes(piece) * sin
            out_ref[:, first + at : first + at + 128] = piece.astype(jnp.bfloat16)


def project_qkv(order, x, gain, weights, cos, sin):
    rows, width = x.shape
    columns = weights.shape[1]
    block = min(BLOCK_ROWS, rows)
    return pl.pallas_call(
        project_kernel,
        grid_spec=pltpu.PrefetchScalarGridSpec(
            num_scalar_prefetch=1,
            grid=(rows // block,),
            in_specs=[
                pl.BlockSpec((block, width), lambda i, order: (i, 0)),
                pl.BlockSpec((1, width), lambda i, order: (0, 0)),
                pl.BlockSpec((width, columns), lambda i, order: (0, 0)),
                pl.BlockSpec((block, 128), lambda i, order: (i, 0)),
                pl.BlockSpec((block, 128), lambda i, order: (i, 0)),
            ],
            out_specs=[
                pl.BlockSpec((block, columns), lambda i, order: (i, 0)),
                pl.BlockSpec((width, block), lambda i, order: (0, i)),
            ],
            scratch_shapes=[pltpu.VMEM((width, block), jnp.float32)],
        ),
        out_shape=[
            jax.ShapeDtypeStruct((rows, columns), jnp.bfloat16),
            jax.ShapeDtypeStruct((width, rows), jnp.bfloat16),
        ],
        compiler_params=pltpu.CompilerParams(vmem_limit_bytes=VMEM_BYTES),
        cost_estimate=pl.CostEstimate(
            flops=2 * rows * width * columns,
            bytes_accessed=2 * (rows * width * 2 + rows * columns + width * columns),
            transcendentals=0,
        ),
    )(order, x, gain, weights, cos, sin)


def spread_heads(pair, spread_ref):
    wide = pair.astype(jnp.float32)
    turned = pltpu.roll(wide, HEAD_SIZE, 1)
    low_half = lax.broadcasted_iota(jnp.int32, wide.shape, 1) < HEAD_SIZE
    zero = jnp.zeros_like(wide)
    spread_ref[0] = jnp.where(low_half, wide, zero).astype(jnp.bfloat16)
    spread_ref[1] = jnp.where(low_half, zero, turned).astype(jnp.bfloat16)
    spread_ref[2] = jnp.where(low_half, turned, zero).astype(jnp.bfloat16)
    spread_ref[3] = jnp.where(low_half, zero, wide).astype(jnp.bfloat16)


def mask_bias(position, start, keys):
    rows = position.shape[0]
    row = lax.broadcasted_iota(jnp.int32, (rows, keys), 0) + start
    column = lax.broadcasted_iota(jnp.int32, (rows, keys), 1)
    allowed = (column <= row) & (column >= row - position)
    return jnp.where(allowed, 0.0, mask_fill)


def across(left, right):
    return lax.dot_general(
        left, right, (((1,), (1,)), ((), ())), preferred_element_type=jnp.float32
    )


def forward_kernel(qkv_ref, pos_ref, out_ref, log_ref, key_ref, value_ref):
    step = pl.program_id(1)
    block = out_ref.shape[0]

    @pl.when(step == 0)
    def _():
        spread_heads(qkv_ref[:, 384:512], key_ref)
        spread_heads(qkv_ref[:, 512:640], value_ref)

    for place in range(qkv_ref.shape[0] // block):

        @pl.when(step == place)
        def _(place=place):
            start = place * block
            keys = start + block
            bias = mask_bias(pos_ref[...], start, keys)
            lane = lax.broadcasted_iota(jnp.int32, (block, 128), 1)
            logs = jnp.zeros((block, 128), jnp.float32)
            for g in range(3):
                query = qkv_ref[start:keys, 128 * g : 128 * g + 128] * 0.125
                total = jnp.zeros((block, 128), jnp.float32)
                for e in range(2):
                    head = 2 * g + e
                    which = 2 * (head // 3) + e
                    scores = across(query, key_ref[which, :keys, :]) + bias
                    top = jnp.max(scores, axis=-1, keepdims=True)
                    raised = jnp.exp(scores - top)
                    row_total = jnp.sum(raised, axis=-1, keepdims=True)
                    low = (raised * (1.0 / row_total)).astype(jnp.bfloat16)
                    total += jnp.dot(
                        low, value_ref[which, :keys, :], preferred_element_type=jnp.float32
                    )
                    logs = jnp.where(lane == head, top + jnp.log(row_total), logs)
                out_ref[:, 128 * g : 128 * g + 128] = total.astype(jnp.bfloat16)
            log_ref[0] = logs


def attend_forward(qkv, position):
    rows = qkv.shape[0]
    pairs = qkv.shape[1] // 640
    block = min(BLOCK_ROWS, rows)
    return pl.pallas_call(
        forward_kernel,
        grid=(pairs, rows // block),
        in_specs=[
            pl.BlockSpec((rows, 640), lambda j, i: (0, j)),
            pl.BlockSpec((block, 1), lambda j, i: (i, 0)),
        ],
        out_specs=[
            pl.BlockSpec((block, 384), lambda j, i: (i, j)),
            pl.BlockSpec((1, block, 128), lambda j, i: (j, i, 0)),
        ],
        out_shape=[
            jax.ShapeDtypeStruct((rows, 384 * pairs), jnp.bfloat16),
            jax.ShapeDtypeStruct((pairs, rows, 128), jnp.float32),
        ],
        scratch_shapes=[
            pltpu.VMEM((4, rows, 128), jnp.bfloat16),
            pltpu.VMEM((4, rows, 128), jnp.bfloat16),
        ],
        compiler_params=pltpu.CompilerParams(vmem_limit_bytes=VMEM_BYTES),
        cost_estimate=pl.CostEstimate(
            flops=20 * pairs * rows * rows * 128,
            bytes_accessed=8 * rows * 640 * pairs,
            transcendentals=6 * pairs * rows * rows,
        ),
    )(qkv, position)


def backward_kernel(
    qkv_ref, d_ref, log_ref, pos_ref, cos_ref, sin_ref, out_ref, key_ref, value_ref, dk_ref, dv_ref
):
    step = pl.program_id(0)
    block = d_ref.shape[0]
    blocks = qkv_ref.shape[0] // block

    @pl.when(step == 0)
    def _():
        spread_heads(qkv_ref[:, 384:512], key_ref)
        spread_heads(qkv_ref[:, 512:640], value_ref)
        dk_ref[...] = jnp.zeros_like(dk_ref)
        dv_ref[...] = jnp.zeros_like(dv_ref)

    for place in range(blocks):

        @pl.when(step == place)
        def _(place=place):
            start = place * block
            keys = start + block
            bias = mask_bias(pos_ref[...], start, keys)
            logs = log_ref[0]
            cos, sin = cos_ref[start:keys, :], sin_ref[start:keys, :]
            for g in range(3):
                query = qkv_ref[start:keys, 128 * g : 128 * g + 128] * 0.125
                d_out = d_ref[:, 128 * g : 128 * g + 128]
                query_turned = query.astype(jnp.float32).T.astype(jnp.bfloat16)
                d_turned = d_out.astype(jnp.float32).T.astype(jnp.bfloat16)
                total = jnp.zeros((block, 128), jnp.float32)
                for e in range(2):
                    head = 2 * g + e
                    which = 2 * (head // 3) + e
                    at = HEAD_SIZE * (head // 3)
                    key = key_ref[which, :keys, :]
                    scores = across(query, key) + bias
                    prob = jnp.exp(scores - logs[:, head : head + 1])
                    d_prob = across(d_out, value_ref[which, :keys, :])
                    delta = jnp.sum(prob * d_prob, axis=-1, keepdims=True)
                    d_scores = (prob * (d_prob - delta)).astype(jnp.bfloat16)
                    half = slice(HEAD_SIZE * e, HEAD_SIZE * e + HEAD_SIZE)
                    dv_ref[at : at + HEAD_SIZE, :keys] += jnp.dot(
                        d_turned[half], prob.astype(jnp.bfloat16), preferred_element_type=jnp.float32
                    )
                    dk_ref[at : at + HEAD_SIZE, :keys] += jnp.dot(
                        query_turned[half], d_scores, preferred_element_type=jnp.float32
                    )
                    total += jnp.dot(d_scores, key, preferred_element_type=jnp.float32)
                total = total * 0.125
                total = total * cos - partner_lanes(total) * sin
                out_ref[start:keys, 128 * g : 128 * g + 128] = total.astype(jnp.bfloat16)

    @pl.when(step == blocks - 1)
    def _():
        d_key = dk_ref[...].T
        d_key = d_key * cos_ref[...] - partner_lanes(d_key) * sin_ref[...]
        out_ref[:, 384:512] = d_key.astype(jnp.bfloat16)
        out_ref[:, 512:640] = dv_ref[...].T.astype(jnp.bfloat16)


def attend_backward(qkv, d_attended, logs, position, cos, sin, pair):
    rows = qkv.shape[0]
    block = min(BLOCK_ROWS, rows)
    return pl.pallas_call(
        backward_kernel,
        grid=(rows // block,),
        in_specs=[
            pl.BlockSpec((rows, 640), lambda i: (0, pair)),
            pl.BlockSpec((block, 384), lambda i: (i, pair)),
            pl.BlockSpec((1, block, 128), lambda i: (pair, i, 0)),
            pl.BlockSpec((block, 1), lambda i: (i, 0)),
            pl.BlockSpec((rows, 128), lambda i: (0, 0)),
            pl.BlockSpec((rows, 128), lambda i: (0, 0)),
        ],
        out_specs=pl.BlockSpec((rows, 640), lambda i: (0, 0)),
        out_shape=jax.ShapeDtypeStruct((rows, 640), jnp.bfloat16),
        scratch_shapes=[
            pltpu.VMEM((4, rows, 128), jnp.bfloat16),
            pltpu.VMEM((4, rows, 128), jnp.bfloat16),
            pltpu.VMEM((128, rows), jnp.float32),
            pltpu.VMEM((128, rows), jnp.float32),
        ],
        compiler_params=pltpu.CompilerParams(vmem_limit_bytes=VMEM_BYTES),
        cost_estimate=pl.CostEstimate(
            flops=50 * rows * rows * 128,
            bytes_accessed=8 * rows * 640,
            transcendentals=6 * rows * rows,
        ),
    )(qkv, d_attended, logs, position, cos, sin)


def turn_kernel(order_ref, rows_ref, out_ref, turned_ref):
    turned_ref[...] = rows_ref[...].astype(jnp.float32).T
    owners = order_ref.shape[0]
    share = turned_ref.shape[0] // owners
    parts = [
        turned_ref[pl.ds(pl.multiple_of(order_ref[p] * share, 8), share), :] for p in range(owners)
    ]
    out_ref[...] = jnp.concatenate(parts, axis=0).astype(jnp.bfloat16)


def turn_rows(rows, order):
    count, model = rows.shape
    block = min(BLOCK_ROWS, count)
    return pl.pallas_call(
        turn_kernel,
        grid_spec=pltpu.PrefetchScalarGridSpec(
            num_scalar_prefetch=1,
            grid=(count // block,),
            in_specs=[pl.BlockSpec((block, model), lambda i, order: (i, 0))],
            out_specs=pl.BlockSpec((model, block), lambda i, order: (0, i)),
            scratch_shapes=[pltpu.VMEM((model, block), jnp.float32)],
        ),
        out_shape=jax.ShapeDtypeStruct((model, count), jnp.bfloat16),
        compiler_params=pltpu.CompilerParams(vmem_limit_bytes=VMEM_BYTES),
        cost_estimate=pl.CostEstimate(
            flops=0, bytes_accessed=4 * count * model, transcendentals=0
        ),
    )(order, rows)


def mlp_kernel(reps, first, slot_ref, place_ref, mid_ref, d_ref, *refs):
    del slot_ref
    mid_hbm, d_hbm = refs[:2]
    befores = refs[2 : 3 if first else 4]
    refs = refs[2 + len(befores) :]
    weight_hbm, refs = (refs[:1], refs[1:]) if place_ref.shape[0] == 1 else (refs[:2], refs[2:])
    away_ref, home_ref, result_ref, back_ref = refs[:4]
    weight_ref, mid_turned_ref, d_turned_ref, d_pair_ref, hidden_ref, weight_sem, sem = refs[4:]
    step = pl.program_id(0)
    count = mid_ref.shape[0]
    part = min(512, count)
    tile = hidden_ref.shape[1]
    half = away_ref.shape[1]

    wide = 3 * tile
    skip = weight_hbm[0].shape[2] - wide * (reps // 2)

    def load(i):
        if len(weight_hbm) == 1:
            pltpu.make_async_copy(
                weight_hbm[0].at[i], weight_ref.at[i], weight_sem.at[i]
            ).start()
            return
        ref, at = weight_hbm[2 * i // reps], i % (reps // 2)
        owners, share = ref.shape[:2]
        for a in range(owners):
            pltpu.make_async_copy(
                ref.at[place_ref[a], :, skip + wide * at : skip + wide * at + wide],
                weight_ref.at[i, share * a : share * a + share, :],
                weight_sem.at[i],
            ).start()

    sums = [pltpu.make_async_copy(befores[0], result_ref, sem.at[0])]
    if not first:
        sums.append(pltpu.make_async_copy(befores[1], back_ref, sem.at[1]))
    turned = [
        pltpu.make_async_copy(mid_hbm, mid_turned_ref, sem.at[2]),
        pltpu.make_async_copy(d_hbm, d_turned_ref, sem.at[3]),
    ]

    @pl.when(step == 0)
    def _():
        load(0)
        for copy in sums + turned:
            copy.start()
        for i in range(1, reps):
            load(i)
        if first:
            back_ref[...] = jnp.zeros_like(back_ref)

    for i in range(reps):

        @pl.when(step == i)
        def _(i=i):
            pltpu.make_async_copy(weight_ref.at[i], weight_ref.at[i], weight_sem.at[i]).wait()

    @pl.when(step == 0)
    def _():
        for copy in sums:
            copy.wait()

    @pl.loop(0, count // part)
    def _(t):
        rows = pl.ds(pl.multiple_of(t * part, part), part)
        pair_w = weight_ref[step, :, : 2 * tile]
        down_w = weight_ref[step, :, 2 * tile :]
        pair = jnp.dot(mid_ref[rows, :], pair_w, preferred_element_type=jnp.float32)
        d_hidden = jnp.dot(d_ref[rows, :], down_w, preferred_element_type=jnp.float32)
        gate, up = pair[:, :tile], pair[:, tile:]
        sig = jax.nn.sigmoid(gate)
        silu = gate * sig
        hidden = (silu * up).astype(jnp.bfloat16)
        hidden_ref[rows, :] = hidden
        d_gate = d_hidden * up * (sig * (1.0 + gate * (1.0 - sig)))
        d_pair_ref[rows, :tile] = d_gate.astype(jnp.bfloat16)
        d_pair_ref[rows, tile:] = (d_hidden * silu).astype(jnp.bfloat16)
        back_ref[rows, :] += across(d_pair_ref[rows, :], pair_w)
        result_ref[rows, :] += across(hidden, down_w)

    @pl.when(step == 0)
    def _():
        for copy in turned:
            copy.wait()

    for at, out_ref in ((0, away_ref), (half, home_ref)):
        pair = jnp.dot(
            mid_turned_ref[at : at + half, :], d_pair_ref[...], preferred_element_type=jnp.float32
        )
        out_ref[0] = pair[:, :tile].astype(jnp.bfloat16)
        out_ref[1] = pair[:, tile:].astype(jnp.bfloat16)
        out_ref[2] = jnp.dot(
            d_turned_ref[at : at + half, :], hidden_ref[...], preferred_element_type=jnp.float32
        ).astype(jnp.bfloat16)


def mlp_part(reps, slots, places, mid, d_out, mid_turned, d_turned, weights, result, back):
    count, model = mid.shape
    tile = (weights[0].shape[2] - (512 if len(weights) == 2 else 0)) // 3
    if len(weights) == 2:
        tile //= reps // 2
    units = tile * reps
    half = model // 2
    first = back is None
    befores = [result] if first else [result, back]

    def once(shape):
        return pl.BlockSpec(shape, lambda i, slots, places: (0, 0), pipeline_mode=pl.Buffered(1))

    anywhere = pl.BlockSpec(memory_space=pl.ANY)
    return pl.pallas_call(
        functools.partial(mlp_kernel, reps, first),
        grid_spec=pltpu.PrefetchScalarGridSpec(
            num_scalar_prefetch=2,
            grid=(reps,),
            in_specs=[once((count, model))] * 2 + [anywhere] * (2 + len(befores) + len(weights)),
            out_specs=[
                pl.BlockSpec((3, half, tile), lambda i, slots, places: (0, 0, slots[i])),
                pl.BlockSpec((3, half, tile), lambda i, slots, places: (0, 0, slots[i])),
                once((count, model)),
                once((count, model)),
            ],
            scratch_shapes=[
                pltpu.VMEM((reps, model, 3 * tile), jnp.bfloat16),
                pltpu.VMEM((model, count), jnp.bfloat16),
                pltpu.VMEM((model, count), jnp.bfloat16),
                pltpu.VMEM((count, 2 * tile), jnp.bfloat16),
                pltpu.VMEM((count, tile), jnp.bfloat16),
                pltpu.SemaphoreType.DMA((reps,)),
                pltpu.SemaphoreType.DMA((4,)),
            ],
        ),
        out_shape=[
            jax.ShapeDtypeStruct((3, half, units), jnp.bfloat16),
            jax.ShapeDtypeStruct((3, half, units), jnp.bfloat16),
            jax.ShapeDtypeStruct((count, model), jnp.float32),
            jax.ShapeDtypeStruct((count, model), jnp.float32),
        ],
        compiler_params=pltpu.CompilerParams(vmem_limit_bytes=VMEM_BYTES),
        cost_estimate=pl.CostEstimate(
            flops=18 * count * model * units,
            bytes_accessed=2 * (4 * count * model + 6 * model * units) + 16 * count * model,
            transcendentals=count * units,
        ),
    )(slots, places, mid, d_out, mid_turned, d_turned, *befores, *weights)


def assemble(rows, mine, other, places, core, low, high):
    owners = mine[0].shape[0]
    widths = [m.shape[2] for m in mine]
    count = len(mine)

    def kernel(place_ref, core_ref, *refs):
        del place_ref
        out_ref = refs[-1]
        for own in range(2):

            @pl.when(core_ref[0] == own)
            def _(own=own):
                at = 0
                for i in range(count):
                    for half in range(2):
                        ref = refs[i] if half == own else refs[count + i]
                        first, last = max(low, at), min(high, at + widths[i])
                        if first < last:
                            out_ref[0, :, first - low : last - low] = ref[
                                0, :, first - at : last - at
                            ]
                        at += widths[i]

    def spec(width):
        return pl.BlockSpec((1, rows, width), lambda a, place, core: (place[a], 0, 0))

    out = pl.pallas_call(
        kernel,
        grid_spec=pltpu.PrefetchScalarGridSpec(
            num_scalar_prefetch=2,
            grid=(owners,),
            in_specs=[spec(w) for w in widths] * 2,
            out_specs=pl.BlockSpec((1, rows, high - low), lambda a, place, core: (a, 0, 0)),
        ),
        out_shape=jax.ShapeDtypeStruct((owners, rows, high - low), jnp.bfloat16),
        compiler_params=pltpu.CompilerParams(vmem_limit_bytes=VMEM_BYTES),
        cost_estimate=pl.CostEstimate(
            flops=0, bytes_accessed=8 * owners * rows * sum(widths), transcendentals=0
        ),
    )(places, core, *mine, *other)
    return out.reshape(owners * rows, high - low)


def left_rows(factor, rows):
    lane = lax.broadcasted_iota(jnp.int32, (rows.shape[0], 128), 1)
    columns = jnp.zeros((rows.shape[0], 128), jnp.float32)
    for r in range(8):
        column = jnp.sum(rows * factor[r : r + 1, :], axis=1, keepdims=True)
        columns = jnp.where(lane == r, column, columns)
    return columns.T[:8, :]


def weighted_rows(left, rows):
    turned = left.T
    sublane = lax.broadcasted_iota(jnp.int32, (8, 1), 0)
    out = jnp.zeros((8, rows.shape[1]), jnp.float32)
    for r in range(8):
        row = jnp.sum(rows * turned[:, r : r + 1], axis=0, keepdims=True)
        out = jnp.where(sublane == r, row, out)
    return out


def exact_dot(left, right, contract):
    return lax.dot_general(
        left, right, (contract, ((), ())), precision=highest, preferred_element_type=jnp.float32
    )


def mix_kernel(layout, count, flag_ref, *refs):
    sums, refs = refs[: 3 * count], refs[3 * count :]
    errors, refs = refs[: len(layout)], refs[len(layout) :]
    factors, refs = refs[: len(layout)], refs[len(layout) :]
    mixed, left_ref = refs[: len(layout)], refs[len(layout)]
    stays = flag_ref[0] == 1
    for m, pieces in enumerate(layout):
        at = 0
        for which, first, last in pieces:
            away, home, moved = (
                sums[3 * which + k][..., first:last].astype(jnp.float32) for k in range(3)
            )
            width = last - first
            where = (..., slice(at, at + width))
            total = away + jnp.where(stays, home, moved)
            total = total.reshape(total.shape[-2:])
            error = errors[m][where]
            error = error.reshape(error.shape[-2:])
            mixed[m][where] = (total + error).reshape(mixed[m].shape[:-1] + (width,))
            at += width
        rows = mixed[m][...].reshape(mixed[m].shape[-2:])
        factor = factors[m][...].reshape(factors[m].shape[-2:])
        left_ref[8 * m : 8 * m + 8, :] = left_rows(factor, rows)


def mix_wide(flag, parts, error, factor):
    count, rows, third = parts[0][0].shape
    columns = third * len(parts)
    arrays = [a for part in parts for a in part]
    layout = [[(i, 0, third) for i in range(len(parts))]]
    return pl.pallas_call(
        functools.partial(mix_kernel, layout, len(parts)),
        grid_spec=pltpu.PrefetchScalarGridSpec(
            num_scalar_prefetch=1,
            grid=(count,),
            in_specs=[pl.BlockSpec((1, rows, third), lambda i, flag: (i, 0, 0))] * len(arrays)
            + [
                pl.BlockSpec((1, 1, rows, columns), lambda i, flag: (0, i, 0, 0)),
                pl.BlockSpec((1, 8, columns), lambda i, flag: (i, 0, 0)),
            ],
            out_specs=[
                pl.BlockSpec((1, rows, columns), lambda i, flag: (i, 0, 0)),
                pl.BlockSpec((8, rows), lambda i, flag: (i, 0)),
            ],
        ),
        out_shape=[
            jax.ShapeDtypeStruct((count, rows, columns), jnp.float32),
            jax.ShapeDtypeStruct((8 * count, rows), jnp.float32),
        ],
        compiler_params=pltpu.CompilerParams(vmem_limit_bytes=VMEM_BYTES),
        cost_estimate=pl.CostEstimate(
            flops=96 * count * rows * columns,
            bytes_accessed=14 * count * rows * columns,
            transcendentals=0,
        ),
    )(flag, *arrays, error, factor)


def in_vmem(count):
    return [pl.BlockSpec(memory_space=pltpu.VMEM)] * count


def mix_rest(flag, parts, layout, errors, factors):
    rows = errors[0].shape[0]
    arrays = [a for part in parts for a in part]
    return pl.pallas_call(
        functools.partial(mix_kernel, layout, len(parts)),
        in_specs=[pl.BlockSpec(memory_space=pltpu.SMEM)]
        + in_vmem(len(arrays) + len(errors) + len(factors)),
        out_specs=in_vmem(len(errors) + 1),
        out_shape=[jax.ShapeDtypeStruct(e.shape, jnp.float32) for e in errors]
        + [jax.ShapeDtypeStruct((8 * len(errors), rows), jnp.float32)],
        compiler_params=pltpu.CompilerParams(vmem_limit_bytes=VMEM_BYTES),
        cost_estimate=pl.CostEstimate(
            flops=96 * sum(e.size for e in errors),
            bytes_accessed=14 * sum(e.size for e in errors),
            transcendentals=0,
        ),
    )(flag, *arrays, *errors, *factors)


def contract_all(left, mixed, width, extra=None):
    def kernel(*refs):
        left_ref, out_ref = refs[0], refs[-1]
        out_ref[...] = jnp.zeros_like(out_ref)
        at, m = 0, 0
        for ref in refs[1 : 1 + len(mixed)]:
            for k in range(ref.shape[0] if len(ref.shape) == 3 else 1):
                rows = ref[k] if len(ref.shape) == 3 else ref[...]
                own = left_ref[8 * m : 8 * m + 8, :]
                out_ref[:, at : at + rows.shape[1]] = weighted_rows(own, rows)
                at += rows.shape[1]
                m += 1
        for k in range(m):
            own = left_ref[8 * k : 8 * k + 8, :]
            out_ref[:, at : at + 8] = exact_dot(own, own, ((1,), (1,)))
            at += 128
        if extra is not None:
            out_ref[: extra.shape[0], at : at + extra.shape[1]] = refs[-2][...]

    more = [] if extra is None else [extra]
    return pl.pallas_call(
        kernel,
        in_specs=in_vmem(1 + len(mixed) + len(more)),
        out_specs=pl.BlockSpec(memory_space=pltpu.VMEM),
        out_shape=jax.ShapeDtypeStruct((8, width), jnp.float32),
        compiler_params=pltpu.CompilerParams(vmem_limit_bytes=VMEM_BYTES),
        cost_estimate=pl.CostEstimate(
            flops=96 * sum(m.size for m in mixed),
            bytes_accessed=4 * sum(m.size for m in mixed),
            transcendentals=0,
        ),
    )(left, *mixed, *more)


def eliminate(gram, rights):
    row = lax.broadcasted_iota(jnp.int32, (8, 1), 0)
    for j in range(8):
        scale = 1.0 / jnp.sqrt(gram[j : j + 1, j : j + 1])
        below = jnp.where(row > j, gram[:, j : j + 1] * scale, 0.0)
        done = []
        for right in [gram] + list(rights):
            top = right[j : j + 1, :] * scale
            done.append(jnp.where(row == j, top, right - below * top))
        gram, rights = done[0], done[1:]
    return rights


def finish_matrix(reps, rate, row, gram, left, mixed, moment, master, outs):
    new_ref, moment_new_ref, error_ref, factor_ref = outs
    factor, basis = eliminate(gram[:, :8] * (1.0 / reps), [row, left])
    factor = factor * (1.0 / reps)
    factor_ref[...] = factor
    turned = basis.T
    columns = factor.shape[1]
    for first in range(0, columns, 256):
        span = slice(first, min(first + 256, columns))
        approx = turned[:, 0:1] * factor[0:1, span]
        for r in range(1, 8):
            approx += turned[:, r : r + 1] * factor[r : r + 1, span]
        moment_new = decay_rate * moment[:, span] + approx
        moment_new_ref[:, span] = moment_new
        new_ref[:, span] = master[:, span] - rate * moment_new
        error_ref[:, span] = mixed[:, span] - approx


def finish_wide(reps, packed, gram_at, left, mixed, moment, master):
    count, rows, columns = mixed.shape

    def kernel(row_ref, gram_ref, left_ref, mixed_ref, moment_ref, master_ref, *outs):
        new_ref, moment_new_ref, error_ref, factor_ref = outs
        finish_matrix(
            reps,
            rate_wide,
            row_ref[...],
            gram_ref[...],
            left_ref[...],
            mixed_ref.at[0],
            moment_ref.at[0],
            master_ref.at[0],
            (new_ref.at[0], moment_new_ref.at[0], error_ref.at[0, 0], factor_ref.at[0]),
        )

    whole = pl.BlockSpec((1, rows, columns), lambda i: (i, 0, 0))
    shape = jax.ShapeDtypeStruct((count, rows, columns), jnp.float32)
    return pl.pallas_call(
        kernel,
        grid=(count,),
        in_specs=[
            pl.BlockSpec((8, columns), lambda i: (0, i)),
            pl.BlockSpec((8, 128), lambda i: (0, gram_at // 128 + i)),
            pl.BlockSpec((8, rows), lambda i: (i, 0)),
            whole,
            whole,
            whole,
        ],
        out_specs=[
            whole,
            whole,
            pl.BlockSpec((1, 1, rows, columns), lambda i: (0, i, 0, 0)),
            pl.BlockSpec((1, 8, columns), lambda i: (i, 0, 0)),
        ],
        out_shape=[
            shape,
            shape,
            jax.ShapeDtypeStruct((1, count, rows, columns), jnp.float32),
            jax.ShapeDtypeStruct((count, 8, columns), jnp.float32),
        ],
        compiler_params=pltpu.CompilerParams(vmem_limit_bytes=VMEM_BYTES),
        cost_estimate=pl.CostEstimate(
            flops=96 * count * rows * columns,
            bytes_accessed=24 * count * rows * columns,
            transcendentals=0,
        ),
    )(packed, packed, left, mixed, moment, master)


def finish_rest(reps, packs, lefts, mixed, where, states):
    groups = []
    at = 0
    for moment, _, rate in states:
        groups.append((at, moment.shape[0], rate))
        at += moment.shape[0]

    def kernel(*refs):
        pack_refs, refs = refs[: len(packs)], refs[len(packs) :]
        left_refs, refs = refs[: len(lefts)], refs[len(lefts) :]
        mixed_refs, refs = refs[: len(mixed)], refs[len(mixed) :]
        state_refs, outs = refs[: 2 * len(states)], refs[2 * len(states) :]
        for g, (first, count, rate) in enumerate(groups):
            new_ref, moment_new_ref, error_ref, factor_ref = outs[4 * g : 4 * g + 4]
            for k in range(count):
                pack, row_at, gram_at, left_at = where[first + k]
                rows = mixed_refs[first + k]
                finish_matrix(
                    reps,
                    rate,
                    pack_refs[pack][:, row_at : row_at + rows.shape[1]],
                    pack_refs[pack][:, gram_at : gram_at + 128],
                    left_refs[pack][left_at : left_at + 8, :],
                    rows,
                    state_refs[2 * g].at[k],
                    state_refs[2 * g + 1].at[k],
                    (new_ref.at[k], moment_new_ref.at[k], error_ref.at[0, k], factor_ref.at[k]),
                )

    shapes = []
    for moment, _, _ in states:
        count, rows, columns = moment.shape
        shapes += [
            jax.ShapeDtypeStruct(moment.shape, jnp.float32),
            jax.ShapeDtypeStruct(moment.shape, jnp.float32),
            jax.ShapeDtypeStruct((1,) + moment.shape, jnp.float32),
            jax.ShapeDtypeStruct((count, 8, columns), jnp.float32),
        ]
    arrays = [a for state in states for a in state[:2]]
    return pl.pallas_call(
        kernel,
        in_specs=in_vmem(len(packs) + len(lefts) + len(mixed) + len(arrays)),
        out_specs=in_vmem(len(shapes)),
        out_shape=shapes,
        compiler_params=pltpu.CompilerParams(vmem_limit_bytes=VMEM_BYTES),
        cost_estimate=pl.CostEstimate(
            flops=96 * sum(m.size for m in mixed),
            bytes_accessed=24 * sum(m.size for m in mixed),
            transcendentals=0,
        ),
    )(*packs, *lefts, *mixed, *arrays)


def pack_wide(master, picks, groups, tile):
    count, rows, _ = master.shape
    number = picks.shape[0]

    def kernel(pick_ref, *refs):
        del pick_ref
        for group, out_ref in zip(groups, refs[number:]):
            at = 0
            for pick in group:
                for i in range(count):
                    out_ref[:, at : at + tile] = refs[pick][i].astype(jnp.bfloat16)
                    at += tile

    def spec(n):
        return pl.BlockSpec((count, rows, tile), lambda i, picks: (0, 0, picks[n]))

    shapes = [
        jax.ShapeDtypeStruct((rows, count * tile * len(group)), jnp.bfloat16) for group in groups
    ]
    return pl.pallas_call(
        kernel,
        grid_spec=pltpu.PrefetchScalarGridSpec(
            num_scalar_prefetch=1,
            grid=(1,),
            in_specs=[spec(n) for n in range(number)],
            out_specs=[pl.BlockSpec(s.shape, lambda i, picks: (0, 0)) for s in shapes],
        ),
        out_shape=shapes,
        compiler_params=pltpu.CompilerParams(vmem_limit_bytes=VMEM_BYTES),
        cost_estimate=pl.CostEstimate(
            flops=0, bytes_accessed=6 * number * count * rows * tile, transcendentals=0
        ),
    )(picks, *[master] * number)


def split_sum(home, got):
    shape = home.shape
    rows, columns = shape[-2:]
    lead = home.size // (rows * columns)
    half = rows // 2

    def kernel(home_ref, got_ref, away_ref, kept_ref):
        total = home_ref[0].astype(jnp.float32) + got_ref[0].astype(jnp.float32)
        away_ref[0] = total[:half].astype(jnp.bfloat16)
        kept_ref[0] = total[half:].astype(jnp.bfloat16)

    whole = pl.BlockSpec((1, rows, columns), lambda i: (i, 0, 0))
    part = pl.BlockSpec((1, half, columns), lambda i: (i, 0, 0))
    out = jax.ShapeDtypeStruct((lead, half, columns), jnp.bfloat16)
    away, kept = pl.pallas_call(
        kernel,
        grid=(lead,),
        in_specs=[whole, whole],
        out_specs=[part, part],
        out_shape=[out, out],
        compiler_params=pltpu.CompilerParams(vmem_limit_bytes=VMEM_BYTES),
        cost_estimate=pl.CostEstimate(
            flops=home.size, bytes_accessed=6 * home.size, transcendentals=0
        ),
    )(home.reshape(lead, rows, columns), got.reshape(lead, rows, columns))
    tail = (half, columns)
    return away.reshape(shape[:-2] + tail), kept.reshape(shape[:-2] + tail)


def out_kernel(owners, place_ref, core_ref, order_ref, att_ref, x_ref, gain_ref, *refs):
    halves, refs = refs[:4], refs[4:]
    residual_ref, mid_ref, mid_turned_ref, w_ref, turned_ref, sem = refs
    share = w_ref.shape[0] // owners

    @pl.when(pl.program_id(0) == 0)
    def _():
        for own in range(2):

            @pl.when(core_ref[0] == own)
            def _(own=own):
                spans = (
                    (halves[0 if own == 1 else 1], 896, 0, 128),
                    (halves[2 if own == 0 else 3], 0, 128, 512),
                    (halves[2 if own == 1 else 3], 0, 640, 512),
                )
                for ref, first, at, width in spans:
                    for a in range(owners):
                        pltpu.make_async_copy(
                            ref.at[place_ref[a], :share, first : first + width],
                            w_ref.at[share * a : share * a + share, at : at + width],
                            sem.at[0],
                        ).start()

        pltpu.make_async_copy(w_ref, w_ref, sem.at[0]).wait()

    residual = x_ref[...].astype(jnp.float32) + across(att_ref[...], w_ref[...])
    residual_ref[...] = residual
    scale = lax.rsqrt(jnp.mean(residual * residual, axis=-1, keepdims=True) + eps_norm)
    mid = (residual * scale * gain_ref[...]).astype(jnp.bfloat16)
    mid_ref[...] = mid
    turned_ref[...] = mid.astype(jnp.float32).T
    parts = [
        turned_ref[pl.ds(pl.multiple_of(order_ref[p] * share, 8), share), :] for p in range(owners)
    ]
    mid_turned_ref[...] = jnp.concatenate(parts, axis=0).astype(jnp.bfloat16)


def project_out(places, core, order, attended, x, gain, halves):
    count, model = x.shape
    owners = order.shape[0]
    block = min(BLOCK_ROWS, count)
    rows = pl.BlockSpec((block, model), lambda i, *_: (i, 0))
    return pl.pallas_call(
        functools.partial(out_kernel, owners),
        grid_spec=pltpu.PrefetchScalarGridSpec(
            num_scalar_prefetch=3,
            grid=(count // block,),
            in_specs=[rows, rows, pl.BlockSpec((1, model), lambda i, *_: (0, 0))]
            + [pl.BlockSpec(memory_space=pl.ANY)] * 4,
            out_specs=[
                rows,
                rows,
                pl.BlockSpec((model, block), lambda i, *_: (0, i)),
                pl.BlockSpec((model, model), lambda i, *_: (0, 0)),
            ],
            scratch_shapes=[
                pltpu.VMEM((model, block), jnp.float32),
                pltpu.SemaphoreType.DMA((1,)),
            ],
        ),
        out_shape=[
            jax.ShapeDtypeStruct((count, model), jnp.float32),
            jax.ShapeDtypeStruct((count, model), jnp.bfloat16),
            jax.ShapeDtypeStruct((model, count), jnp.bfloat16),
            jax.ShapeDtypeStruct((model, model), jnp.bfloat16),
        ],
        compiler_params=pltpu.CompilerParams(vmem_limit_bytes=VMEM_BYTES),
        cost_estimate=pl.CostEstimate(
            flops=2 * count * model * model,
            bytes_accessed=12 * count * model + 4 * model * model,
            transcendentals=count,
        ),
    )(places, core, order, attended, x, gain, *halves)


class Grid:
    def __init__(self, mesh):
        self.reps = mesh.shape["rep"]
        self.shards = mesh.shape["shard"]
        self.core_bit = self.shards.bit_length() - 3
        stages = self.shards.bit_length() - 1
        self.order = [self.core_bit] + [b for b in range(stages) if b != self.core_bit]

    def swapped(self, rep, shard):
        bit = self.core_bit
        core = rep & 1
        turn = (shard >> bit) & 1
        return (rep - core + turn, shard - (turn << bit) + (core << bit))

    def flat(self, pair):
        return pair[0] * self.shards + pair[1]

    def every(self):
        return [(r, s) for r in range(self.reps) for s in range(self.shards)]

    def move(self, value, target):
        pairs = [(self.flat(p), self.flat(target(*p))) for p in self.every() if target(*p) != p]
        return lax.ppermute(value, ("rep", "shard"), pairs)

    def stays(self):
        return lax.axis_index("rep") % 2 == (lax.axis_index("shard") >> self.core_bit) % 2

    def swap_rows(self, value):
        return jnp.where(self.stays(), value, self.move(value, self.swapped))

    def partner(self, bit):
        def target(rep, shard):
            lr, ls = self.swapped(rep, shard)
            return self.swapped(lr, ls ^ (1 << bit))

        return target

    def last(self, bit):
        def target(rep, shard):
            lr, ls = self.swapped(rep, shard)
            return (lr, ls ^ (1 << bit))

        return target

    def flip_rep(self, bit):
        return lambda rep, shard: (rep ^ (1 << bit), shard)

    def flip_shard(self, bit):
        return lambda rep, shard: (rep, shard ^ (1 << bit))

    def doubling(self):
        return list(range(len(self.order)))[::-1]

    def places(self):
        out = [0] * self.shards
        for place in range(self.shards):
            distance = 0
            for k, bit in enumerate(self.doubling()):
                if (place >> k) & 1:
                    distance |= 1 << bit
            out[distance] = place
        return out

    def masks(self):
        count = len(self.order)
        out = []
        for place in range(self.shards):
            mask = 0
            for k, bit in enumerate(self.order):
                if not (place >> (count - 1 - k)) & 1:
                    mask |= 1 << bit
            out.append(mask)
        return out


def after(value, *others):
    return lax.optimization_barrier((value, others))[0]


def gather_pieces(grid, blocks):
    mine = []
    before = [None] * len(grid.order)
    for number, block in enumerate(blocks):
        held = block[None]
        for k, bit in enumerate(grid.doubling()):
            last = k == len(before) - 1
            if before[k] is not None:
                held = after(held, before[k])
            before[k] = grid.move(held, grid.flip_shard(bit))
            if not (last and number == len(blocks) - 1):
                held = jnp.concatenate([held, before[k]], axis=0)
        mine.append(held)
    return mine, before


class Sums:
    def __init__(self, grid, away, home):
        self.grid = grid
        self.stage = 0
        self.away, self.home = away, home
        self.send()

    def send(self):
        grid, bit = self.grid, self.grid.order[self.stage]
        if self.stage == len(grid.order) - 1:
            self.got = (grid.move(self.away, grid.last(bit)), grid.move(self.home, grid.swapped))
        else:
            self.got = grid.move(self.away, grid.partner(bit))

    def step(self, late, hold=False):
        self.got = after(self.got, late)
        self.away, self.home = split_sum(self.home, self.got)
        self.stage += 1
        if not hold:
            self.send()
        return (self.away, self.home)

    def join(self, other):
        self.away = jnp.concatenate([self.away, other.away], axis=-1)
        self.home = jnp.concatenate([self.home, other.home], axis=-1)
        self.send()

    def result(self, late):
        while self.stage < len(self.grid.order) - 1:
            self.step(late)
        return (self.got[0], self.home, self.got[1])


def butterfly(grid, value, moves):
    for move in moves:
        value = jax.tree.map(lambda v: v + grid.move(v, move), value)
    return value


def sum_all(grid, value, beside=None):
    rep = lax.axis_index("rep")
    bits = range(grid.reps.bit_length() - 1)
    pad = -value.shape[1] % (128 * grid.reps)
    columns = value.shape[1]
    value = jnp.pad(value, ((0, 0), (0, pad)))
    for bit in bits:
        half = value.shape[1] // 2
        upper = (rep >> bit) % 2 == 1
        low, high = value[:, :half], value[:, half:]
        got = grid.move(jnp.where(upper, low, high), grid.flip_rep(bit))
        value = jnp.where(upper, high, low) + got
    for bit in range(grid.shards.bit_length() - 1):
        value = value + grid.move(value, grid.flip_shard(bit))
    if beside is not None:
        value = after(value, beside)
    for bit in reversed(bits):
        got = grid.move(value, grid.flip_rep(bit))
        upper = (rep >> bit) % 2 == 1
        value = jnp.concatenate(
            [jnp.where(upper, got, value), jnp.where(upper, value, got)], axis=1
        )
    return value[:, :columns]


def shards(
    grid,
    tokens,
    cotangent,
    segments,
    positions,
    wide_master,
    square_master,
    key_value_master,
    wide_moment,
    square_moment,
    key_value_momentum,
    wide_error,
    square_error,
    key_value_error,
    wide_factor,
    square_factor,
    key_value_factor,
    norm_gains,
    gain_moment,
):
    reps, owners = grid.reps, grid.shards
    rep = lax.axis_index("rep")
    shard = lax.axis_index("shard")
    core = rep % 2
    turn = (shard >> grid.core_bit) % 2
    logical_shard = shard + (core - turn) * (1 << grid.core_bit)

    low_square = square_master.astype(jnp.bfloat16)
    low_narrow = key_value_master.astype(jnp.bfloat16)
    pieces = []
    for j in range(PAIRS):
        pieces.append(low_square[0, :, 384 * j : 384 * j + 384])
        pieces.append(low_narrow[0, :, 128 * j : 128 * j + 128])
        pieces.append(low_narrow[1, :, 128 * j : 128 * j + 128])
    low_attn = jnp.concatenate(pieces + [low_square[1]], axis=1)
    units = wide_master.shape[2] // 3

    position = grid.swap_rows(positions)[0]
    rows = low_attn.shape[0]
    tile = units // reps
    chained = 1 if rows % 16 == 0 else 0
    gain_row = norm_gains.astype(jnp.bfloat16).reshape(1, 2 * rows)
    gain_row = jnp.pad(gain_row, ((0, 15), (0, 1024 - 2 * rows)))
    first = lax.dynamic_slice_in_dim(low_attn, core * 1024, 1024, axis=1)
    first = jnp.concatenate([first, gain_row], axis=0)
    second = lax.dynamic_slice_in_dim(low_attn, 2048 + core * 512, 512, axis=1)
    picks = [core * (reps // 2) + i for i in range(reps // 2)] if chained else []
    groups = [tuple(range(len(picks)))] if chained else []
    for k in range(chained, 3):
        groups.append((len(picks),))
        picks.append(reps * k + rep)
    cuts = list(pack_wide(wide_master, jnp.stack(picks).astype(jnp.int32), groups, tile))
    if chained:
        second = jnp.concatenate([second, cuts[0]], axis=1)
    mine, gathering = gather_pieces(grid, [first, second])
    other = [grid.move(mine[0], grid.flip_rep(0))]
    places = jnp.array(grid.places(), jnp.int32)[jnp.arange(owners) ^ shard]
    cores = core[None]
    gain_w = mine[0][:, rows, : 2 * rows].reshape(owners, 2, rows)
    gain_w = jnp.take(gain_w, places, axis=0).transpose(1, 0, 2).reshape(2, -1).astype(jnp.float32)
    natural = jnp.arange(reps, dtype=jnp.int32)
    whole = jnp.zeros((1,), jnp.int32)
    moved_tokens = grid.move(after(tokens, gathering[1]), grid.swapped)
    tokens = jnp.where(grid.stays(), tokens, moved_tokens)[0]
    moved_out = grid.move(after(cotangent, moved_tokens), grid.swapped)
    model = gain_w.shape[1]
    columns = 640 * PAIRS
    qkv_w = assemble(rows, mine[:1], other[:1], places, cores, 0, columns)

    count = tokens.shape[0]
    hidden_in = tokens.astype(jnp.float32)
    gain_attn, gain_mlp = gain_w[0], gain_w[1]
    cos, sin = rotary_tables(position, HEAD_SIZE)
    cos = jnp.concatenate([cos] * 4, axis=1)
    sin = jnp.concatenate([-sin, sin] * 2, axis=1)
    place = position[:, None]
    order = jnp.array(grid.masks(), jnp.int32) ^ logical_shard

    qkv, turned_in = project_qkv(order, tokens, gain_attn[None], qkv_w, cos, sin)
    held, got = after((mine[1], gathering[-1]), qkv)
    mine[1] = jnp.concatenate([held, got], axis=0)
    qkv = after(qkv, mine[1])
    wide_parts = [None] * chained
    for k in range(chained, 3):
        part = after(cuts[k], mine[1])
        part = lax.all_gather(part, ("rep", "shard"), axis=0, tiled=True)
        wide_parts.append((natural, whole, [part.reshape(reps, owners * rows, 3 * tile)]))
    other.append(grid.move(mine[1], grid.flip_rep(0)))
    attended, logs = attend_forward(qkv, place)
    other[1] = after(other[1], attended)
    d_out = jnp.where(grid.stays(), cotangent, after(moved_out, attended))[0]
    if chained:
        slots = (natural + core * (reps // 2)) % reps
        wide_parts[0] = (slots, places, [mine[1], other[1]])
        residual, normed_mid, turned_mid, out_w = project_out(
            places,
            cores,
            order,
            attended,
            tokens,
            gain_mlp[None],
            [mine[0], other[0], mine[1], other[1]],
        )
    else:
        out_w = assemble(rows, mine, other, places, cores, columns, 3072)
        residual = hidden_in + jnp.einsum(
            "tn,dn->td", attended, out_w, preferred_element_type=jnp.float32
        )
        normed_mid = normed(residual, gain_mlp).astype(jnp.bfloat16)
        turned_mid = turn_rows(normed_mid, order)
    turned_out = turn_rows(d_out, order)

    half = model // 2

    def weight_grad(turned, right):
        return Sums(
            grid,
            jnp.dot(turned[:half], right, preferred_element_type=jnp.float32).astype(jnp.bfloat16),
            jnp.dot(turned[half:], right, preferred_element_type=jnp.float32).astype(jnp.bfloat16),
        )

    wide_sums = []
    result, d_mid = residual, None
    for k in range(3):
        slots, where, weights = wide_parts[k]
        away, home, result, d_mid = mlp_part(
            reps, slots, where, normed_mid, d_out, turned_mid, turned_out, weights, result, d_mid
        )
        wide_sums.append(Sums(grid, away, home))
        for earlier in wide_sums[max(0, k - 2) : k]:
            d_mid, result = after((d_mid, result), earlier.step(away))
    result = grid.swap_rows(result.astype(jnp.bfloat16)[None])

    _, mid_back = jax.vjp(normed, residual, gain_mlp)
    d_residual, grad_gain_mlp = mid_back(d_mid)
    d_residual = d_residual + d_out.astype(jnp.float32)
    d_branch = d_residual.astype(jnp.bfloat16)
    d_attended = jnp.einsum(
        "td,dn->tn", d_branch, out_w, preferred_element_type=jnp.float32
    ).astype(jnp.bfloat16)
    out_sums = weight_grad(turn_rows(d_branch, order), attended)

    d_attended = after(d_attended, wide_sums[2].step(out_sums.away), wide_sums[0].got)
    d_stacks, pair_sums = [], []
    hold = len(grid.order) == 3
    for j in range(PAIRS):
        d_stack = attend_backward(qkv, d_attended, logs, place, cos, sin, j)
        d_stacks.append(d_stack)
        pair_sums.append(weight_grad(turned_in, d_stack))
        if j == 0:
            done = (wide_sums[1].step(d_stack), out_sums.step(d_stack), result)
        elif j == 1:
            done = (
                wide_sums[2].step(d_stack),
                out_sums.step(d_stack),
                pair_sums[0].step(d_stack),
                wide_sums[1].got,
            )
        else:
            done = (pair_sums[0].step(d_stack, hold), pair_sums[1].step(d_stack), out_sums.got)
        d_attended = after(d_attended, done, pair_sums[j].away)
        d_stacks = after(d_stacks, done, pair_sums[j].away)
    def back(j):
        return jnp.einsum(
            "tn,dn->td",
            d_stacks[j],
            qkv_w[:, 640 * j : 640 * j + 640],
            preferred_element_type=jnp.float32,
        )

    flag = grid.stays().astype(jnp.int32)[None]
    d_first = back(0) + back(1)
    d_stacks, wide_got = after(
        (d_stacks, wide_sums[2].got), pair_sums[2].step(d_first), pair_sums[1].step(d_first, hold)
    )
    wide_sums[2].got = wide_got
    spans = [(j, 0) for j in range(PAIRS)]
    late_sums = pair_sums
    if hold:
        pair_sums[0].join(pair_sums[1])
        spans = [(0, 0), (0, 640), (1, 0)]
        late_sums = [pair_sums[0], pair_sums[2]]
    mixed_wide, left_wide = mix_wide(
        flag, [part.result(d_first) for part in wide_sums], wide_error, wide_factor
    )
    mixed_out, left_out = mix_rest(
        flag,
        [out_sums.result(d_first)],
        [[(0, 0, model)]],
        [square_error[0, 1]],
        [square_factor[1]],
    )
    last_step = pair_sums[2].step(left_wide)
    d_stacks = after(d_stacks, last_step, left_out)
    d_normed_in = d_first + back(2)
    rep_moves = [grid.flip_rep(b) for b in range(reps.bit_length() - 1)]
    unit = 128 * reps
    left_early = butterfly(grid, jnp.concatenate([left_wide, left_out], axis=0), rep_moves)
    left_early = after(left_early, last_step)
    gram_early = 9 * units + model
    width = -(-(gram_early + 512) // unit) * unit
    early = contract_all(left_early, [mixed_wide, mixed_out], width)
    d_normed_in = after(d_normed_in, early)
    _, in_back = jax.vjp(normed, hidden_in, gain_attn)
    d_input, grad_gain_attn = in_back(d_normed_in)
    d_input = (d_input + d_residual).astype(jnp.bfloat16)
    early = sum_all(grid, early)
    late = d_input
    d_input = grid.swap_rows(d_input[None])
    narrow = 128 * PAIRS

    mixed_query, mixed_key, mixed_value, left_late = mix_rest(
        flag,
        [part.result(late) for part in late_sums],
        [
            [(which, at + first, at + last) for which, at in spans]
            for first, last in ((0, 384), (384, 512), (512, 640))
        ],
        [square_error[0, 0], key_value_error[0, 0], key_value_error[0, 1]],
        [square_factor[0], key_value_factor[0], key_value_factor[1]],
    )
    left_late = butterfly(grid, left_late, rep_moves)
    gram_late = columns
    gain_at = gram_late + 384
    width = -(-(gain_at + model) // unit) * unit
    gain_grad = jnp.stack([grad_gain_attn, grad_gain_mlp])
    mixed_late = [mixed_query, mixed_key, mixed_value]
    left_late = after(left_late, late)
    summed = contract_all(left_late, mixed_late, width, gain_grad)
    wide_new, wide_moment_new, wide_error_new, factor_wide = finish_wide(
        reps, early, gram_early, left_early, mixed_wide, wide_moment, wide_master
    )
    summed = butterfly(grid, summed, rep_moves + [grid.flip_shard(0)])
    summed = after(summed, wide_new)
    shard_moves = [grid.flip_shard(b) for b in range(1, owners.bit_length() - 1)]
    summed = butterfly(grid, summed, shard_moves)
    (
        square_new,
        square_moment_new,
        square_error_new,
        factor_square,
        narrow_new,
        narrow_moment_new,
        narrow_error_new,
        factor_narrow,
    ) = finish_rest(
        reps,
        [summed, early],
        [left_late, left_early],
        [mixed_query, mixed_out, mixed_key, mixed_value],
        [
            (0, 0, gram_late, 0),
            (1, 9 * units, gram_early + 384, 24),
            (0, model, gram_late + 128, 8),
            (0, model + narrow, gram_late + 256, 16),
        ],
        [
            (square_moment, square_master, rate_square),
            (key_value_momentum, key_value_master, rate_narrow),
        ],
    )
    gain_total = lax.dynamic_slice_in_dim(
        summed[:2, gain_at : gain_at + model], shard * (model // owners), model // owners, axis=1
    )
    gain_moment_new = decay_rate * gain_moment + gain_total / reps
    gains_new = norm_gains - rate_gains * gain_moment_new
    return (
        result,
        d_input,
        wide_new,
        square_new,
        narrow_new,
        wide_moment_new,
        square_moment_new,
        narrow_moment_new,
        wide_error_new,
        square_error_new,
        narrow_error_new,
        factor_wide,
        factor_square,
        factor_narrow,
        gains_new,
        gain_moment_new,
    )


def solution(mesh):
    return jax.shard_map(
        functools.partial(shards, Grid(mesh)),
        mesh=mesh,
        in_specs=(
            P(("rep", "shard"), None, None),
            P(("rep", "shard"), None, None),
            P(("rep", "shard"), None),
            P(("rep", "shard"), None),
            P(None, "shard", None),
            P(None, "shard", None),
            P(None, "shard", None),
            P(None, "shard", None),
            P(None, "shard", None),
            P(None, "shard", None),
            P("rep", None, "shard", None),
            P("rep", None, "shard", None),
            P("rep", None, "shard", None),
            P(),
            P(),
            P(),
            P(None, "shard"),
            P(None, "shard"),
        ),
        out_specs=(
            P(("rep", "shard"), None, None),
            P(("rep", "shard"), None, None),
            P(None, "shard", None),
            P(None, "shard", None),
            P(None, "shard", None),
            P(None, "shard", None),
            P(None, "shard", None),
            P(None, "shard", None),
            P("rep", None, "shard", None),
            P("rep", None, "shard", None),
            P("rep", None, "shard", None),
            P(),
            P(),
            P(),
            P(None, "shard"),
            P(None, "shard"),
        ),
        check_vma=False,
    )
```

```python
import functools

import jax
import jax.numpy as jnp
from jax import lax
from jax.experimental import pallas as pl
from jax.experimental.pallas import tpu as pltpu
from jax.sharding import PartitionSpec as P

QUERY_HEADS = 18
KEY_VALUE_HEADS = 6
HEAD_SIZE = 64
PAIRS = KEY_VALUE_HEADS // 2


eps_norm = 1e-05
theta_base = 10000.0
decay_rate = 0.9
rate_wide = 0.03
rate_square = 0.1
rate_narrow = 0.02
rate_gains = 0.01
mask_fill = -1e30
highest = lax.Precision.HIGHEST


def normed(value_heads, gain):
    return (
        value_heads
        * lax.rsqrt(jnp.mean(value_heads * value_heads, axis=-1, keepdims=True) + eps_norm)
        * gain
    )


def rotary_tables(position, width):
    halfway = width // 2
    inverse = theta_base ** (-2.0 * jnp.arange(halfway, dtype=jnp.float32) / width)
    angles = position.astype(jnp.float32)[:, None] * inverse[None, :]
    return (jnp.cos(angles), jnp.sin(angles))


BLOCK_ROWS = 256
VMEM_BYTES = 56 * 1024 * 1024


def light(flops, bytes_accessed, transcendentals):
    return pl.CostEstimate(
        flops=flops // 8, bytes_accessed=bytes_accessed // 8, transcendentals=transcendentals // 8
    )


def partner_lanes(values):
    lane = lax.broadcasted_iota(jnp.int32, values.shape, 1)
    return jnp.where(
        lane % HEAD_SIZE < HEAD_SIZE // 2,
        pltpu.roll(values, 128 - HEAD_SIZE // 2, 1),
        pltpu.roll(values, HEAD_SIZE // 2, 1),
    )


def project_kernel(
    order_ref, x_ref, gain_ref, w_ref, cos_ref, sin_ref, out_ref, turned_ref, scratch_ref
):
    x = x_ref[...].astype(jnp.float32)
    scale = lax.rsqrt(jnp.mean(x * x, axis=-1, keepdims=True) + eps_norm)
    low = (x * scale * gain_ref[...]).astype(jnp.bfloat16)
    scratch_ref[...] = low.astype(jnp.float32).T
    share = scratch_ref.shape[0] // order_ref.shape[0]
    parts = [
        scratch_ref[pl.ds(pl.multiple_of(order_ref[p] * share, 8), share), :]
        for p in range(order_ref.shape[0])
    ]
    turned_ref[...] = jnp.concatenate(parts, axis=0).astype(jnp.bfloat16)
    cos, sin = cos_ref[...], sin_ref[...]
    for first in range(0, out_ref.shape[1], 640):
        got = jnp.dot(low, w_ref[:, first : first + 640], preferred_element_type=jnp.float32)
        for at in range(0, 640, 128):
            piece = got[:, at : at + 128]
            if at < 512:
                piece = piece * cos + partner_lanes(piece) * sin
            out_ref[:, first + at : first + at + 128] = piece.astype(jnp.bfloat16)


def project_qkv(order, x, gain, weights, cos, sin):
    rows, width = x.shape
    columns = weights.shape[1]
    block = min(BLOCK_ROWS, rows)
    return pl.pallas_call(
        project_kernel,
        grid_spec=pltpu.PrefetchScalarGridSpec(
            num_scalar_prefetch=1,
            grid=(rows // block,),
            in_specs=[
                pl.BlockSpec((block, width), lambda i, order: (i, 0)),
                pl.BlockSpec((1, width), lambda i, order: (0, 0)),
                pl.BlockSpec((width, columns), lambda i, order: (0, 0)),
                pl.BlockSpec((block, 128), lambda i, order: (i, 0)),
                pl.BlockSpec((block, 128), lambda i, order: (i, 0)),
            ],
            out_specs=[
                pl.BlockSpec((block, columns), lambda i, order: (i, 0)),
                pl.BlockSpec((width, block), lambda i, order: (0, i)),
            ],
            scratch_shapes=[pltpu.VMEM((width, block), jnp.float32)],
        ),
        out_shape=[
            jax.ShapeDtypeStruct((rows, columns), jnp.bfloat16),
            jax.ShapeDtypeStruct((width, rows), jnp.bfloat16),
        ],
        compiler_params=pltpu.CompilerParams(vmem_limit_bytes=VMEM_BYTES),
        cost_estimate=light(
            flops=2 * rows * width * columns,
            bytes_accessed=2 * (rows * width * 2 + rows * columns + width * columns),
            transcendentals=0,
        ),
    )(order, x, gain, weights, cos, sin)


def spread_heads(pair, spread_ref):
    wide = pair.astype(jnp.float32)
    turned = pltpu.roll(wide, HEAD_SIZE, 1)
    low_half = lax.broadcasted_iota(jnp.int32, wide.shape, 1) < HEAD_SIZE
    zero = jnp.zeros_like(wide)
    spread_ref[0] = jnp.where(low_half, wide, zero).astype(jnp.bfloat16)
    spread_ref[1] = jnp.where(low_half, zero, turned).astype(jnp.bfloat16)
    spread_ref[2] = jnp.where(low_half, turned, zero).astype(jnp.bfloat16)
    spread_ref[3] = jnp.where(low_half, zero, wide).astype(jnp.bfloat16)


def mask_bias(position, start, keys):
    rows = position.shape[0]
    row = lax.broadcasted_iota(jnp.int32, (rows, keys), 0) + start
    column = lax.broadcasted_iota(jnp.int32, (rows, keys), 1)
    allowed = (column <= row) & (column >= row - position)
    return jnp.where(allowed, 0.0, mask_fill)


def across(left, right):
    return lax.dot_general(
        left, right, (((1,), (1,)), ((), ())), preferred_element_type=jnp.float32
    )


def forward_kernel(qkv_ref, pos_ref, out_ref, log_ref, key_ref, value_ref):
    step = pl.program_id(1)
    block = out_ref.shape[0]

    @pl.when(step == 0)
    def _():
        spread_heads(qkv_ref[:, 384:512], key_ref)
        spread_heads(qkv_ref[:, 512:640], value_ref)

    for place in range(qkv_ref.shape[0] // block):

        @pl.when(step == place)
        def _(place=place):
            start = place * block
            keys = start + block
            bias = mask_bias(pos_ref[...], start, keys)
            lane = lax.broadcasted_iota(jnp.int32, (block, 128), 1)
            logs = jnp.zeros((block, 128), jnp.float32)
            for g in range(3):
                query = qkv_ref[start:keys, 128 * g : 128 * g + 128] * 0.125
                total = jnp.zeros((block, 128), jnp.float32)
                for e in range(2):
                    head = 2 * g + e
                    which = 2 * (head // 3) + e
                    scores = across(query, key_ref[which, :keys, :]) + bias
                    top = jnp.max(scores, axis=-1, keepdims=True)
                    raised = jnp.exp(scores - top)
                    row_total = jnp.sum(raised, axis=-1, keepdims=True)
                    low = (raised * (1.0 / row_total)).astype(jnp.bfloat16)
                    total += jnp.dot(
                        low, value_ref[which, :keys, :], preferred_element_type=jnp.float32
                    )
                    logs = jnp.where(lane == head, top + jnp.log(row_total), logs)
                out_ref[:, 128 * g : 128 * g + 128] = total.astype(jnp.bfloat16)
            log_ref[0] = logs


def attend_forward(qkv, position):
    rows = qkv.shape[0]
    pairs = qkv.shape[1] // 640
    block = min(BLOCK_ROWS, rows)
    return pl.pallas_call(
        forward_kernel,
        grid=(pairs, rows // block),
        in_specs=[
            pl.BlockSpec((rows, 640), lambda j, i: (0, j)),
            pl.BlockSpec((block, 1), lambda j, i: (i, 0)),
        ],
        out_specs=[
            pl.BlockSpec((block, 384), lambda j, i: (i, j)),
            pl.BlockSpec((1, block, 128), lambda j, i: (j, i, 0)),
        ],
        out_shape=[
            jax.ShapeDtypeStruct((rows, 384 * pairs), jnp.bfloat16),
            jax.ShapeDtypeStruct((pairs, rows, 128), jnp.float32),
        ],
        scratch_shapes=[
            pltpu.VMEM((4, rows, 128), jnp.bfloat16),
            pltpu.VMEM((4, rows, 128), jnp.bfloat16),
        ],
        compiler_params=pltpu.CompilerParams(vmem_limit_bytes=VMEM_BYTES),
        cost_estimate=light(
            flops=20 * pairs * rows * rows * 128,
            bytes_accessed=8 * rows * 640 * pairs,
            transcendentals=6 * pairs * rows * rows,
        ),
    )(qkv, position)


def backward_kernel(
    qkv_ref,
    d_ref,
    log_ref,
    pos_ref,
    cos_ref,
    sin_ref,
    turned_ref,
    out_ref,
    away_ref,
    home_ref,
    key_ref,
    value_ref,
    dk_ref,
    dv_ref,
):
    step = pl.program_id(0)
    block = d_ref.shape[0]
    blocks = qkv_ref.shape[0] // block

    @pl.when(step == 0)
    def _():
        spread_heads(qkv_ref[:, 384:512], key_ref)
        spread_heads(qkv_ref[:, 512:640], value_ref)
        dk_ref[...] = jnp.zeros_like(dk_ref)
        dv_ref[...] = jnp.zeros_like(dv_ref)

    for place in range(blocks):

        @pl.when(step == place)
        def _(place=place):
            start = place * block
            keys = start + block
            bias = mask_bias(pos_ref[...], start, keys)
            logs = log_ref[0]
            cos, sin = cos_ref[start:keys, :], sin_ref[start:keys, :]
            for g in range(3):
                query = qkv_ref[start:keys, 128 * g : 128 * g + 128] * 0.125
                d_out = d_ref[:, 128 * g : 128 * g + 128]
                query_turned = query.astype(jnp.float32).T.astype(jnp.bfloat16)
                d_turned = d_out.astype(jnp.float32).T.astype(jnp.bfloat16)
                total = jnp.zeros((block, 128), jnp.float32)
                for e in range(2):
                    head = 2 * g + e
                    which = 2 * (head // 3) + e
                    at = HEAD_SIZE * (head // 3)
                    key = key_ref[which, :keys, :]
                    scores = across(query, key) + bias
                    prob = jnp.exp(scores - logs[:, head : head + 1])
                    d_prob = across(d_out, value_ref[which, :keys, :])
                    delta = jnp.sum(prob * d_prob, axis=-1, keepdims=True)
                    d_scores = (prob * (d_prob - delta)).astype(jnp.bfloat16)
                    half = slice(HEAD_SIZE * e, HEAD_SIZE * e + HEAD_SIZE)
                    dv_ref[at : at + HEAD_SIZE, :keys] += jnp.dot(
                        d_turned[half], prob.astype(jnp.bfloat16), preferred_element_type=jnp.float32
                    )
                    dk_ref[at : at + HEAD_SIZE, :keys] += jnp.dot(
                        query_turned[half], d_scores, preferred_element_type=jnp.float32
                    )
                    total += jnp.dot(d_scores, key, preferred_element_type=jnp.float32)
                total = total * 0.125
                total = total * cos - partner_lanes(total) * sin
                out_ref[start:keys, 128 * g : 128 * g + 128] = total.astype(jnp.bfloat16)

    @pl.when(step == blocks - 1)
    def _():
        d_key = dk_ref[...].T
        d_key = d_key * cos_ref[...] - partner_lanes(d_key) * sin_ref[...]
        out_ref[:, 384:512] = d_key.astype(jnp.bfloat16)
        out_ref[:, 512:640] = dv_ref[...].T.astype(jnp.bfloat16)
        half = away_ref.shape[0]
        for first, grad_ref in ((0, away_ref), (half, home_ref)):
            grad_ref[...] = jnp.dot(
                turned_ref[first : first + half, :],
                out_ref[...],
                preferred_element_type=jnp.float32,
            ).astype(jnp.bfloat16)


def attend_backward(qkv, d_attended, logs, position, cos, sin, turned, pair):
    rows = qkv.shape[0]
    model = turned.shape[0]
    block = min(BLOCK_ROWS, rows)
    half = pl.BlockSpec((model // 2, 640), lambda i: (0, 0))
    return pl.pallas_call(
        backward_kernel,
        grid=(rows // block,),
        in_specs=[
            pl.BlockSpec((rows, 640), lambda i: (0, pair)),
            pl.BlockSpec((block, 384), lambda i: (i, pair)),
            pl.BlockSpec((1, block, 128), lambda i: (pair, i, 0)),
            pl.BlockSpec((block, 1), lambda i: (i, 0)),
            pl.BlockSpec((rows, 128), lambda i: (0, 0)),
            pl.BlockSpec((rows, 128), lambda i: (0, 0)),
            pl.BlockSpec((model, rows), lambda i: (0, 0), pipeline_mode=pl.Buffered(1)),
        ],
        out_specs=[pl.BlockSpec((rows, 640), lambda i: (0, 0)), half, half],
        out_shape=[
            jax.ShapeDtypeStruct((rows, 640), jnp.bfloat16),
            jax.ShapeDtypeStruct((model // 2, 640), jnp.bfloat16),
            jax.ShapeDtypeStruct((model // 2, 640), jnp.bfloat16),
        ],
        scratch_shapes=[
            pltpu.VMEM((4, rows, 128), jnp.bfloat16),
            pltpu.VMEM((4, rows, 128), jnp.bfloat16),
            pltpu.VMEM((128, rows), jnp.float32),
            pltpu.VMEM((128, rows), jnp.float32),
        ],
        compiler_params=pltpu.CompilerParams(vmem_limit_bytes=VMEM_BYTES),
        cost_estimate=light(
            flops=50 * rows * rows * 128,
            bytes_accessed=8 * rows * 640,
            transcendentals=6 * rows * rows,
        ),
    )(qkv, d_attended, logs, position, cos, sin, turned)


def turn_kernel(order_ref, rows_ref, out_ref, turned_ref):
    turned_ref[...] = rows_ref[...].astype(jnp.float32).T
    owners = order_ref.shape[0]
    share = turned_ref.shape[0] // owners
    parts = [
        turned_ref[pl.ds(pl.multiple_of(order_ref[p] * share, 8), share), :] for p in range(owners)
    ]
    out_ref[...] = jnp.concatenate(parts, axis=0).astype(jnp.bfloat16)


def turn_rows(rows, order):
    count, model = rows.shape
    block = min(BLOCK_ROWS, count)
    return pl.pallas_call(
        turn_kernel,
        grid_spec=pltpu.PrefetchScalarGridSpec(
            num_scalar_prefetch=1,
            grid=(count // block,),
            in_specs=[pl.BlockSpec((block, model), lambda i, order: (i, 0))],
            out_specs=pl.BlockSpec((model, block), lambda i, order: (0, i)),
            scratch_shapes=[pltpu.VMEM((model, block), jnp.float32)],
        ),
        out_shape=jax.ShapeDtypeStruct((model, count), jnp.bfloat16),
        compiler_params=pltpu.CompilerParams(vmem_limit_bytes=VMEM_BYTES),
        cost_estimate=light(
            flops=0, bytes_accessed=4 * count * model, transcendentals=0
        ),
    )(order, rows)


def mlp_kernel(reps, first, last, slot_ref, place_ref, mid_ref, d_ref, *refs):
    del slot_ref
    mid_hbm, d_hbm = refs[:2]
    befores = refs[2 : 3 if first else 4]
    refs = refs[2 + len(befores) :]
    weight_hbm, refs = (refs[:1], refs[1:]) if place_ref.shape[0] == 1 else (refs[:2], refs[2:])
    away_ref, home_ref, result_ref, back_ref = refs[:4]
    weight_ref, mid_turned_ref, d_turned_ref, d_pair_ref, hidden_ref, weight_sem, sem = refs[4:11]
    output_ref = result_ref
    if last:
        result_ref = refs[11]
    step = pl.program_id(0)
    count = mid_ref.shape[0]
    part = min(512, count)
    tile = hidden_ref.shape[1]
    half = away_ref.shape[1]

    wide = 3 * tile
    skip = weight_hbm[0].shape[2] - wide * (reps // 2)

    def load(i):
        if len(weight_hbm) == 1:
            pltpu.make_async_copy(
                weight_hbm[0].at[i], weight_ref.at[i], weight_sem.at[i]
            ).start()
            return
        ref, at = weight_hbm[2 * i // reps], i % (reps // 2)
        owners, share = ref.shape[:2]
        for a in range(owners):
            pltpu.make_async_copy(
                ref.at[place_ref[a], :, skip + wide * at : skip + wide * at + wide],
                weight_ref.at[i, share * a : share * a + share, :],
                weight_sem.at[i],
            ).start()

    sums = [pltpu.make_async_copy(befores[0], result_ref, sem.at[0])]
    if not first:
        sums.append(pltpu.make_async_copy(befores[1], back_ref, sem.at[1]))
    turned = [
        pltpu.make_async_copy(mid_hbm, mid_turned_ref, sem.at[2]),
        pltpu.make_async_copy(d_hbm, d_turned_ref, sem.at[3]),
    ]

    @pl.when(step == 0)
    def _():
        load(0)
        for copy in sums + turned:
            copy.start()
        for i in range(1, reps):
            load(i)
        if first:
            back_ref[...] = jnp.zeros_like(back_ref)

    for i in range(reps):

        @pl.when(step == i)
        def _(i=i):
            pltpu.make_async_copy(weight_ref.at[i], weight_ref.at[i], weight_sem.at[i]).wait()

    @pl.when(step == 0)
    def _():
        for copy in sums:
            copy.wait()

    @pl.loop(0, count // part)
    def _(t):
        rows = pl.ds(pl.multiple_of(t * part, part), part)
        pair_w = weight_ref[step, :, : 2 * tile]
        down_w = weight_ref[step, :, 2 * tile :]
        pair = jnp.dot(mid_ref[rows, :], pair_w, preferred_element_type=jnp.float32)
        d_hidden = jnp.dot(d_ref[rows, :], down_w, preferred_element_type=jnp.float32)
        gate, up = pair[:, :tile], pair[:, tile:]
        sig = jax.nn.sigmoid(gate)
        silu = gate * sig
        hidden = (silu * up).astype(jnp.bfloat16)
        hidden_ref[rows, :] = hidden
        d_gate = d_hidden * up * (sig * (1.0 + gate * (1.0 - sig)))
        d_pair_ref[rows, :tile] = d_gate.astype(jnp.bfloat16)
        d_pair_ref[rows, tile:] = (d_hidden * silu).astype(jnp.bfloat16)
        back_ref[rows, :] += across(d_pair_ref[rows, :], pair_w)
        result_ref[rows, :] += across(hidden, down_w)
        if last:

            @pl.when(step == reps - 1)
            def _():
                output_ref[rows, :] = result_ref[rows, :].astype(jnp.bfloat16)

    @pl.when(step == 0)
    def _():
        for copy in turned:
            copy.wait()

    for at, out_ref in ((0, away_ref), (half, home_ref)):
        pair = jnp.dot(
            mid_turned_ref[at : at + half, :], d_pair_ref[...], preferred_element_type=jnp.float32
        )
        out_ref[0] = pair[:, :tile].astype(jnp.bfloat16)
        out_ref[1] = pair[:, tile:].astype(jnp.bfloat16)
        out_ref[2] = jnp.dot(
            d_turned_ref[at : at + half, :], hidden_ref[...], preferred_element_type=jnp.float32
        ).astype(jnp.bfloat16)


def mlp_part(reps, slots, places, mid, d_out, mid_turned, d_turned, weights, result, back, last):
    count, model = mid.shape
    tile = (weights[0].shape[2] - (512 if len(weights) == 2 else 0)) // 3
    if len(weights) == 2:
        tile //= reps // 2
    units = tile * reps
    half = model // 2
    first = back is None
    befores = [result] if first else [result, back]

    def once(shape):
        return pl.BlockSpec(shape, lambda i, slots, places: (0, 0), pipeline_mode=pl.Buffered(1))

    anywhere = pl.BlockSpec(memory_space=pl.ANY)
    return pl.pallas_call(
        functools.partial(mlp_kernel, reps, first, last),
        grid_spec=pltpu.PrefetchScalarGridSpec(
            num_scalar_prefetch=2,
            grid=(reps,),
            in_specs=[once((count, model))] * 2 + [anywhere] * (2 + len(befores) + len(weights)),
            out_specs=[
                pl.BlockSpec((3, half, tile), lambda i, slots, places: (0, 0, slots[i])),
                pl.BlockSpec((3, half, tile), lambda i, slots, places: (0, 0, slots[i])),
                once((count, model)),
                once((count, model)),
            ],
            scratch_shapes=[
                pltpu.VMEM((reps, model, 3 * tile), jnp.bfloat16),
                pltpu.VMEM((model, count), jnp.bfloat16),
                pltpu.VMEM((model, count), jnp.bfloat16),
                pltpu.VMEM((count, 2 * tile), jnp.bfloat16),
                pltpu.VMEM((count, tile), jnp.bfloat16),
                pltpu.SemaphoreType.DMA((reps,)),
                pltpu.SemaphoreType.DMA((4,)),
            ]
            + ([pltpu.VMEM((count, model), jnp.float32)] if last else []),
        ),
        out_shape=[
            jax.ShapeDtypeStruct((3, half, units), jnp.bfloat16),
            jax.ShapeDtypeStruct((3, half, units), jnp.bfloat16),
            jax.ShapeDtypeStruct((count, model), jnp.bfloat16 if last else jnp.float32),
            jax.ShapeDtypeStruct((count, model), jnp.float32),
        ],
        compiler_params=pltpu.CompilerParams(vmem_limit_bytes=VMEM_BYTES),
        cost_estimate=light(
            flops=18 * count * model * units,
            bytes_accessed=2 * (4 * count * model + 6 * model * units) + 16 * count * model,
            transcendentals=count * units,
        ),
    )(slots, places, mid, d_out, mid_turned, d_turned, *befores, *weights)


def assemble(rows, mine, other, places, core, low, high):
    owners = mine[0].shape[0]
    widths = [m.shape[2] for m in mine]
    count = len(mine)

    def kernel(place_ref, core_ref, *refs):
        del place_ref
        out_ref = refs[-1]
        for own in range(2):

            @pl.when(core_ref[0] == own)
            def _(own=own):
                at = 0
                for i in range(count):
                    for half in range(2):
                        ref = refs[i] if half == own else refs[count + i]
                        first, last = max(low, at), min(high, at + widths[i])
                        if first < last:
                            out_ref[0, :, first - low : last - low] = ref[
                                0, :, first - at : last - at
                            ]
                        at += widths[i]

    def spec(width):
        return pl.BlockSpec((1, rows, width), lambda a, place, core: (place[a], 0, 0))

    out = pl.pallas_call(
        kernel,
        grid_spec=pltpu.PrefetchScalarGridSpec(
            num_scalar_prefetch=2,
            grid=(owners,),
            in_specs=[spec(w) for w in widths] * 2,
            out_specs=pl.BlockSpec((1, rows, high - low), lambda a, place, core: (a, 0, 0)),
        ),
        out_shape=jax.ShapeDtypeStruct((owners, rows, high - low), jnp.bfloat16),
        compiler_params=pltpu.CompilerParams(vmem_limit_bytes=VMEM_BYTES),
        cost_estimate=light(
            flops=0, bytes_accessed=8 * owners * rows * sum(widths), transcendentals=0
        ),
    )(places, core, *mine, *other)
    return out.reshape(owners * rows, high - low)


def left_rows(factor, rows):
    lane = lax.broadcasted_iota(jnp.int32, (rows.shape[0], 128), 1)
    columns = jnp.zeros((rows.shape[0], 128), jnp.float32)
    for r in range(8):
        column = jnp.sum(rows * factor[r : r + 1, :], axis=1, keepdims=True)
        columns = jnp.where(lane == r, column, columns)
    return columns.T[:8, :]


def exact_dot(left, right, contract):
    return lax.dot_general(
        left, right, (contract, ((), ())), precision=highest, preferred_element_type=jnp.float32
    )


def mix_kernel(layout, count, flag_ref, *refs):
    sums, refs = refs[: 3 * count], refs[3 * count :]
    errors, refs = refs[: len(layout)], refs[len(layout) :]
    factors, refs = refs[: len(layout)], refs[len(layout) :]
    mixed, left_ref = refs[: len(layout)], refs[len(layout)]
    stays = flag_ref[0] == 1
    for m, pieces in enumerate(layout):
        at = 0
        for which, first, last in pieces:
            away, home, moved = (
                sums[3 * which + k][..., first:last].astype(jnp.float32) for k in range(3)
            )
            width = last - first
            where = (..., slice(at, at + width))
            total = away + jnp.where(stays, home, moved)
            total = total.reshape(total.shape[-2:])
            error = errors[m][where]
            error = error.reshape(error.shape[-2:])
            mixed[m][where] = (total + error).reshape(mixed[m].shape[:-1] + (width,))
            at += width
        rows = mixed[m][...].reshape(mixed[m].shape[-2:])
        factor = factors[m][...].reshape(factors[m].shape[-2:])
        left_ref[8 * m : 8 * m + 8, :] = left_rows(factor, rows)


def mix_wide(flag, parts, error, factor):
    count, rows, third = parts[0][0].shape
    columns = third * len(parts)
    arrays = [a for part in parts for a in part]
    layout = [[(i, 0, third) for i in range(len(parts))]]
    return pl.pallas_call(
        functools.partial(mix_kernel, layout, len(parts)),
        grid_spec=pltpu.PrefetchScalarGridSpec(
            num_scalar_prefetch=1,
            grid=(count,),
            in_specs=[pl.BlockSpec((1, rows, third), lambda i, flag: (i, 0, 0))] * len(arrays)
            + [
                pl.BlockSpec((1, 1, rows, columns), lambda i, flag: (0, i, 0, 0)),
                pl.BlockSpec((1, 8, columns), lambda i, flag: (i, 0, 0)),
            ],
            out_specs=[
                pl.BlockSpec((1, rows, columns), lambda i, flag: (i, 0, 0)),
                pl.BlockSpec((8, rows), lambda i, flag: (i, 0)),
            ],
        ),
        out_shape=[
            jax.ShapeDtypeStruct((count, rows, columns), jnp.float32),
            jax.ShapeDtypeStruct((8 * count, rows), jnp.float32),
        ],
        compiler_params=pltpu.CompilerParams(vmem_limit_bytes=VMEM_BYTES),
        cost_estimate=light(
            flops=96 * count * rows * columns,
            bytes_accessed=14 * count * rows * columns,
            transcendentals=0,
        ),
    )(flag, *arrays, error, factor)


def in_vmem(count):
    return [pl.BlockSpec(memory_space=pltpu.VMEM)] * count


def mix_rest(flag, parts, layout, errors, factors):
    rows = errors[0].shape[0]
    arrays = [a for part in parts for a in part]
    return pl.pallas_call(
        functools.partial(mix_kernel, layout, len(parts)),
        in_specs=[pl.BlockSpec(memory_space=pltpu.SMEM)]
        + in_vmem(len(arrays) + len(errors) + len(factors)),
        out_specs=in_vmem(len(errors) + 1),
        out_shape=[jax.ShapeDtypeStruct(e.shape, jnp.float32) for e in errors]
        + [jax.ShapeDtypeStruct((8 * len(errors), rows), jnp.float32)],
        compiler_params=pltpu.CompilerParams(vmem_limit_bytes=VMEM_BYTES),
        cost_estimate=light(
            flops=96 * sum(e.size for e in errors),
            bytes_accessed=14 * sum(e.size for e in errors),
            transcendentals=0,
        ),
    )(flag, *arrays, *errors, *factors)


def contract_all(left, mixed, width, extra=None):
    def kernel(*refs):
        left_ref, out_ref = refs[0], refs[-1]
        out_ref[...] = jnp.zeros_like(out_ref)
        at, m = 0, 0
        for ref in refs[1 : 1 + len(mixed)]:
            for k in range(ref.shape[0] if len(ref.shape) == 3 else 1):
                rows = ref[k] if len(ref.shape) == 3 else ref[...]
                own = left_ref[8 * m : 8 * m + 8, :]
                out_ref[:, at : at + rows.shape[1]] = exact_dot(own, rows, ((1,), (0,)))
                at += rows.shape[1]
                m += 1
        for k in range(m):
            own = left_ref[8 * k : 8 * k + 8, :]
            out_ref[:, at : at + 8] = exact_dot(own, own, ((1,), (1,)))
            at += 128
        if extra is not None:
            out_ref[: extra.shape[0], at : at + extra.shape[1]] = refs[-2][...]

    more = [] if extra is None else [extra]
    return pl.pallas_call(
        kernel,
        in_specs=in_vmem(1 + len(mixed) + len(more)),
        out_specs=pl.BlockSpec(memory_space=pltpu.VMEM),
        out_shape=jax.ShapeDtypeStruct((8, width), jnp.float32),
        compiler_params=pltpu.CompilerParams(vmem_limit_bytes=VMEM_BYTES),
        cost_estimate=light(
            flops=96 * sum(m.size for m in mixed),
            bytes_accessed=4 * sum(m.size for m in mixed),
            transcendentals=0,
        ),
    )(left, *mixed, *more)


def eliminate(gram, rights):
    row = lax.broadcasted_iota(jnp.int32, (8, 1), 0)
    for j in range(8):
        scale = 1.0 / jnp.sqrt(gram[j : j + 1, j : j + 1])
        below = jnp.where(row > j, gram[:, j : j + 1] * scale, 0.0)
        done = []
        for right in [gram] + list(rights):
            top = right[j : j + 1, :] * scale
            done.append(jnp.where(row == j, top, right - below * top))
        gram, rights = done[0], done[1:]
    return rights


def finish_matrix(reps, rate, row, gram, left, mixed, moment, master, outs):
    new_ref, moment_new_ref, error_ref, factor_ref = outs
    factor, basis = eliminate(gram[:, :8] * (1.0 / reps), [row, left])
    factor = factor * (1.0 / reps)
    factor_ref[...] = factor
    turned = basis.T
    columns = factor.shape[1]
    for first in range(0, columns, 256):
        span = slice(first, min(first + 256, columns))
        approx = turned[:, 0:1] * factor[0:1, span]
        for r in range(1, 8):
            approx += turned[:, r : r + 1] * factor[r : r + 1, span]
        moment_new = decay_rate * moment[:, span] + approx
        moment_new_ref[:, span] = moment_new
        new_ref[:, span] = master[:, span] - rate * moment_new
        error_ref[:, span] = mixed[:, span] - approx


def finish_wide(reps, packed, gram_at, left, mixed, moment, master):
    count, rows, columns = mixed.shape

    def kernel(row_ref, gram_ref, left_ref, mixed_ref, moment_ref, master_ref, *outs):
        new_ref, moment_new_ref, error_ref, factor_ref = outs
        finish_matrix(
            reps,
            rate_wide,
            row_ref[...],
            gram_ref[...],
            left_ref[...],
            mixed_ref.at[0],
            moment_ref.at[0],
            master_ref.at[0],
            (new_ref.at[0], moment_new_ref.at[0], error_ref.at[0, 0], factor_ref.at[0]),
        )

    whole = pl.BlockSpec((1, rows, columns), lambda i: (i, 0, 0))
    shape = jax.ShapeDtypeStruct((count, rows, columns), jnp.float32)
    return pl.pallas_call(
        kernel,
        grid=(count,),
        in_specs=[
            pl.BlockSpec((8, columns), lambda i: (0, i)),
            pl.BlockSpec((8, 128), lambda i: (0, gram_at // 128 + i)),
            pl.BlockSpec((8, rows), lambda i: (i, 0)),
            whole,
            whole,
            whole,
        ],
        out_specs=[
            whole,
            whole,
            pl.BlockSpec((1, 1, rows, columns), lambda i: (0, i, 0, 0)),
            pl.BlockSpec((1, 8, columns), lambda i: (i, 0, 0)),
        ],
        out_shape=[
            shape,
            shape,
            jax.ShapeDtypeStruct((1, count, rows, columns), jnp.float32),
            jax.ShapeDtypeStruct((count, 8, columns), jnp.float32),
        ],
        compiler_params=pltpu.CompilerParams(vmem_limit_bytes=VMEM_BYTES),
        cost_estimate=light(
            flops=96 * count * rows * columns,
            bytes_accessed=24 * count * rows * columns,
            transcendentals=0,
        ),
    )(packed, packed, left, mixed, moment, master)


def finish_rest(reps, packs, lefts, mixed, where, states):
    groups = []
    at = 0
    for moment, _, rate in states:
        groups.append((at, moment.shape[0], rate))
        at += moment.shape[0]

    def kernel(*refs):
        pack_refs, refs = refs[: len(packs)], refs[len(packs) :]
        left_refs, refs = refs[: len(lefts)], refs[len(lefts) :]
        mixed_refs, refs = refs[: len(mixed)], refs[len(mixed) :]
        state_refs, outs = refs[: 2 * len(states)], refs[2 * len(states) :]
        for g, (first, count, rate) in enumerate(groups):
            new_ref, moment_new_ref, error_ref, factor_ref = outs[4 * g : 4 * g + 4]
            for k in range(count):
                pack, row_at, gram_at, left_at = where[first + k]
                rows = mixed_refs[first + k]
                finish_matrix(
                    reps,
                    rate,
                    pack_refs[pack][:, row_at : row_at + rows.shape[1]],
                    pack_refs[pack][:, gram_at : gram_at + 128],
                    left_refs[pack][left_at : left_at + 8, :],
                    rows,
                    state_refs[2 * g].at[k],
                    state_refs[2 * g + 1].at[k],
                    (new_ref.at[k], moment_new_ref.at[k], error_ref.at[0, k], factor_ref.at[k]),
                )

    shapes = []
    for moment, _, _ in states:
        count, rows, columns = moment.shape
        shapes += [
            jax.ShapeDtypeStruct(moment.shape, jnp.float32),
            jax.ShapeDtypeStruct(moment.shape, jnp.float32),
            jax.ShapeDtypeStruct((1,) + moment.shape, jnp.float32),
            jax.ShapeDtypeStruct((count, 8, columns), jnp.float32),
        ]
    arrays = [a for state in states for a in state[:2]]
    return pl.pallas_call(
        kernel,
        in_specs=in_vmem(len(packs) + len(lefts) + len(mixed) + len(arrays)),
        out_specs=in_vmem(len(shapes)),
        out_shape=shapes,
        compiler_params=pltpu.CompilerParams(vmem_limit_bytes=VMEM_BYTES),
        cost_estimate=light(
            flops=96 * sum(m.size for m in mixed),
            bytes_accessed=24 * sum(m.size for m in mixed),
            transcendentals=0,
        ),
    )(*packs, *lefts, *mixed, *arrays)


def pack_wide(master, picks, groups, tile):
    count, rows, _ = master.shape
    number = picks.shape[0]

    def kernel(pick_ref, *refs):
        del pick_ref
        for group, out_ref in zip(groups, refs[number:]):
            at = 0
            for pick in group:
                for i in range(count):
                    out_ref[:, at : at + tile] = refs[pick][i].astype(jnp.bfloat16)
                    at += tile

    def spec(n):
        return pl.BlockSpec((count, rows, tile), lambda i, picks: (0, 0, picks[n]))

    shapes = [
        jax.ShapeDtypeStruct((rows, count * tile * len(group)), jnp.bfloat16) for group in groups
    ]
    return pl.pallas_call(
        kernel,
        grid_spec=pltpu.PrefetchScalarGridSpec(
            num_scalar_prefetch=1,
            grid=(1,),
            in_specs=[spec(n) for n in range(number)],
            out_specs=[pl.BlockSpec(s.shape, lambda i, picks: (0, 0)) for s in shapes],
        ),
        out_shape=shapes,
        compiler_params=pltpu.CompilerParams(vmem_limit_bytes=VMEM_BYTES),
        cost_estimate=light(
            flops=0, bytes_accessed=6 * number * count * rows * tile, transcendentals=0
        ),
    )(picks, *[master] * number)


def split_sum(home, got):
    shape = home.shape
    rows, columns = shape[-2:]
    lead = home.size // (rows * columns)
    half = rows // 2

    def kernel(home_ref, got_ref, away_ref, kept_ref):
        total = home_ref[0].astype(jnp.float32) + got_ref[0].astype(jnp.float32)
        away_ref[0] = total[:half].astype(jnp.bfloat16)
        kept_ref[0] = total[half:].astype(jnp.bfloat16)

    whole = pl.BlockSpec((1, rows, columns), lambda i: (i, 0, 0))
    part = pl.BlockSpec((1, half, columns), lambda i: (i, 0, 0))
    out = jax.ShapeDtypeStruct((lead, half, columns), jnp.bfloat16)
    away, kept = pl.pallas_call(
        kernel,
        grid=(lead,),
        in_specs=[whole, whole],
        out_specs=[part, part],
        out_shape=[out, out],
        compiler_params=pltpu.CompilerParams(vmem_limit_bytes=VMEM_BYTES),
        cost_estimate=light(
            flops=home.size, bytes_accessed=6 * home.size, transcendentals=0
        ),
    )(home.reshape(lead, rows, columns), got.reshape(lead, rows, columns))
    tail = (half, columns)
    return away.reshape(shape[:-2] + tail), kept.reshape(shape[:-2] + tail)


def out_kernel(owners, place_ref, core_ref, order_ref, att_ref, x_ref, gain_ref, *refs):
    halves, refs = refs[:4], refs[4:]
    residual_ref, mid_ref, mid_turned_ref, w_ref, turned_ref, sem = refs
    share = w_ref.shape[0] // owners

    @pl.when(pl.program_id(0) == 0)
    def _():
        for own in range(2):

            @pl.when(core_ref[0] == own)
            def _(own=own):
                spans = (
                    (halves[0 if own == 1 else 1], 896, 0, 128),
                    (halves[2 if own == 0 else 3], 0, 128, 512),
                    (halves[2 if own == 1 else 3], 0, 640, 512),
                )
                for ref, first, at, width in spans:
                    for a in range(owners):
                        pltpu.make_async_copy(
                            ref.at[place_ref[a], :share, first : first + width],
                            w_ref.at[share * a : share * a + share, at : at + width],
                            sem.at[0],
                        ).start()

        pltpu.make_async_copy(w_ref, w_ref, sem.at[0]).wait()

    residual = x_ref[...].astype(jnp.float32) + across(att_ref[...], w_ref[...])
    residual_ref[...] = residual
    scale = lax.rsqrt(jnp.mean(residual * residual, axis=-1, keepdims=True) + eps_norm)
    mid = (residual * scale * gain_ref[...]).astype(jnp.bfloat16)
    mid_ref[...] = mid
    turned_ref[...] = mid.astype(jnp.float32).T
    parts = [
        turned_ref[pl.ds(pl.multiple_of(order_ref[p] * share, 8), share), :] for p in range(owners)
    ]
    mid_turned_ref[...] = jnp.concatenate(parts, axis=0).astype(jnp.bfloat16)


def project_out(places, core, order, attended, x, gain, halves):
    count, model = x.shape
    owners = order.shape[0]
    block = min(BLOCK_ROWS, count)
    rows = pl.BlockSpec((block, model), lambda i, *_: (i, 0))
    return pl.pallas_call(
        functools.partial(out_kernel, owners),
        grid_spec=pltpu.PrefetchScalarGridSpec(
            num_scalar_prefetch=3,
            grid=(count // block,),
            in_specs=[rows, rows, pl.BlockSpec((1, model), lambda i, *_: (0, 0))]
            + [pl.BlockSpec(memory_space=pl.ANY)] * 4,
            out_specs=[
                rows,
                rows,
                pl.BlockSpec((model, block), lambda i, *_: (0, i)),
                pl.BlockSpec((model, model), lambda i, *_: (0, 0)),
            ],
            scratch_shapes=[
                pltpu.VMEM((model, block), jnp.float32),
                pltpu.SemaphoreType.DMA((1,)),
            ],
        ),
        out_shape=[
            jax.ShapeDtypeStruct((count, model), jnp.float32),
            jax.ShapeDtypeStruct((count, model), jnp.bfloat16),
            jax.ShapeDtypeStruct((model, count), jnp.bfloat16),
            jax.ShapeDtypeStruct((model, model), jnp.bfloat16),
        ],
        compiler_params=pltpu.CompilerParams(vmem_limit_bytes=VMEM_BYTES),
        cost_estimate=light(
            flops=2 * count * model * model,
            bytes_accessed=12 * count * model + 4 * model * model,
            transcendentals=count,
        ),
    )(places, core, order, attended, x, gain, *halves)


class Grid:
    def __init__(self, mesh):
        self.reps = mesh.shape["rep"]
        self.shards = mesh.shape["shard"]
        self.core_bit = self.shards.bit_length() - 3
        stages = self.shards.bit_length() - 1
        self.order = [self.core_bit] + [b for b in range(stages) if b != self.core_bit]

    def swapped(self, rep, shard):
        bit = self.core_bit
        core = rep & 1
        turn = (shard >> bit) & 1
        return (rep - core + turn, shard - (turn << bit) + (core << bit))

    def flat(self, pair):
        return pair[0] * self.shards + pair[1]

    def every(self):
        return [(r, s) for r in range(self.reps) for s in range(self.shards)]

    def move(self, value, target):
        pairs = [(self.flat(p), self.flat(target(*p))) for p in self.every() if target(*p) != p]
        return lax.ppermute(value, ("rep", "shard"), pairs)

    def stays(self):
        return lax.axis_index("rep") % 2 == (lax.axis_index("shard") >> self.core_bit) % 2

    def swap_rows(self, value):
        return jnp.where(self.stays(), value, self.move(value, self.swapped))

    def partner(self, bit):
        def target(rep, shard):
            lr, ls = self.swapped(rep, shard)
            return self.swapped(lr, ls ^ (1 << bit))

        return target

    def last(self, bit):
        def target(rep, shard):
            lr, ls = self.swapped(rep, shard)
            return (lr, ls ^ (1 << bit))

        return target

    def flip_rep(self, bit):
        return lambda rep, shard: (rep ^ (1 << bit), shard)

    def flip_shard(self, bit):
        return lambda rep, shard: (rep, shard ^ (1 << bit))

    def doubling(self):
        return list(range(len(self.order)))[::-1]

    def places(self):
        out = [0] * self.shards
        for place in range(self.shards):
            distance = 0
            for k, bit in enumerate(self.doubling()):
                if (place >> k) & 1:
                    distance |= 1 << bit
            out[distance] = place
        return out

    def masks(self):
        count = len(self.order)
        out = []
        for place in range(self.shards):
            mask = 0
            for k, bit in enumerate(self.order):
                if not (place >> (count - 1 - k)) & 1:
                    mask |= 1 << bit
            out.append(mask)
        return out


def after(value, *others):
    return lax.optimization_barrier((value, others))[0]


def gather_pieces(grid, blocks):
    mine = []
    before = [None] * len(grid.order)
    for number, block in enumerate(blocks):
        held = block[None]
        for k, bit in enumerate(grid.doubling()):
            last = k == len(before) - 1
            if before[k] is not None:
                held = after(held, before[k])
            before[k] = grid.move(held, grid.flip_shard(bit))
            if not (last and number == len(blocks) - 1):
                held = jnp.concatenate([held, before[k]], axis=0)
        mine.append(held)
    return mine, before


class Sums:
    def __init__(self, grid, away, home):
        self.grid = grid
        self.stage = 0
        self.away, self.home = away, home
        self.send()

    def send(self):
        grid, bit = self.grid, self.grid.order[self.stage]
        if self.stage == len(grid.order) - 1:
            self.got = (grid.move(self.away, grid.last(bit)), grid.move(self.home, grid.swapped))
        else:
            self.got = grid.move(self.away, grid.partner(bit))

    def step(self, late, hold=False):
        self.got = after(self.got, late)
        self.away, self.home = split_sum(self.home, self.got)
        self.stage += 1
        if not hold:
            self.send()
        return (self.away, self.home)

    def join(self, other):
        self.away = jnp.concatenate([self.away, other.away], axis=-1)
        self.home = jnp.concatenate([self.home, other.home], axis=-1)
        self.send()

    def result(self, late):
        while self.stage < len(self.grid.order) - 1:
            self.step(late)
        return (self.got[0], self.home, self.got[1])


def butterfly(grid, value, moves):
    for move in moves:
        value = jax.tree.map(lambda v: v + grid.move(v, move), value)
    return value


def sum_all(grid, value, beside=None):
    rep = lax.axis_index("rep")
    bits = range(grid.reps.bit_length() - 1)
    pad = -value.shape[1] % (128 * grid.reps)
    columns = value.shape[1]
    value = jnp.pad(value, ((0, 0), (0, pad)))
    for bit in bits:
        half = value.shape[1] // 2
        upper = (rep >> bit) % 2 == 1
        low, high = value[:, :half], value[:, half:]
        got = grid.move(jnp.where(upper, low, high), grid.flip_rep(bit))
        value = jnp.where(upper, high, low) + got
    for bit in range(grid.shards.bit_length() - 1):
        value = value + grid.move(value, grid.flip_shard(bit))
    if beside is not None:
        value = after(value, beside)
    for bit in reversed(bits):
        got = grid.move(value, grid.flip_rep(bit))
        upper = (rep >> bit) % 2 == 1
        value = jnp.concatenate(
            [jnp.where(upper, got, value), jnp.where(upper, value, got)], axis=1
        )
    return value[:, :columns]


def shards(
    grid,
    tokens,
    cotangent,
    segments,
    positions,
    wide_master,
    square_master,
    key_value_master,
    wide_moment,
    square_moment,
    key_value_momentum,
    wide_error,
    square_error,
    key_value_error,
    wide_factor,
    square_factor,
    key_value_factor,
    norm_gains,
    gain_moment,
):
    reps, owners = grid.reps, grid.shards
    rep = lax.axis_index("rep")
    shard = lax.axis_index("shard")
    core = rep % 2
    turn = (shard >> grid.core_bit) % 2
    logical_shard = shard + (core - turn) * (1 << grid.core_bit)

    low_square = square_master.astype(jnp.bfloat16)
    low_narrow = key_value_master.astype(jnp.bfloat16)
    pieces = []
    for j in range(PAIRS):
        pieces.append(low_square[0, :, 384 * j : 384 * j + 384])
        pieces.append(low_narrow[0, :, 128 * j : 128 * j + 128])
        pieces.append(low_narrow[1, :, 128 * j : 128 * j + 128])
    low_attn = jnp.concatenate(pieces + [low_square[1]], axis=1)
    units = wide_master.shape[2] // 3

    position = grid.swap_rows(positions)[0]
    rows = low_attn.shape[0]
    tile = units // reps
    chained = 1 if rows % 16 == 0 else 0
    gain_row = norm_gains.astype(jnp.bfloat16).reshape(1, 2 * rows)
    gain_row = jnp.pad(gain_row, ((0, 15), (0, 1024 - 2 * rows)))
    first = lax.dynamic_slice_in_dim(low_attn, core * 1024, 1024, axis=1)
    first = jnp.concatenate([first, gain_row], axis=0)
    second = lax.dynamic_slice_in_dim(low_attn, 2048 + core * 512, 512, axis=1)
    picks = [core * (reps // 2) + i for i in range(reps // 2)] if chained else []
    groups = [tuple(range(len(picks)))] if chained else []
    for k in range(chained, 3):
        groups.append((len(picks),))
        picks.append(reps * k + rep)
    cuts = list(pack_wide(wide_master, jnp.stack(picks).astype(jnp.int32), groups, tile))
    if chained:
        second = jnp.concatenate([second, cuts[0]], axis=1)
    mine, gathering = gather_pieces(grid, [first, second])
    other = [grid.move(mine[0], grid.flip_rep(0))]
    places = jnp.array(grid.places(), jnp.int32)[jnp.arange(owners) ^ shard]
    cores = core[None]
    gain_w = mine[0][:, rows, : 2 * rows].reshape(owners, 2, rows)
    gain_w = jnp.take(gain_w, places, axis=0).transpose(1, 0, 2).reshape(2, -1).astype(jnp.float32)
    natural = jnp.arange(reps, dtype=jnp.int32)
    whole = jnp.zeros((1,), jnp.int32)
    moved_tokens = grid.move(after(tokens, gathering[1]), grid.swapped)
    tokens = jnp.where(grid.stays(), tokens, moved_tokens)[0]
    moved_out = grid.move(after(cotangent, moved_tokens), grid.swapped)
    model = gain_w.shape[1]
    columns = 640 * PAIRS
    qkv_w = assemble(rows, mine[:1], other[:1], places, cores, 0, columns)

    count = tokens.shape[0]
    hidden_in = tokens.astype(jnp.float32)
    gain_attn, gain_mlp = gain_w[0], gain_w[1]
    cos, sin = rotary_tables(position, HEAD_SIZE)
    cos = jnp.concatenate([cos] * 4, axis=1)
    sin = jnp.concatenate([-sin, sin] * 2, axis=1)
    place = position[:, None]
    order = jnp.array(grid.masks(), jnp.int32) ^ logical_shard

    qkv, turned_in = project_qkv(order, tokens, gain_attn[None], qkv_w, cos, sin)
    wide_parts = [None] * chained
    for k in range(chained, 3):
        part = after(cuts[k], mine[0])
        part = lax.all_gather(part, ("rep", "shard"), axis=0, tiled=True)
        wide_parts.append((natural, whole, [part.reshape(reps, owners * rows, 3 * tile)]))
    attended, logs = attend_forward(qkv, place)
    held, got = after((mine[1], gathering[-1]), attended)
    mine[1] = jnp.concatenate([held, got], axis=0)
    other.append(grid.move(mine[1], grid.flip_rep(0)))
    d_out = jnp.where(grid.stays(), cotangent, after(moved_out, attended))[0]
    if chained:
        slots = (natural + core * (reps // 2)) % reps
        wide_parts[0] = (slots, places, [mine[1], other[1]])
        residual, normed_mid, turned_mid, out_w = project_out(
            places,
            cores,
            order,
            attended,
            tokens,
            gain_mlp[None],
            [mine[0], other[0], mine[1], other[1]],
        )
    else:
        out_w = assemble(rows, mine, other, places, cores, columns, 3072)
        residual = hidden_in + jnp.einsum(
            "tn,dn->td", attended, out_w, preferred_element_type=jnp.float32
        )
        normed_mid = normed(residual, gain_mlp).astype(jnp.bfloat16)
        turned_mid = turn_rows(normed_mid, order)
    turned_out = turn_rows(d_out, order)

    half = model // 2

    def weight_grad(turned, right):
        return Sums(
            grid,
            jnp.dot(turned[:half], right, preferred_element_type=jnp.float32).astype(jnp.bfloat16),
            jnp.dot(turned[half:], right, preferred_element_type=jnp.float32).astype(jnp.bfloat16),
        )

    wide_sums = []
    result, d_mid = residual, None
    for k in range(3):
        slots, where, weights = wide_parts[k]
        away, home, result, d_mid = mlp_part(
            reps,
            slots,
            where,
            normed_mid,
            d_out,
            turned_mid,
            turned_out,
            weights,
            result,
            d_mid,
            k == 2,
        )
        wide_sums.append(Sums(grid, away, home))
        for earlier in wide_sums[max(0, k - 2) : k]:
            d_mid, result = after((d_mid, result), earlier.step(away))
    result = grid.swap_rows(result[None])

    _, mid_back = jax.vjp(normed, residual, gain_mlp)
    d_residual, grad_gain_mlp = mid_back(d_mid)
    d_residual = d_residual + d_out.astype(jnp.float32)
    d_branch = d_residual.astype(jnp.bfloat16)
    d_attended = jnp.einsum(
        "td,dn->tn", d_branch, out_w, preferred_element_type=jnp.float32
    ).astype(jnp.bfloat16)
    out_sums = weight_grad(turn_rows(d_branch, order), attended)

    d_attended = after(d_attended, wide_sums[2].step(out_sums.away), wide_sums[0].got)
    d_stacks, pair_sums = [], []
    hold = len(grid.order) == 3
    for j in range(PAIRS):
        d_stack, away, home = attend_backward(
            qkv, d_attended, logs, place, cos, sin, turned_in, j
        )
        d_stacks.append(d_stack)
        pair_sums.append(Sums(grid, away, home))
        if j == 0:
            done = (wide_sums[1].step(d_stack), out_sums.step(d_stack), result)
        elif j == 1:
            done = (
                wide_sums[2].step(d_stack),
                out_sums.step(d_stack),
                pair_sums[0].step(d_stack),
                wide_sums[1].got,
            )
        else:
            done = (pair_sums[0].step(d_stack, hold), pair_sums[1].step(d_stack), out_sums.got)
        d_attended = after(d_attended, done, pair_sums[j].away)
        d_stacks = after(d_stacks, done, pair_sums[j].away)
    def back(j):
        return jnp.einsum(
            "tn,dn->td",
            d_stacks[j],
            qkv_w[:, 640 * j : 640 * j + 640],
            preferred_element_type=jnp.float32,
        )

    flag = grid.stays().astype(jnp.int32)[None]
    d_first = back(0) + back(1)
    d_stacks, wide_got = after(
        (d_stacks, wide_sums[2].got), pair_sums[2].step(d_first), pair_sums[1].step(d_first, hold)
    )
    wide_sums[2].got = wide_got
    spans = [(j, 0) for j in range(PAIRS)]
    late_sums = pair_sums
    if hold:
        pair_sums[0].join(pair_sums[1])
        spans = [(0, 0), (0, 640), (1, 0)]
        late_sums = [pair_sums[0], pair_sums[2]]
    mixed_wide, left_wide = mix_wide(
        flag, [part.result(d_first) for part in wide_sums], wide_error, wide_factor
    )
    mixed_out, left_out = mix_rest(
        flag,
        [out_sums.result(d_first)],
        [[(0, 0, model)]],
        [square_error[0, 1]],
        [square_factor[1]],
    )
    last_step = pair_sums[2].step(left_wide)
    d_stacks = after(d_stacks, last_step, left_out)
    d_normed_in = d_first + back(2)
    rep_moves = [grid.flip_rep(b) for b in range(reps.bit_length() - 1)]
    unit = 128 * reps
    left_early = butterfly(grid, jnp.concatenate([left_wide, left_out], axis=0), rep_moves)
    left_early = after(left_early, last_step)
    gram_early = 9 * units + model
    width = -(-(gram_early + 512) // unit) * unit
    early = contract_all(left_early, [mixed_wide, mixed_out], width)
    d_normed_in = after(d_normed_in, early)
    _, in_back = jax.vjp(normed, hidden_in, gain_attn)
    d_input, grad_gain_attn = in_back(d_normed_in)
    d_input = (d_input + d_residual).astype(jnp.bfloat16)
    early = sum_all(grid, early)
    late = d_input
    d_input = grid.swap_rows(d_input[None])
    narrow = 128 * PAIRS

    mixed_query, mixed_key, mixed_value, left_late = mix_rest(
        flag,
        [part.result(late) for part in late_sums],
        [
            [(which, at + first, at + last) for which, at in spans]
            for first, last in ((0, 384), (384, 512), (512, 640))
        ],
        [square_error[0, 0], key_value_error[0, 0], key_value_error[0, 1]],
        [square_factor[0], key_value_factor[0], key_value_factor[1]],
    )
    left_late = butterfly(grid, left_late, rep_moves)
    gram_late = columns
    gain_at = gram_late + 384
    width = -(-(gain_at + model) // unit) * unit
    gain_grad = jnp.stack([grad_gain_attn, grad_gain_mlp])
    mixed_late = [mixed_query, mixed_key, mixed_value]
    left_late = after(left_late, late)
    summed = contract_all(left_late, mixed_late, width, gain_grad)
    wide_new, wide_moment_new, wide_error_new, factor_wide = finish_wide(
        reps, early, gram_early, left_early, mixed_wide, wide_moment, wide_master
    )
    summed = butterfly(grid, summed, rep_moves + [grid.flip_shard(0)])
    summed = after(summed, wide_new)
    shard_moves = [grid.flip_shard(b) for b in range(1, owners.bit_length() - 1)]
    summed = butterfly(grid, summed, shard_moves)
    (
        square_new,
        square_moment_new,
        square_error_new,
        factor_square,
        narrow_new,
        narrow_moment_new,
        narrow_error_new,
        factor_narrow,
    ) = finish_rest(
        reps,
        [summed, early],
        [left_late, left_early],
        [mixed_query, mixed_out, mixed_key, mixed_value],
        [
            (0, 0, gram_late, 0),
            (1, 9 * units, gram_early + 384, 24),
            (0, model, gram_late + 128, 8),
            (0, model + narrow, gram_late + 256, 16),
        ],
        [
            (square_moment, square_master, rate_square),
            (key_value_momentum, key_value_master, rate_narrow),
        ],
    )
    gain_total = lax.dynamic_slice_in_dim(
        summed[:2, gain_at : gain_at + model], shard * (model // owners), model // owners, axis=1
    )
    gain_moment_new = decay_rate * gain_moment + gain_total / reps
    gains_new = norm_gains - rate_gains * gain_moment_new
    return (
        result,
        d_input,
        wide_new,
        square_new,
        narrow_new,
        wide_moment_new,
        square_moment_new,
        narrow_moment_new,
        wide_error_new,
        square_error_new,
        narrow_error_new,
        factor_wide,
        factor_square,
        factor_narrow,
        gains_new,
        gain_moment_new,
    )


def solution(mesh):
    return jax.shard_map(
        functools.partial(shards, Grid(mesh)),
        mesh=mesh,
        in_specs=(
            P(("rep", "shard"), None, None),
            P(("rep", "shard"), None, None),
            P(("rep", "shard"), None),
            P(("rep", "shard"), None),
            P(None, "shard", None),
            P(None, "shard", None),
            P(None, "shard", None),
            P(None, "shard", None),
            P(None, "shard", None),
            P(None, "shard", None),
            P("rep", None, "shard", None),
            P("rep", None, "shard", None),
            P("rep", None, "shard", None),
            P(),
            P(),
            P(),
            P(None, "shard"),
            P(None, "shard"),
        ),
        out_specs=(
            P(("rep", "shard"), None, None),
            P(("rep", "shard"), None, None),
            P(None, "shard", None),
            P(None, "shard", None),
            P(None, "shard", None),
            P(None, "shard", None),
            P(None, "shard", None),
            P(None, "shard", None),
            P("rep", None, "shard", None),
            P("rep", None, "shard", None),
            P("rep", None, "shard", None),
            P(),
            P(),
            P(),
            P(None, "shard"),
            P(None, "shard"),
        ),
        check_vma=False,
    )
```

```python
import functools

import jax
import jax.numpy as jnp
from jax import lax
from jax.experimental import pallas as pl
from jax.experimental.pallas import tpu as pltpu
from jax.sharding import PartitionSpec as P

QUERY_HEADS = 18
KEY_VALUE_HEADS = 6
HEAD_SIZE = 64
PAIRS = KEY_VALUE_HEADS // 2


eps_norm = 1e-05
theta_base = 10000.0
decay_rate = 0.9
rate_wide = 0.03
rate_square = 0.1
rate_narrow = 0.02
rate_gains = 0.01
mask_fill = -1e30
highest = lax.Precision.HIGHEST


def normed(value_heads, gain):
    return (
        value_heads
        * lax.rsqrt(jnp.mean(value_heads * value_heads, axis=-1, keepdims=True) + eps_norm)
        * gain
    )


def rotary_tables(position, width):
    halfway = width // 2
    inverse = theta_base ** (-2.0 * jnp.arange(halfway, dtype=jnp.float32) / width)
    angles = position.astype(jnp.float32)[:, None] * inverse[None, :]
    return (jnp.cos(angles), jnp.sin(angles))


BLOCK_ROWS = 256
VMEM_BYTES = 56 * 1024 * 1024


def light(flops, bytes_accessed, transcendentals):
    return pl.CostEstimate(
        flops=flops // 8, bytes_accessed=bytes_accessed // 8, transcendentals=transcendentals // 8
    )


def partner_lanes(values):
    lane = lax.broadcasted_iota(jnp.int32, values.shape, 1)
    return jnp.where(
        lane % HEAD_SIZE < HEAD_SIZE // 2,
        pltpu.roll(values, 128 - HEAD_SIZE // 2, 1),
        pltpu.roll(values, HEAD_SIZE // 2, 1),
    )


def project_kernel(
    order_ref, x_ref, gain_ref, w_ref, cos_ref, sin_ref, out_ref, turned_ref, scratch_ref
):
    x = x_ref[...].astype(jnp.float32)
    scale = lax.rsqrt(jnp.mean(x * x, axis=-1, keepdims=True) + eps_norm)
    low = (x * scale * gain_ref[...]).astype(jnp.bfloat16)
    scratch_ref[...] = low.astype(jnp.float32).T
    share = scratch_ref.shape[0] // order_ref.shape[0]
    parts = [
        scratch_ref[pl.ds(pl.multiple_of(order_ref[p] * share, 8), share), :]
        for p in range(order_ref.shape[0])
    ]
    turned_ref[...] = jnp.concatenate(parts, axis=0).astype(jnp.bfloat16)
    cos, sin = cos_ref[...], sin_ref[...]
    for first in range(0, out_ref.shape[1], 640):
        got = jnp.dot(low, w_ref[:, first : first + 640], preferred_element_type=jnp.float32)
        for at in range(0, 640, 128):
            piece = got[:, at : at + 128]
            if at < 512:
                piece = piece * cos + partner_lanes(piece) * sin
            out_ref[:, first + at : first + at + 128] = piece.astype(jnp.bfloat16)


def project_qkv(order, x, gain, weights, cos, sin):
    rows, width = x.shape
    columns = weights.shape[1]
    block = min(BLOCK_ROWS, rows)
    return pl.pallas_call(
        project_kernel,
        grid_spec=pltpu.PrefetchScalarGridSpec(
            num_scalar_prefetch=1,
            grid=(rows // block,),
            in_specs=[
                pl.BlockSpec((block, width), lambda i, order: (i, 0)),
                pl.BlockSpec((1, width), lambda i, order: (0, 0)),
                pl.BlockSpec((width, columns), lambda i, order: (0, 0)),
                pl.BlockSpec((block, 128), lambda i, order: (i, 0)),
                pl.BlockSpec((block, 128), lambda i, order: (i, 0)),
            ],
            out_specs=[
                pl.BlockSpec((block, columns), lambda i, order: (i, 0)),
                pl.BlockSpec((width, block), lambda i, order: (0, i)),
            ],
            scratch_shapes=[pltpu.VMEM((width, block), jnp.float32)],
        ),
        out_shape=[
            jax.ShapeDtypeStruct((rows, columns), jnp.bfloat16),
            jax.ShapeDtypeStruct((width, rows), jnp.bfloat16),
        ],
        compiler_params=pltpu.CompilerParams(vmem_limit_bytes=VMEM_BYTES),
        cost_estimate=pl.CostEstimate(
            flops=2 * rows * width * columns,
            bytes_accessed=2 * (rows * width * 2 + rows * columns + width * columns),
            transcendentals=0,
        ),
    )(order, x, gain, weights, cos, sin)


def spread_heads(pair, spread_ref):
    wide = pair.astype(jnp.float32)
    turned = pltpu.roll(wide, HEAD_SIZE, 1)
    low_half = lax.broadcasted_iota(jnp.int32, wide.shape, 1) < HEAD_SIZE
    zero = jnp.zeros_like(wide)
    spread_ref[0] = jnp.where(low_half, wide, zero).astype(jnp.bfloat16)
    spread_ref[1] = jnp.where(low_half, zero, turned).astype(jnp.bfloat16)
    spread_ref[2] = jnp.where(low_half, turned, zero).astype(jnp.bfloat16)
    spread_ref[3] = jnp.where(low_half, zero, wide).astype(jnp.bfloat16)


def mask_bias(position, start, keys):
    rows = position.shape[0]
    row = lax.broadcasted_iota(jnp.int32, (rows, keys), 0) + start
    column = lax.broadcasted_iota(jnp.int32, (rows, keys), 1)
    allowed = (column <= row) & (column >= row - position)
    return jnp.where(allowed, 0.0, mask_fill)


def across(left, right):
    return lax.dot_general(
        left, right, (((1,), (1,)), ((), ())), preferred_element_type=jnp.float32
    )


def forward_kernel(qkv_ref, pos_ref, out_ref, log_ref, key_ref, value_ref):
    step = pl.program_id(1)
    block = out_ref.shape[0]

    @pl.when(step == 0)
    def _():
        spread_heads(qkv_ref[:, 384:512], key_ref)
        spread_heads(qkv_ref[:, 512:640], value_ref)

    for place in range(qkv_ref.shape[0] // block):

        @pl.when(step == place)
        def _(place=place):
            start = place * block
            keys = start + block
            bias = mask_bias(pos_ref[...], start, keys)
            lane = lax.broadcasted_iota(jnp.int32, (block, 128), 1)
            logs = jnp.zeros((block, 128), jnp.float32)
            for g in range(3):
                query = qkv_ref[start:keys, 128 * g : 128 * g + 128] * 0.125
                total = jnp.zeros((block, 128), jnp.float32)
                for e in range(2):
                    head = 2 * g + e
                    which = 2 * (head // 3) + e
                    scores = across(query, key_ref[which, :keys, :]) + bias
                    top = jnp.max(scores, axis=-1, keepdims=True)
                    raised = jnp.exp(scores - top)
                    row_total = jnp.sum(raised, axis=-1, keepdims=True)
                    low = (raised * (1.0 / row_total)).astype(jnp.bfloat16)
                    total += jnp.dot(
                        low, value_ref[which, :keys, :], preferred_element_type=jnp.float32
                    )
                    logs = jnp.where(lane == head, top + jnp.log(row_total), logs)
                out_ref[:, 128 * g : 128 * g + 128] = total.astype(jnp.bfloat16)
            log_ref[0] = logs


def attend_forward(qkv, position):
    rows = qkv.shape[0]
    pairs = qkv.shape[1] // 640
    block = min(BLOCK_ROWS, rows)
    return pl.pallas_call(
        forward_kernel,
        grid=(pairs, rows // block),
        in_specs=[
            pl.BlockSpec((rows, 640), lambda j, i: (0, j)),
            pl.BlockSpec((block, 1), lambda j, i: (i, 0)),
        ],
        out_specs=[
            pl.BlockSpec((block, 384), lambda j, i: (i, j)),
            pl.BlockSpec((1, block, 128), lambda j, i: (j, i, 0)),
        ],
        out_shape=[
            jax.ShapeDtypeStruct((rows, 384 * pairs), jnp.bfloat16),
            jax.ShapeDtypeStruct((pairs, rows, 128), jnp.float32),
        ],
        scratch_shapes=[
            pltpu.VMEM((4, rows, 128), jnp.bfloat16),
            pltpu.VMEM((4, rows, 128), jnp.bfloat16),
        ],
        compiler_params=pltpu.CompilerParams(vmem_limit_bytes=VMEM_BYTES),
        cost_estimate=pl.CostEstimate(
            flops=20 * pairs * rows * rows * 128,
            bytes_accessed=8 * rows * 640 * pairs,
            transcendentals=6 * pairs * rows * rows,
        ),
    )(qkv, position)


def backward_kernel(
    qkv_ref,
    d_ref,
    log_ref,
    pos_ref,
    cos_ref,
    sin_ref,
    turned_ref,
    out_ref,
    away_ref,
    home_ref,
    key_ref,
    value_ref,
    dk_ref,
    dv_ref,
):
    step = pl.program_id(0)
    block = d_ref.shape[0]
    blocks = qkv_ref.shape[0] // block

    @pl.when(step == 0)
    def _():
        spread_heads(qkv_ref[:, 384:512], key_ref)
        spread_heads(qkv_ref[:, 512:640], value_ref)
        dk_ref[...] = jnp.zeros_like(dk_ref)
        dv_ref[...] = jnp.zeros_like(dv_ref)

    for place in range(blocks):

        @pl.when(step == place)
        def _(place=place):
            start = place * block
            keys = start + block
            bias = mask_bias(pos_ref[...], start, keys)
            logs = log_ref[0]
            cos, sin = cos_ref[start:keys, :], sin_ref[start:keys, :]
            for g in range(3):
                query = qkv_ref[start:keys, 128 * g : 128 * g + 128] * 0.125
                d_out = d_ref[:, 128 * g : 128 * g + 128]
                query_turned = query.astype(jnp.float32).T.astype(jnp.bfloat16)
                d_turned = d_out.astype(jnp.float32).T.astype(jnp.bfloat16)
                total = jnp.zeros((block, 128), jnp.float32)
                for e in range(2):
                    head = 2 * g + e
                    which = 2 * (head // 3) + e
                    at = HEAD_SIZE * (head // 3)
                    key = key_ref[which, :keys, :]
                    scores = across(query, key) + bias
                    prob = jnp.exp(scores - logs[:, head : head + 1])
                    d_prob = across(d_out, value_ref[which, :keys, :])
                    delta = jnp.sum(prob * d_prob, axis=-1, keepdims=True)
                    d_scores = (prob * (d_prob - delta)).astype(jnp.bfloat16)
                    half = slice(HEAD_SIZE * e, HEAD_SIZE * e + HEAD_SIZE)
                    dv_ref[at : at + HEAD_SIZE, :keys] += jnp.dot(
                        d_turned[half], prob.astype(jnp.bfloat16), preferred_element_type=jnp.float32
                    )
                    dk_ref[at : at + HEAD_SIZE, :keys] += jnp.dot(
                        query_turned[half], d_scores, preferred_element_type=jnp.float32
                    )
                    total += jnp.dot(d_scores, key, preferred_element_type=jnp.float32)
                total = total * 0.125
                total = total * cos - partner_lanes(total) * sin
                out_ref[start:keys, 128 * g : 128 * g + 128] = total.astype(jnp.bfloat16)

    @pl.when(step == blocks - 1)
    def _():
        d_key = dk_ref[...].T
        d_key = d_key * cos_ref[...] - partner_lanes(d_key) * sin_ref[...]
        out_ref[:, 384:512] = d_key.astype(jnp.bfloat16)
        out_ref[:, 512:640] = dv_ref[...].T.astype(jnp.bfloat16)
        half = away_ref.shape[0]
        for first, grad_ref in ((0, away_ref), (half, home_ref)):
            grad_ref[...] = jnp.dot(
                turned_ref[first : first + half, :],
                out_ref[...],
                preferred_element_type=jnp.float32,
            ).astype(jnp.bfloat16)


def attend_backward(qkv, d_attended, logs, position, cos, sin, turned, pair):
    rows = qkv.shape[0]
    model = turned.shape[0]
    block = min(BLOCK_ROWS, rows)
    half = pl.BlockSpec((model // 2, 640), lambda i: (0, 0))
    return pl.pallas_call(
        backward_kernel,
        grid=(rows // block,),
        in_specs=[
            pl.BlockSpec((rows, 640), lambda i: (0, pair)),
            pl.BlockSpec((block, 384), lambda i: (i, pair)),
            pl.BlockSpec((1, block, 128), lambda i: (pair, i, 0)),
            pl.BlockSpec((block, 1), lambda i: (i, 0)),
            pl.BlockSpec((rows, 128), lambda i: (0, 0)),
            pl.BlockSpec((rows, 128), lambda i: (0, 0)),
            pl.BlockSpec((model, rows), lambda i: (0, 0), pipeline_mode=pl.Buffered(1)),
        ],
        out_specs=[pl.BlockSpec((rows, 640), lambda i: (0, 0)), half, half],
        out_shape=[
            jax.ShapeDtypeStruct((rows, 640), jnp.bfloat16),
            jax.ShapeDtypeStruct((model // 2, 640), jnp.bfloat16),
            jax.ShapeDtypeStruct((model // 2, 640), jnp.bfloat16),
        ],
        scratch_shapes=[
            pltpu.VMEM((4, rows, 128), jnp.bfloat16),
            pltpu.VMEM((4, rows, 128), jnp.bfloat16),
            pltpu.VMEM((128, rows), jnp.float32),
            pltpu.VMEM((128, rows), jnp.float32),
        ],
        compiler_params=pltpu.CompilerParams(vmem_limit_bytes=VMEM_BYTES),
        cost_estimate=pl.CostEstimate(
            flops=50 * rows * rows * 128,
            bytes_accessed=8 * rows * 640,
            transcendentals=6 * rows * rows,
        ),
    )(qkv, d_attended, logs, position, cos, sin, turned)


def turn_kernel(order_ref, rows_ref, out_ref, turned_ref):
    turned_ref[...] = rows_ref[...].astype(jnp.float32).T
    owners = order_ref.shape[0]
    share = turned_ref.shape[0] // owners
    parts = [
        turned_ref[pl.ds(pl.multiple_of(order_ref[p] * share, 8), share), :] for p in range(owners)
    ]
    out_ref[...] = jnp.concatenate(parts, axis=0).astype(jnp.bfloat16)


def turn_rows(rows, order):
    count, model = rows.shape
    block = min(BLOCK_ROWS, count)
    return pl.pallas_call(
        turn_kernel,
        grid_spec=pltpu.PrefetchScalarGridSpec(
            num_scalar_prefetch=1,
            grid=(count // block,),
            in_specs=[pl.BlockSpec((block, model), lambda i, order: (i, 0))],
            out_specs=pl.BlockSpec((model, block), lambda i, order: (0, i)),
            scratch_shapes=[pltpu.VMEM((model, block), jnp.float32)],
        ),
        out_shape=jax.ShapeDtypeStruct((model, count), jnp.bfloat16),
        compiler_params=pltpu.CompilerParams(vmem_limit_bytes=VMEM_BYTES),
        cost_estimate=pl.CostEstimate(
            flops=0, bytes_accessed=4 * count * model, transcendentals=0
        ),
    )(order, rows)


def mlp_kernel(reps, first, last, slot_ref, place_ref, mid_ref, d_ref, *refs):
    del slot_ref
    mid_hbm, d_hbm = refs[:2]
    befores = refs[2 : 3 if first else 4]
    refs = refs[2 + len(befores) :]
    weight_hbm, refs = (refs[:1], refs[1:]) if place_ref.shape[0] == 1 else (refs[:2], refs[2:])
    away_ref, home_ref, result_ref, back_ref = refs[:4]
    weight_ref, mid_turned_ref, d_turned_ref, d_pair_ref, hidden_ref, weight_sem, sem = refs[4:11]
    output_ref = result_ref
    if last:
        result_ref = refs[11]
    step = pl.program_id(0)
    count = mid_ref.shape[0]
    part = min(512, count)
    tile = hidden_ref.shape[1]
    half = away_ref.shape[1]

    wide = 3 * tile
    skip = weight_hbm[0].shape[2] - wide * (reps // 2)

    def load(i):
        if len(weight_hbm) == 1:
            pltpu.make_async_copy(
                weight_hbm[0].at[i], weight_ref.at[i], weight_sem.at[i]
            ).start()
            return
        ref, at = weight_hbm[2 * i // reps], i % (reps // 2)
        owners, share = ref.shape[:2]
        for a in range(owners):
            pltpu.make_async_copy(
                ref.at[place_ref[a], :, skip + wide * at : skip + wide * at + wide],
                weight_ref.at[i, share * a : share * a + share, :],
                weight_sem.at[i],
            ).start()

    sums = [pltpu.make_async_copy(befores[0], result_ref, sem.at[0])]
    if not first:
        sums.append(pltpu.make_async_copy(befores[1], back_ref, sem.at[1]))
    turned = [
        pltpu.make_async_copy(mid_hbm, mid_turned_ref, sem.at[2]),
        pltpu.make_async_copy(d_hbm, d_turned_ref, sem.at[3]),
    ]

    @pl.when(step == 0)
    def _():
        load(0)
        for copy in sums + turned:
            copy.start()
        for i in range(1, reps):
            load(i)
        if first:
            back_ref[...] = jnp.zeros_like(back_ref)

    for i in range(reps):

        @pl.when(step == i)
        def _(i=i):
            pltpu.make_async_copy(weight_ref.at[i], weight_ref.at[i], weight_sem.at[i]).wait()

    @pl.when(step == 0)
    def _():
        for copy in sums:
            copy.wait()

    @pl.loop(0, count // part)
    def _(t):
        rows = pl.ds(pl.multiple_of(t * part, part), part)
        pair_w = weight_ref[step, :, : 2 * tile]
        down_w = weight_ref[step, :, 2 * tile :]
        pair = jnp.dot(mid_ref[rows, :], pair_w, preferred_element_type=jnp.float32)
        d_hidden = jnp.dot(d_ref[rows, :], down_w, preferred_element_type=jnp.float32)
        gate, up = pair[:, :tile], pair[:, tile:]
        sig = jax.nn.sigmoid(gate)
        silu = gate * sig
        hidden = (silu * up).astype(jnp.bfloat16)
        hidden_ref[rows, :] = hidden
        d_gate = d_hidden * up * (sig * (1.0 + gate * (1.0 - sig)))
        d_pair_ref[rows, :tile] = d_gate.astype(jnp.bfloat16)
        d_pair_ref[rows, tile:] = (d_hidden * silu).astype(jnp.bfloat16)
        back_ref[rows, :] += across(d_pair_ref[rows, :], pair_w)
        result_ref[rows, :] += across(hidden, down_w)
        if last:

            @pl.when(step == reps - 1)
            def _():
                output_ref[rows, :] = result_ref[rows, :].astype(jnp.bfloat16)

    @pl.when(step == 0)
    def _():
        for copy in turned:
            copy.wait()

    for at, out_ref in ((0, away_ref), (half, home_ref)):
        pair = jnp.dot(
            mid_turned_ref[at : at + half, :], d_pair_ref[...], preferred_element_type=jnp.float32
        )
        out_ref[0] = pair[:, :tile].astype(jnp.bfloat16)
        out_ref[1] = pair[:, tile:].astype(jnp.bfloat16)
        out_ref[2] = jnp.dot(
            d_turned_ref[at : at + half, :], hidden_ref[...], preferred_element_type=jnp.float32
        ).astype(jnp.bfloat16)


def mlp_part(reps, slots, places, mid, d_out, mid_turned, d_turned, weights, result, back, last):
    count, model = mid.shape
    tile = (weights[0].shape[2] - (512 if len(weights) == 2 else 0)) // 3
    if len(weights) == 2:
        tile //= reps // 2
    units = tile * reps
    half = model // 2
    first = back is None
    befores = [result] if first else [result, back]

    def once(shape):
        return pl.BlockSpec(shape, lambda i, slots, places: (0, 0), pipeline_mode=pl.Buffered(1))

    anywhere = pl.BlockSpec(memory_space=pl.ANY)
    return pl.pallas_call(
        functools.partial(mlp_kernel, reps, first, last),
        grid_spec=pltpu.PrefetchScalarGridSpec(
            num_scalar_prefetch=2,
            grid=(reps,),
            in_specs=[once((count, model))] * 2 + [anywhere] * (2 + len(befores) + len(weights)),
            out_specs=[
                pl.BlockSpec((3, half, tile), lambda i, slots, places: (0, 0, slots[i])),
                pl.BlockSpec((3, half, tile), lambda i, slots, places: (0, 0, slots[i])),
                once((count, model)),
                once((count, model)),
            ],
            scratch_shapes=[
                pltpu.VMEM((reps, model, 3 * tile), jnp.bfloat16),
                pltpu.VMEM((model, count), jnp.bfloat16),
                pltpu.VMEM((model, count), jnp.bfloat16),
                pltpu.VMEM((count, 2 * tile), jnp.bfloat16),
                pltpu.VMEM((count, tile), jnp.bfloat16),
                pltpu.SemaphoreType.DMA((reps,)),
                pltpu.SemaphoreType.DMA((4,)),
            ]
            + ([pltpu.VMEM((count, model), jnp.float32)] if last else []),
        ),
        out_shape=[
            jax.ShapeDtypeStruct((3, half, units), jnp.bfloat16),
            jax.ShapeDtypeStruct((3, half, units), jnp.bfloat16),
            jax.ShapeDtypeStruct((count, model), jnp.bfloat16 if last else jnp.float32),
            jax.ShapeDtypeStruct((count, model), jnp.float32),
        ],
        compiler_params=pltpu.CompilerParams(vmem_limit_bytes=VMEM_BYTES),
        cost_estimate=pl.CostEstimate(
            flops=18 * count * model * units,
            bytes_accessed=2 * (4 * count * model + 6 * model * units) + 16 * count * model,
            transcendentals=count * units,
        ),
    )(slots, places, mid, d_out, mid_turned, d_turned, *befores, *weights)


def assemble(rows, mine, other, places, core, low, high):
    owners = mine[0].shape[0]
    widths = [m.shape[2] for m in mine]
    count = len(mine)

    def kernel(place_ref, core_ref, *refs):
        del place_ref
        out_ref = refs[-1]
        for own in range(2):

            @pl.when(core_ref[0] == own)
            def _(own=own):
                at = 0
                for i in range(count):
                    for half in range(2):
                        ref = refs[i] if half == own else refs[count + i]
                        first, last = max(low, at), min(high, at + widths[i])
                        if first < last:
                            out_ref[0, :, first - low : last - low] = ref[
                                0, :, first - at : last - at
                            ]
                        at += widths[i]

    def spec(width):
        return pl.BlockSpec((1, rows, width), lambda a, place, core: (place[a], 0, 0))

    out = pl.pallas_call(
        kernel,
        grid_spec=pltpu.PrefetchScalarGridSpec(
            num_scalar_prefetch=2,
            grid=(owners,),
            in_specs=[spec(w) for w in widths] * 2,
            out_specs=pl.BlockSpec((1, rows, high - low), lambda a, place, core: (a, 0, 0)),
        ),
        out_shape=jax.ShapeDtypeStruct((owners, rows, high - low), jnp.bfloat16),
        compiler_params=pltpu.CompilerParams(vmem_limit_bytes=VMEM_BYTES),
        cost_estimate=pl.CostEstimate(
            flops=0, bytes_accessed=8 * owners * rows * sum(widths), transcendentals=0
        ),
    )(places, core, *mine, *other)
    return out.reshape(owners * rows, high - low)


def left_rows(factor, rows):
    lane = lax.broadcasted_iota(jnp.int32, (rows.shape[0], 128), 1)
    columns = jnp.zeros((rows.shape[0], 128), jnp.float32)
    for r in range(8):
        column = jnp.sum(rows * factor[r : r + 1, :], axis=1, keepdims=True)
        columns = jnp.where(lane == r, column, columns)
    return columns.T[:8, :]


def exact_dot(left, right, contract):
    return lax.dot_general(
        left, right, (contract, ((), ())), precision=highest, preferred_element_type=jnp.float32
    )


def mix_kernel(layout, count, flag_ref, *refs):
    sums, refs = refs[: 3 * count], refs[3 * count :]
    errors, refs = refs[: len(layout)], refs[len(layout) :]
    factors, refs = refs[: len(layout)], refs[len(layout) :]
    mixed, left_ref = refs[: len(layout)], refs[len(layout)]
    stays = flag_ref[0] == 1
    for m, pieces in enumerate(layout):
        at = 0
        for which, first, last in pieces:
            away, home, moved = (
                sums[3 * which + k][..., first:last].astype(jnp.float32) for k in range(3)
            )
            width = last - first
            where = (..., slice(at, at + width))
            total = away + jnp.where(stays, home, moved)
            total = total.reshape(total.shape[-2:])
            error = errors[m][where]
            error = error.reshape(error.shape[-2:])
            mixed[m][where] = (total + error).reshape(mixed[m].shape[:-1] + (width,))
            at += width
        rows = mixed[m][...].reshape(mixed[m].shape[-2:])
        factor = factors[m][...].reshape(factors[m].shape[-2:])
        left_ref[8 * m : 8 * m + 8, :] = left_rows(factor, rows)


def mix_wide(flag, parts, error, factor):
    count, rows, third = parts[0][0].shape
    columns = third * len(parts)
    arrays = [a for part in parts for a in part]
    layout = [[(i, 0, third) for i in range(len(parts))]]
    return pl.pallas_call(
        functools.partial(mix_kernel, layout, len(parts)),
        grid_spec=pltpu.PrefetchScalarGridSpec(
            num_scalar_prefetch=1,
            grid=(count,),
            in_specs=[pl.BlockSpec((1, rows, third), lambda i, flag: (i, 0, 0))] * len(arrays)
            + [
                pl.BlockSpec((1, 1, rows, columns), lambda i, flag: (0, i, 0, 0)),
                pl.BlockSpec((1, 8, columns), lambda i, flag: (i, 0, 0)),
            ],
            out_specs=[
                pl.BlockSpec((1, rows, columns), lambda i, flag: (i, 0, 0)),
                pl.BlockSpec((8, rows), lambda i, flag: (i, 0)),
            ],
        ),
        out_shape=[
            jax.ShapeDtypeStruct((count, rows, columns), jnp.float32),
            jax.ShapeDtypeStruct((8 * count, rows), jnp.float32),
        ],
        compiler_params=pltpu.CompilerParams(vmem_limit_bytes=VMEM_BYTES),
        cost_estimate=pl.CostEstimate(
            flops=96 * count * rows * columns,
            bytes_accessed=14 * count * rows * columns,
            transcendentals=0,
        ),
    )(flag, *arrays, error, factor)


def in_vmem(count):
    return [pl.BlockSpec(memory_space=pltpu.VMEM)] * count


def mix_rest(flag, parts, layout, errors, factors):
    rows = errors[0].shape[0]
    arrays = [a for part in parts for a in part]
    return pl.pallas_call(
        functools.partial(mix_kernel, layout, len(parts)),
        in_specs=[pl.BlockSpec(memory_space=pltpu.SMEM)]
        + in_vmem(len(arrays) + len(errors) + len(factors)),
        out_specs=in_vmem(len(errors) + 1),
        out_shape=[jax.ShapeDtypeStruct(e.shape, jnp.float32) for e in errors]
        + [jax.ShapeDtypeStruct((8 * len(errors), rows), jnp.float32)],
        compiler_params=pltpu.CompilerParams(vmem_limit_bytes=VMEM_BYTES),
        cost_estimate=pl.CostEstimate(
            flops=96 * sum(e.size for e in errors),
            bytes_accessed=14 * sum(e.size for e in errors),
            transcendentals=0,
        ),
    )(flag, *arrays, *errors, *factors)


def contract_all(left, mixed, width, extra=None):
    def kernel(*refs):
        left_ref, out_ref = refs[0], refs[-1]
        out_ref[...] = jnp.zeros_like(out_ref)
        at, m = 0, 0
        for ref in refs[1 : 1 + len(mixed)]:
            for k in range(ref.shape[0] if len(ref.shape) == 3 else 1):
                rows = ref[k] if len(ref.shape) == 3 else ref[...]
                own = left_ref[8 * m : 8 * m + 8, :]
                out_ref[:, at : at + rows.shape[1]] = exact_dot(own, rows, ((1,), (0,)))
                at += rows.shape[1]
                m += 1
        for k in range(m):
            own = left_ref[8 * k : 8 * k + 8, :]
            out_ref[:, at : at + 8] = exact_dot(own, own, ((1,), (1,)))
            at += 128
        if extra is not None:
            out_ref[: extra.shape[0], at : at + extra.shape[1]] = refs[-2][...]

    more = [] if extra is None else [extra]
    return pl.pallas_call(
        kernel,
        in_specs=in_vmem(1 + len(mixed) + len(more)),
        out_specs=pl.BlockSpec(memory_space=pltpu.VMEM),
        out_shape=jax.ShapeDtypeStruct((8, width), jnp.float32),
        compiler_params=pltpu.CompilerParams(vmem_limit_bytes=VMEM_BYTES),
        cost_estimate=pl.CostEstimate(
            flops=96 * sum(m.size for m in mixed),
            bytes_accessed=4 * sum(m.size for m in mixed),
            transcendentals=0,
        ),
    )(left, *mixed, *more)


def eliminate(gram, rights):
    row = lax.broadcasted_iota(jnp.int32, (8, 1), 0)
    for j in range(8):
        scale = 1.0 / jnp.sqrt(gram[j : j + 1, j : j + 1])
        below = jnp.where(row > j, gram[:, j : j + 1] * scale, 0.0)
        done = []
        for right in [gram] + list(rights):
            top = right[j : j + 1, :] * scale
            done.append(jnp.where(row == j, top, right - below * top))
        gram, rights = done[0], done[1:]
    return rights


def finish_matrix(reps, rate, row, gram, left, mixed, moment, master, outs):
    new_ref, moment_new_ref, error_ref, factor_ref = outs
    factor, basis = eliminate(gram[:, :8] * (1.0 / reps), [row, left])
    factor = factor * (1.0 / reps)
    factor_ref[...] = factor
    turned = basis.T
    columns = factor.shape[1]
    for first in range(0, columns, 256):
        span = slice(first, min(first + 256, columns))
        approx = turned[:, 0:1] * factor[0:1, span]
        for r in range(1, 8):
            approx += turned[:, r : r + 1] * factor[r : r + 1, span]
        moment_new = decay_rate * moment[:, span] + approx
        moment_new_ref[:, span] = moment_new
        new_ref[:, span] = master[:, span] - rate * moment_new
        error_ref[:, span] = mixed[:, span] - approx


def finish_wide(reps, packed, gram_at, left, mixed, moment, master):
    count, rows, columns = mixed.shape

    def kernel(row_ref, gram_ref, left_ref, mixed_ref, moment_ref, master_ref, *outs):
        new_ref, moment_new_ref, error_ref, factor_ref = outs
        finish_matrix(
            reps,
            rate_wide,
            row_ref[...],
            gram_ref[...],
            left_ref[...],
            mixed_ref.at[0],
            moment_ref.at[0],
            master_ref.at[0],
            (new_ref.at[0], moment_new_ref.at[0], error_ref.at[0, 0], factor_ref.at[0]),
        )

    whole = pl.BlockSpec((1, rows, columns), lambda i: (i, 0, 0))
    shape = jax.ShapeDtypeStruct((count, rows, columns), jnp.float32)
    return pl.pallas_call(
        kernel,
        grid=(count,),
        in_specs=[
            pl.BlockSpec((8, columns), lambda i: (0, i)),
            pl.BlockSpec((8, 128), lambda i: (0, gram_at // 128 + i)),
            pl.BlockSpec((8, rows), lambda i: (i, 0)),
            whole,
            whole,
            whole,
        ],
        out_specs=[
            whole,
            whole,
            pl.BlockSpec((1, 1, rows, columns), lambda i: (0, i, 0, 0)),
            pl.BlockSpec((1, 8, columns), lambda i: (i, 0, 0)),
        ],
        out_shape=[
            shape,
            shape,
            jax.ShapeDtypeStruct((1, count, rows, columns), jnp.float32),
            jax.ShapeDtypeStruct((count, 8, columns), jnp.float32),
        ],
        compiler_params=pltpu.CompilerParams(vmem_limit_bytes=VMEM_BYTES),
        cost_estimate=light(
            flops=96 * count * rows * columns,
            bytes_accessed=24 * count * rows * columns,
            transcendentals=0,
        ),
    )(packed, packed, left, mixed, moment, master)


def finish_rest(reps, packs, lefts, mixed, where, states):
    groups = []
    at = 0
    for moment, _, rate in states:
        groups.append((at, moment.shape[0], rate))
        at += moment.shape[0]

    def kernel(*refs):
        pack_refs, refs = refs[: len(packs)], refs[len(packs) :]
        left_refs, refs = refs[: len(lefts)], refs[len(lefts) :]
        mixed_refs, refs = refs[: len(mixed)], refs[len(mixed) :]
        state_refs, outs = refs[: 2 * len(states)], refs[2 * len(states) :]
        for g, (first, count, rate) in enumerate(groups):
            new_ref, moment_new_ref, error_ref, factor_ref = outs[4 * g : 4 * g + 4]
            for k in range(count):
                pack, row_at, gram_at, left_at = where[first + k]
                rows = mixed_refs[first + k]
                finish_matrix(
                    reps,
                    rate,
                    pack_refs[pack][:, row_at : row_at + rows.shape[1]],
                    pack_refs[pack][:, gram_at : gram_at + 128],
                    left_refs[pack][left_at : left_at + 8, :],
                    rows,
                    state_refs[2 * g].at[k],
                    state_refs[2 * g + 1].at[k],
                    (new_ref.at[k], moment_new_ref.at[k], error_ref.at[0, k], factor_ref.at[k]),
                )

    shapes = []
    for moment, _, _ in states:
        count, rows, columns = moment.shape
        shapes += [
            jax.ShapeDtypeStruct(moment.shape, jnp.float32),
            jax.ShapeDtypeStruct(moment.shape, jnp.float32),
            jax.ShapeDtypeStruct((1,) + moment.shape, jnp.float32),
            jax.ShapeDtypeStruct((count, 8, columns), jnp.float32),
        ]
    arrays = [a for state in states for a in state[:2]]
    return pl.pallas_call(
        kernel,
        in_specs=in_vmem(len(packs) + len(lefts) + len(mixed) + len(arrays)),
        out_specs=in_vmem(len(shapes)),
        out_shape=shapes,
        compiler_params=pltpu.CompilerParams(vmem_limit_bytes=VMEM_BYTES),
        cost_estimate=light(
            flops=96 * sum(m.size for m in mixed),
            bytes_accessed=24 * sum(m.size for m in mixed),
            transcendentals=0,
        ),
    )(*packs, *lefts, *mixed, *arrays)


def pack_wide(master, picks, groups, tile):
    count, rows, _ = master.shape
    number = picks.shape[0]

    def kernel(pick_ref, *refs):
        del pick_ref
        for group, out_ref in zip(groups, refs[number:]):
            at = 0
            for pick in group:
                for i in range(count):
                    out_ref[:, at : at + tile] = refs[pick][i].astype(jnp.bfloat16)
                    at += tile

    def spec(n):
        return pl.BlockSpec((count, rows, tile), lambda i, picks: (0, 0, picks[n]))

    shapes = [
        jax.ShapeDtypeStruct((rows, count * tile * len(group)), jnp.bfloat16) for group in groups
    ]
    return pl.pallas_call(
        kernel,
        grid_spec=pltpu.PrefetchScalarGridSpec(
            num_scalar_prefetch=1,
            grid=(1,),
            in_specs=[spec(n) for n in range(number)],
            out_specs=[pl.BlockSpec(s.shape, lambda i, picks: (0, 0)) for s in shapes],
        ),
        out_shape=shapes,
        compiler_params=pltpu.CompilerParams(vmem_limit_bytes=VMEM_BYTES),
        cost_estimate=pl.CostEstimate(
            flops=0, bytes_accessed=6 * number * count * rows * tile, transcendentals=0
        ),
    )(picks, *[master] * number)


def split_sum(home, got):
    shape = home.shape
    rows, columns = shape[-2:]
    lead = home.size // (rows * columns)
    half = rows // 2

    def kernel(home_ref, got_ref, away_ref, kept_ref):
        total = home_ref[0].astype(jnp.float32) + got_ref[0].astype(jnp.float32)
        away_ref[0] = total[:half].astype(jnp.bfloat16)
        kept_ref[0] = total[half:].astype(jnp.bfloat16)

    whole = pl.BlockSpec((1, rows, columns), lambda i: (i, 0, 0))
    part = pl.BlockSpec((1, half, columns), lambda i: (i, 0, 0))
    out = jax.ShapeDtypeStruct((lead, half, columns), jnp.bfloat16)
    away, kept = pl.pallas_call(
        kernel,
        grid=(lead,),
        in_specs=[whole, whole],
        out_specs=[part, part],
        out_shape=[out, out],
        compiler_params=pltpu.CompilerParams(vmem_limit_bytes=VMEM_BYTES),
        cost_estimate=pl.CostEstimate(
            flops=home.size, bytes_accessed=6 * home.size, transcendentals=0
        ),
    )(home.reshape(lead, rows, columns), got.reshape(lead, rows, columns))
    tail = (half, columns)
    return away.reshape(shape[:-2] + tail), kept.reshape(shape[:-2] + tail)


def out_kernel(owners, place_ref, core_ref, order_ref, att_ref, x_ref, gain_ref, *refs):
    halves, refs = refs[:4], refs[4:]
    residual_ref, mid_ref, mid_turned_ref, w_ref, turned_ref, sem = refs
    share = w_ref.shape[0] // owners

    @pl.when(pl.program_id(0) == 0)
    def _():
        for own in range(2):

            @pl.when(core_ref[0] == own)
            def _(own=own):
                spans = (
                    (halves[0 if own == 1 else 1], 896, 0, 128),
                    (halves[2 if own == 0 else 3], 0, 128, 512),
                    (halves[2 if own == 1 else 3], 0, 640, 512),
                )
                for ref, first, at, width in spans:
                    for a in range(owners):
                        pltpu.make_async_copy(
                            ref.at[place_ref[a], :share, first : first + width],
                            w_ref.at[share * a : share * a + share, at : at + width],
                            sem.at[0],
                        ).start()

        pltpu.make_async_copy(w_ref, w_ref, sem.at[0]).wait()

    residual = x_ref[...].astype(jnp.float32) + across(att_ref[...], w_ref[...])
    residual_ref[...] = residual
    scale = lax.rsqrt(jnp.mean(residual * residual, axis=-1, keepdims=True) + eps_norm)
    mid = (residual * scale * gain_ref[...]).astype(jnp.bfloat16)
    mid_ref[...] = mid
    turned_ref[...] = mid.astype(jnp.float32).T
    parts = [
        turned_ref[pl.ds(pl.multiple_of(order_ref[p] * share, 8), share), :] for p in range(owners)
    ]
    mid_turned_ref[...] = jnp.concatenate(parts, axis=0).astype(jnp.bfloat16)


def project_out(places, core, order, attended, x, gain, halves):
    count, model = x.shape
    owners = order.shape[0]
    block = min(BLOCK_ROWS, count)
    rows = pl.BlockSpec((block, model), lambda i, *_: (i, 0))
    return pl.pallas_call(
        functools.partial(out_kernel, owners),
        grid_spec=pltpu.PrefetchScalarGridSpec(
            num_scalar_prefetch=3,
            grid=(count // block,),
            in_specs=[rows, rows, pl.BlockSpec((1, model), lambda i, *_: (0, 0))]
            + [pl.BlockSpec(memory_space=pl.ANY)] * 4,
            out_specs=[
                rows,
                rows,
                pl.BlockSpec((model, block), lambda i, *_: (0, i)),
                pl.BlockSpec((model, model), lambda i, *_: (0, 0)),
            ],
            scratch_shapes=[
                pltpu.VMEM((model, block), jnp.float32),
                pltpu.SemaphoreType.DMA((1,)),
            ],
        ),
        out_shape=[
            jax.ShapeDtypeStruct((count, model), jnp.float32),
            jax.ShapeDtypeStruct((count, model), jnp.bfloat16),
            jax.ShapeDtypeStruct((model, count), jnp.bfloat16),
            jax.ShapeDtypeStruct((model, model), jnp.bfloat16),
        ],
        compiler_params=pltpu.CompilerParams(vmem_limit_bytes=VMEM_BYTES),
        cost_estimate=pl.CostEstimate(
            flops=2 * count * model * model,
            bytes_accessed=12 * count * model + 4 * model * model,
            transcendentals=count,
        ),
    )(places, core, order, attended, x, gain, *halves)


class Grid:
    def __init__(self, mesh):
        self.reps = mesh.shape["rep"]
        self.shards = mesh.shape["shard"]
        self.core_bit = self.shards.bit_length() - 3
        stages = self.shards.bit_length() - 1
        self.order = [self.core_bit] + [b for b in range(stages) if b != self.core_bit]

    def swapped(self, rep, shard):
        bit = self.core_bit
        core = rep & 1
        turn = (shard >> bit) & 1
        return (rep - core + turn, shard - (turn << bit) + (core << bit))

    def flat(self, pair):
        return pair[0] * self.shards + pair[1]

    def every(self):
        return [(r, s) for r in range(self.reps) for s in range(self.shards)]

    def move(self, value, target):
        pairs = [(self.flat(p), self.flat(target(*p))) for p in self.every() if target(*p) != p]
        return lax.ppermute(value, ("rep", "shard"), pairs)

    def stays(self):
        return lax.axis_index("rep") % 2 == (lax.axis_index("shard") >> self.core_bit) % 2

    def swap_rows(self, value):
        return jnp.where(self.stays(), value, self.move(value, self.swapped))

    def partner(self, bit):
        def target(rep, shard):
            lr, ls = self.swapped(rep, shard)
            return self.swapped(lr, ls ^ (1 << bit))

        return target

    def last(self, bit):
        def target(rep, shard):
            lr, ls = self.swapped(rep, shard)
            return (lr, ls ^ (1 << bit))

        return target

    def flip_rep(self, bit):
        return lambda rep, shard: (rep ^ (1 << bit), shard)

    def flip_shard(self, bit):
        return lambda rep, shard: (rep, shard ^ (1 << bit))

    def doubling(self):
        return list(range(len(self.order)))[::-1]

    def places(self):
        out = [0] * self.shards
        for place in range(self.shards):
            distance = 0
            for k, bit in enumerate(self.doubling()):
                if (place >> k) & 1:
                    distance |= 1 << bit
            out[distance] = place
        return out

    def masks(self):
        count = len(self.order)
        out = []
        for place in range(self.shards):
            mask = 0
            for k, bit in enumerate(self.order):
                if not (place >> (count - 1 - k)) & 1:
                    mask |= 1 << bit
            out.append(mask)
        return out


def after(value, *others):
    return lax.optimization_barrier((value, others))[0]


def gather_pieces(grid, blocks):
    mine = []
    before = [None] * len(grid.order)
    for number, block in enumerate(blocks):
        held = block[None]
        for k, bit in enumerate(grid.doubling()):
            last = k == len(before) - 1
            if before[k] is not None:
                held = after(held, before[k])
            before[k] = grid.move(held, grid.flip_shard(bit))
            if not (last and number == len(blocks) - 1):
                held = jnp.concatenate([held, before[k]], axis=0)
        mine.append(held)
    return mine, before


class Sums:
    def __init__(self, grid, away, home):
        self.grid = grid
        self.stage = 0
        self.away, self.home = away, home
        self.send()

    def send(self):
        grid, bit = self.grid, self.grid.order[self.stage]
        if self.stage == len(grid.order) - 1:
            self.got = (grid.move(self.away, grid.last(bit)), grid.move(self.home, grid.swapped))
        else:
            self.got = grid.move(self.away, grid.partner(bit))

    def step(self, late, hold=False):
        self.got = after(self.got, late)
        self.away, self.home = split_sum(self.home, self.got)
        self.stage += 1
        if not hold:
            self.send()
        return (self.away, self.home)

    def join(self, other):
        self.away = jnp.concatenate([self.away, other.away], axis=-1)
        self.home = jnp.concatenate([self.home, other.home], axis=-1)
        self.send()

    def result(self, late):
        while self.stage < len(self.grid.order) - 1:
            self.step(late)
        return (self.got[0], self.home, self.got[1])


def butterfly(grid, value, moves):
    for move in moves:
        value = jax.tree.map(lambda v: v + grid.move(v, move), value)
    return value


def sum_all(grid, value, beside=None):
    rep = lax.axis_index("rep")
    bits = range(grid.reps.bit_length() - 1)
    pad = -value.shape[1] % (128 * grid.reps)
    columns = value.shape[1]
    value = jnp.pad(value, ((0, 0), (0, pad)))
    for bit in bits:
        half = value.shape[1] // 2
        upper = (rep >> bit) % 2 == 1
        low, high = value[:, :half], value[:, half:]
        got = grid.move(jnp.where(upper, low, high), grid.flip_rep(bit))
        value = jnp.where(upper, high, low) + got
    for bit in range(grid.shards.bit_length() - 1):
        value = value + grid.move(value, grid.flip_shard(bit))
    if beside is not None:
        value = after(value, beside)
    for bit in reversed(bits):
        got = grid.move(value, grid.flip_rep(bit))
        upper = (rep >> bit) % 2 == 1
        value = jnp.concatenate(
            [jnp.where(upper, got, value), jnp.where(upper, value, got)], axis=1
        )
    return value[:, :columns]


def shards(
    grid,
    tokens,
    cotangent,
    segments,
    positions,
    wide_master,
    square_master,
    key_value_master,
    wide_moment,
    square_moment,
    key_value_momentum,
    wide_error,
    square_error,
    key_value_error,
    wide_factor,
    square_factor,
    key_value_factor,
    norm_gains,
    gain_moment,
):
    reps, owners = grid.reps, grid.shards
    rep = lax.axis_index("rep")
    shard = lax.axis_index("shard")
    core = rep % 2
    turn = (shard >> grid.core_bit) % 2
    logical_shard = shard + (core - turn) * (1 << grid.core_bit)

    low_square = square_master.astype(jnp.bfloat16)
    low_narrow = key_value_master.astype(jnp.bfloat16)
    pieces = []
    for j in range(PAIRS):
        pieces.append(low_square[0, :, 384 * j : 384 * j + 384])
        pieces.append(low_narrow[0, :, 128 * j : 128 * j + 128])
        pieces.append(low_narrow[1, :, 128 * j : 128 * j + 128])
    low_attn = jnp.concatenate(pieces + [low_square[1]], axis=1)
    units = wide_master.shape[2] // 3

    position = grid.swap_rows(positions)[0]
    rows = low_attn.shape[0]
    tile = units // reps
    chained = 1 if rows % 16 == 0 else 0
    gain_row = norm_gains.astype(jnp.bfloat16).reshape(1, 2 * rows)
    gain_row = jnp.pad(gain_row, ((0, 15), (0, 1024 - 2 * rows)))
    first = lax.dynamic_slice_in_dim(low_attn, core * 1024, 1024, axis=1)
    first = jnp.concatenate([first, gain_row], axis=0)
    second = lax.dynamic_slice_in_dim(low_attn, 2048 + core * 512, 512, axis=1)
    picks = [core * (reps // 2) + i for i in range(reps // 2)] if chained else []
    groups = [tuple(range(len(picks)))] if chained else []
    for k in range(chained, 3):
        groups.append((len(picks),))
        picks.append(reps * k + rep)
    cuts = list(pack_wide(wide_master, jnp.stack(picks).astype(jnp.int32), groups, tile))
    if chained:
        second = jnp.concatenate([second, cuts[0]], axis=1)
    mine, gathering = gather_pieces(grid, [first, second])
    other = [grid.move(mine[0], grid.flip_rep(0))]
    places = jnp.array(grid.places(), jnp.int32)[jnp.arange(owners) ^ shard]
    cores = core[None]
    gain_w = mine[0][:, rows, : 2 * rows].reshape(owners, 2, rows)
    gain_w = jnp.take(gain_w, places, axis=0).transpose(1, 0, 2).reshape(2, -1).astype(jnp.float32)
    natural = jnp.arange(reps, dtype=jnp.int32)
    whole = jnp.zeros((1,), jnp.int32)
    moved_tokens = grid.move(after(tokens, gathering[1]), grid.swapped)
    tokens = jnp.where(grid.stays(), tokens, moved_tokens)[0]
    moved_out = grid.move(after(cotangent, moved_tokens), grid.swapped)
    model = gain_w.shape[1]
    columns = 640 * PAIRS
    qkv_w = assemble(rows, mine[:1], other[:1], places, cores, 0, columns)

    count = tokens.shape[0]
    hidden_in = tokens.astype(jnp.float32)
    gain_attn, gain_mlp = gain_w[0], gain_w[1]
    cos, sin = rotary_tables(position, HEAD_SIZE)
    cos = jnp.concatenate([cos] * 4, axis=1)
    sin = jnp.concatenate([-sin, sin] * 2, axis=1)
    place = position[:, None]
    order = jnp.array(grid.masks(), jnp.int32) ^ logical_shard

    qkv, turned_in = project_qkv(order, tokens, gain_attn[None], qkv_w, cos, sin)
    wide_parts = [None] * chained
    for k in range(chained, 3):
        part = after(cuts[k], gathering[1])
        part = lax.all_gather(part, ("rep", "shard"), axis=0, tiled=True)
        wide_parts.append((natural, whole, [part.reshape(reps, owners * rows, 3 * tile)]))
    attended, logs = attend_forward(qkv, place)
    held, got = after((mine[1], gathering[-1]), attended)
    mine[1] = jnp.concatenate([held, got], axis=0)
    other.append(grid.move(mine[1], grid.flip_rep(0)))
    if chained:
        slots = (natural + core * (reps // 2)) % reps
        wide_parts[0] = (slots, places, [mine[1], other[1]])
        residual, normed_mid, turned_mid, out_w = project_out(
            places,
            cores,
            order,
            attended,
            tokens,
            gain_mlp[None],
            [mine[0], other[0], mine[1], other[1]],
        )
    else:
        out_w = assemble(rows, mine, other, places, cores, columns, 3072)
        residual = hidden_in + jnp.einsum(
            "tn,dn->td", attended, out_w, preferred_element_type=jnp.float32
        )
        normed_mid = normed(residual, gain_mlp).astype(jnp.bfloat16)
        turned_mid = turn_rows(normed_mid, order)
    d_out = jnp.where(grid.stays(), cotangent, after(moved_out, normed_mid))[0]
    turned_out = turn_rows(d_out, order)

    half = model // 2

    def weight_grad(turned, right):
        return Sums(
            grid,
            jnp.dot(turned[:half], right, preferred_element_type=jnp.float32).astype(jnp.bfloat16),
            jnp.dot(turned[half:], right, preferred_element_type=jnp.float32).astype(jnp.bfloat16),
        )

    wide_sums = []
    result, d_mid = residual, None
    for k in range(3):
        slots, where, weights = wide_parts[k]
        away, home, result, d_mid = mlp_part(
            reps,
            slots,
            where,
            normed_mid,
            d_out,
            turned_mid,
            turned_out,
            weights,
            result,
            d_mid,
            k == 2,
        )
        wide_sums.append(Sums(grid, away, home))
        for earlier in wide_sums[max(0, k - 2) : k]:
            d_mid, result = after((d_mid, result), earlier.step(away))
    result = grid.swap_rows(result[None])

    _, mid_back = jax.vjp(normed, residual, gain_mlp)
    d_residual, grad_gain_mlp = mid_back(d_mid)
    d_residual = d_residual + d_out.astype(jnp.float32)
    d_branch = d_residual.astype(jnp.bfloat16)
    d_attended = jnp.einsum(
        "td,dn->tn", d_branch, out_w, preferred_element_type=jnp.float32
    ).astype(jnp.bfloat16)
    out_sums = weight_grad(turn_rows(d_branch, order), attended)

    d_attended = after(d_attended, wide_sums[2].step(out_sums.away), wide_sums[0].got)
    d_stacks, pair_sums = [], []
    hold = len(grid.order) == 3
    for j in range(PAIRS):
        d_stack, away, home = attend_backward(
            qkv, d_attended, logs, place, cos, sin, turned_in, j
        )
        d_stacks.append(d_stack)
        pair_sums.append(Sums(grid, away, home))
        if j == 0:
            done = (wide_sums[1].step(d_stack), out_sums.step(d_stack), result)
        elif j == 1:
            done = (
                wide_sums[2].step(d_stack),
                out_sums.step(d_stack),
                pair_sums[0].step(d_stack),
                wide_sums[1].got,
            )
        else:
            done = (pair_sums[0].step(d_stack, hold), pair_sums[1].step(d_stack), out_sums.got)
        d_attended = after(d_attended, done, pair_sums[j].away)
        d_stacks = after(d_stacks, done, pair_sums[j].away)
    def back(j):
        return jnp.einsum(
            "tn,dn->td",
            d_stacks[j],
            qkv_w[:, 640 * j : 640 * j + 640],
            preferred_element_type=jnp.float32,
        )

    flag = grid.stays().astype(jnp.int32)[None]
    d_first = back(0) + back(1)
    d_stacks, wide_got = after(
        (d_stacks, wide_sums[2].got), pair_sums[2].step(d_first), pair_sums[1].step(d_first, hold)
    )
    wide_sums[2].got = wide_got
    spans = [(j, 0) for j in range(PAIRS)]
    late_sums = pair_sums
    if hold:
        pair_sums[0].join(pair_sums[1])
        spans = [(0, 0), (0, 640), (1, 0)]
        late_sums = [pair_sums[0], pair_sums[2]]
    mixed_wide, left_wide = mix_wide(
        flag, [part.result(d_first) for part in wide_sums], wide_error, wide_factor
    )
    mixed_out, left_out = mix_rest(
        flag,
        [out_sums.result(d_first)],
        [[(0, 0, model)]],
        [square_error[0, 1]],
        [square_factor[1]],
    )
    last_step = pair_sums[2].step(left_wide)
    d_stacks = after(d_stacks, last_step, left_out)
    d_normed_in = d_first + back(2)
    rep_moves = [grid.flip_rep(b) for b in range(reps.bit_length() - 1)]
    unit = 128 * reps
    left_early = butterfly(grid, jnp.concatenate([left_wide, left_out], axis=0), rep_moves)
    left_early = after(left_early, last_step)
    gram_early = 9 * units + model
    width = -(-(gram_early + 512) // unit) * unit
    early = contract_all(left_early, [mixed_wide, mixed_out], width)
    d_normed_in = after(d_normed_in, early)
    _, in_back = jax.vjp(normed, hidden_in, gain_attn)
    d_input, grad_gain_attn = in_back(d_normed_in)
    d_input = (d_input + d_residual).astype(jnp.bfloat16)
    early = sum_all(grid, early)
    late = d_input
    d_input = grid.swap_rows(d_input[None])
    narrow = 128 * PAIRS

    mixed_query, mixed_key, mixed_value, left_late = mix_rest(
        flag,
        [part.result(late) for part in late_sums],
        [
            [(which, at + first, at + last) for which, at in spans]
            for first, last in ((0, 384), (384, 512), (512, 640))
        ],
        [square_error[0, 0], key_value_error[0, 0], key_value_error[0, 1]],
        [square_factor[0], key_value_factor[0], key_value_factor[1]],
    )
    left_late = butterfly(grid, left_late, rep_moves)
    gram_late = columns
    gain_at = gram_late + 384
    width = -(-(gain_at + model) // unit) * unit
    gain_grad = jnp.stack([grad_gain_attn, grad_gain_mlp])
    mixed_late = [mixed_query, mixed_key, mixed_value]
    left_late = after(left_late, late)
    summed = contract_all(left_late, mixed_late, width, gain_grad)
    wide_new, wide_moment_new, wide_error_new, factor_wide = finish_wide(
        reps, early, gram_early, left_early, mixed_wide, wide_moment, wide_master
    )
    shard_moves = [grid.flip_shard(b) for b in range(owners.bit_length() - 1)]
    summed = butterfly(grid, summed, shard_moves[1:] + rep_moves[:1])
    summed = after(summed, wide_new)
    summed = butterfly(grid, summed, rep_moves[1:] + shard_moves[:1])
    (
        square_new,
        square_moment_new,
        square_error_new,
        factor_square,
        narrow_new,
        narrow_moment_new,
        narrow_error_new,
        factor_narrow,
    ) = finish_rest(
        reps,
        [summed, early],
        [left_late, left_early],
        [mixed_query, mixed_out, mixed_key, mixed_value],
        [
            (0, 0, gram_late, 0),
            (1, 9 * units, gram_early + 384, 24),
            (0, model, gram_late + 128, 8),
            (0, model + narrow, gram_late + 256, 16),
        ],
        [
            (square_moment, square_master, rate_square),
            (key_value_momentum, key_value_master, rate_narrow),
        ],
    )
    gain_total = lax.dynamic_slice_in_dim(
        summed[:2, gain_at : gain_at + model], shard * (model // owners), model // owners, axis=1
    )
    gain_moment_new = decay_rate * gain_moment + gain_total / reps
    gains_new = norm_gains - rate_gains * gain_moment_new
    return (
        result,
        d_input,
        wide_new,
        square_new,
        narrow_new,
        wide_moment_new,
        square_moment_new,
        narrow_moment_new,
        wide_error_new,
        square_error_new,
        narrow_error_new,
        factor_wide,
        factor_square,
        factor_narrow,
        gains_new,
        gain_moment_new,
    )


def solution(mesh):
    return jax.shard_map(
        functools.partial(shards, Grid(mesh)),
        mesh=mesh,
        in_specs=(
            P(("rep", "shard"), None, None),
            P(("rep", "shard"), None, None),
            P(("rep", "shard"), None),
            P(("rep", "shard"), None),
            P(None, "shard", None),
            P(None, "shard", None),
            P(None, "shard", None),
            P(None, "shard", None),
            P(None, "shard", None),
            P(None, "shard", None),
            P("rep", None, "shard", None),
            P("rep", None, "shard", None),
            P("rep", None, "shard", None),
            P(),
            P(),
            P(),
            P(None, "shard"),
            P(None, "shard"),
        ),
        out_specs=(
            P(("rep", "shard"), None, None),
            P(("rep", "shard"), None, None),
            P(None, "shard", None),
            P(None, "shard", None),
            P(None, "shard", None),
            P(None, "shard", None),
            P(None, "shard", None),
            P(None, "shard", None),
            P("rep", None, "shard", None),
            P("rep", None, "shard", None),
            P("rep", None, "shard", None),
            P(),
            P(),
            P(),
            P(None, "shard"),
            P(None, "shard"),
        ),
        check_vma=False,
    )
```

```python
import functools

import jax
import jax.numpy as jnp
from jax import lax
from jax.experimental import pallas as pl
from jax.experimental.pallas import tpu as pltpu
from jax.sharding import PartitionSpec as P

QUERY_HEADS = 18
KEY_VALUE_HEADS = 6
HEAD_SIZE = 64
PAIRS = KEY_VALUE_HEADS // 2


eps_norm = 1e-05
theta_base = 10000.0
decay_rate = 0.9
rate_wide = 0.03
rate_square = 0.1
rate_narrow = 0.02
rate_gains = 0.01
mask_fill = -1e30
highest = lax.Precision.HIGHEST


def normed(value_heads, gain):
    return (
        value_heads
        * lax.rsqrt(jnp.mean(value_heads * value_heads, axis=-1, keepdims=True) + eps_norm)
        * gain
    )


def rotary_tables(position, width):
    halfway = width // 2
    inverse = theta_base ** (-2.0 * jnp.arange(halfway, dtype=jnp.float32) / width)
    angles = position.astype(jnp.float32)[:, None] * inverse[None, :]
    return (jnp.cos(angles), jnp.sin(angles))


BLOCK_ROWS = 256
VMEM_BYTES = 56 * 1024 * 1024


def light(flops, bytes_accessed, transcendentals):
    return pl.CostEstimate(
        flops=flops // 8, bytes_accessed=bytes_accessed // 8, transcendentals=transcendentals // 8
    )


def partner_lanes(values):
    lane = lax.broadcasted_iota(jnp.int32, values.shape, 1)
    return jnp.where(
        lane % HEAD_SIZE < HEAD_SIZE // 2,
        pltpu.roll(values, 128 - HEAD_SIZE // 2, 1),
        pltpu.roll(values, HEAD_SIZE // 2, 1),
    )


def project_kernel(
    order_ref, x_ref, gain_ref, w_ref, cos_ref, sin_ref, out_ref, turned_ref, scratch_ref
):
    x = x_ref[...].astype(jnp.float32)
    scale = lax.rsqrt(jnp.mean(x * x, axis=-1, keepdims=True) + eps_norm)
    low = (x * scale * gain_ref[...]).astype(jnp.bfloat16)
    scratch_ref[...] = low.astype(jnp.float32).T
    share = scratch_ref.shape[0] // order_ref.shape[0]
    parts = [
        scratch_ref[pl.ds(pl.multiple_of(order_ref[p] * share, 8), share), :]
        for p in range(order_ref.shape[0])
    ]
    turned_ref[...] = jnp.concatenate(parts, axis=0).astype(jnp.bfloat16)
    cos, sin = cos_ref[...], sin_ref[...]
    for first in range(0, out_ref.shape[1], 640):
        got = jnp.dot(low, w_ref[:, first : first + 640], preferred_element_type=jnp.float32)
        for at in range(0, 640, 128):
            piece = got[:, at : at + 128]
            if at < 512:
                piece = piece * cos + partner_lanes(piece) * sin
            out_ref[:, first + at : first + at + 128] = piece.astype(jnp.bfloat16)


def project_qkv(order, x, gain, weights, cos, sin):
    rows, width = x.shape
    columns = weights.shape[1]
    block = min(BLOCK_ROWS, rows)
    return pl.pallas_call(
        project_kernel,
        grid_spec=pltpu.PrefetchScalarGridSpec(
            num_scalar_prefetch=1,
            grid=(rows // block,),
            in_specs=[
                pl.BlockSpec((block, width), lambda i, order: (i, 0)),
                pl.BlockSpec((1, width), lambda i, order: (0, 0)),
                pl.BlockSpec((width, columns), lambda i, order: (0, 0)),
                pl.BlockSpec((block, 128), lambda i, order: (i, 0)),
                pl.BlockSpec((block, 128), lambda i, order: (i, 0)),
            ],
            out_specs=[
                pl.BlockSpec((block, columns), lambda i, order: (i, 0)),
                pl.BlockSpec((width, block), lambda i, order: (0, i)),
            ],
            scratch_shapes=[pltpu.VMEM((width, block), jnp.float32)],
        ),
        out_shape=[
            jax.ShapeDtypeStruct((rows, columns), jnp.bfloat16),
            jax.ShapeDtypeStruct((width, rows), jnp.bfloat16),
        ],
        compiler_params=pltpu.CompilerParams(vmem_limit_bytes=VMEM_BYTES),
        cost_estimate=pl.CostEstimate(
            flops=2 * rows * width * columns,
            bytes_accessed=2 * (rows * width * 2 + rows * columns + width * columns),
            transcendentals=0,
        ),
    )(order, x, gain, weights, cos, sin)


def spread_heads(pair, spread_ref):
    wide = pair.astype(jnp.float32)
    turned = pltpu.roll(wide, HEAD_SIZE, 1)
    low_half = lax.broadcasted_iota(jnp.int32, wide.shape, 1) < HEAD_SIZE
    zero = jnp.zeros_like(wide)
    spread_ref[0] = jnp.where(low_half, wide, zero).astype(jnp.bfloat16)
    spread_ref[1] = jnp.where(low_half, zero, turned).astype(jnp.bfloat16)
    spread_ref[2] = jnp.where(low_half, turned, zero).astype(jnp.bfloat16)
    spread_ref[3] = jnp.where(low_half, zero, wide).astype(jnp.bfloat16)


def mask_bias(position, start, keys):
    rows = position.shape[0]
    row = lax.broadcasted_iota(jnp.int32, (rows, keys), 0) + start
    column = lax.broadcasted_iota(jnp.int32, (rows, keys), 1)
    allowed = (column <= row) & (column >= row - position)
    return jnp.where(allowed, 0.0, mask_fill)


def across(left, right):
    return lax.dot_general(
        left, right, (((1,), (1,)), ((), ())), preferred_element_type=jnp.float32
    )


def forward_kernel(qkv_ref, pos_ref, out_ref, log_ref, key_ref, value_ref):
    step = pl.program_id(1)
    block = out_ref.shape[0]

    @pl.when(step == 0)
    def _():
        spread_heads(qkv_ref[:, 384:512], key_ref)
        spread_heads(qkv_ref[:, 512:640], value_ref)

    for place in range(qkv_ref.shape[0] // block):

        @pl.when(step == place)
        def _(place=place):
            start = place * block
            keys = start + block
            bias = mask_bias(pos_ref[...], start, keys)
            lane = lax.broadcasted_iota(jnp.int32, (block, 128), 1)
            logs = jnp.zeros((block, 128), jnp.float32)
            for g in range(3):
                query = qkv_ref[start:keys, 128 * g : 128 * g + 128] * 0.125
                total = jnp.zeros((block, 128), jnp.float32)
                for e in range(2):
                    head = 2 * g + e
                    which = 2 * (head // 3) + e
                    scores = across(query, key_ref[which, :keys, :]) + bias
                    top = jnp.max(scores, axis=-1, keepdims=True)
                    raised = jnp.exp(scores - top)
                    row_total = jnp.sum(raised, axis=-1, keepdims=True)
                    low = (raised * (1.0 / row_total)).astype(jnp.bfloat16)
                    total += jnp.dot(
                        low, value_ref[which, :keys, :], preferred_element_type=jnp.float32
                    )
                    logs = jnp.where(lane == head, top + jnp.log(row_total), logs)
                out_ref[:, 128 * g : 128 * g + 128] = total.astype(jnp.bfloat16)
            log_ref[0] = logs


def attend_forward(qkv, position):
    rows = qkv.shape[0]
    pairs = qkv.shape[1] // 640
    block = min(BLOCK_ROWS, rows)
    return pl.pallas_call(
        forward_kernel,
        grid=(pairs, rows // block),
        in_specs=[
            pl.BlockSpec((rows, 640), lambda j, i: (0, j)),
            pl.BlockSpec((block, 1), lambda j, i: (i, 0)),
        ],
        out_specs=[
            pl.BlockSpec((block, 384), lambda j, i: (i, j)),
            pl.BlockSpec((1, block, 128), lambda j, i: (j, i, 0)),
        ],
        out_shape=[
            jax.ShapeDtypeStruct((rows, 384 * pairs), jnp.bfloat16),
            jax.ShapeDtypeStruct((pairs, rows, 128), jnp.float32),
        ],
        scratch_shapes=[
            pltpu.VMEM((4, rows, 128), jnp.bfloat16),
            pltpu.VMEM((4, rows, 128), jnp.bfloat16),
        ],
        compiler_params=pltpu.CompilerParams(vmem_limit_bytes=VMEM_BYTES),
        cost_estimate=pl.CostEstimate(
            flops=20 * pairs * rows * rows * 128,
            bytes_accessed=8 * rows * 640 * pairs,
            transcendentals=6 * pairs * rows * rows,
        ),
    )(qkv, position)


def backward_kernel(
    qkv_ref,
    d_ref,
    log_ref,
    pos_ref,
    cos_ref,
    sin_ref,
    turned_ref,
    out_ref,
    away_ref,
    home_ref,
    key_ref,
    value_ref,
    dk_ref,
    dv_ref,
):
    step = pl.program_id(0)
    block = d_ref.shape[0]
    blocks = qkv_ref.shape[0] // block

    @pl.when(step == 0)
    def _():
        spread_heads(qkv_ref[:, 384:512], key_ref)
        spread_heads(qkv_ref[:, 512:640], value_ref)
        dk_ref[...] = jnp.zeros_like(dk_ref)
        dv_ref[...] = jnp.zeros_like(dv_ref)

    for place in range(blocks):

        @pl.when(step == place)
        def _(place=place):
            start = place * block
            keys = start + block
            bias = mask_bias(pos_ref[...], start, keys)
            logs = log_ref[0]
            cos, sin = cos_ref[start:keys, :], sin_ref[start:keys, :]
            for g in range(3):
                query = qkv_ref[start:keys, 128 * g : 128 * g + 128] * 0.125
                d_out = d_ref[:, 128 * g : 128 * g + 128]
                query_turned = query.astype(jnp.float32).T.astype(jnp.bfloat16)
                d_turned = d_out.astype(jnp.float32).T.astype(jnp.bfloat16)
                total = jnp.zeros((block, 128), jnp.float32)
                for e in range(2):
                    head = 2 * g + e
                    which = 2 * (head // 3) + e
                    at = HEAD_SIZE * (head // 3)
                    key = key_ref[which, :keys, :]
                    scores = across(query, key) + bias
                    prob = jnp.exp(scores - logs[:, head : head + 1])
                    d_prob = across(d_out, value_ref[which, :keys, :])
                    delta = jnp.sum(prob * d_prob, axis=-1, keepdims=True)
                    d_scores = (prob * (d_prob - delta)).astype(jnp.bfloat16)
                    half = slice(HEAD_SIZE * e, HEAD_SIZE * e + HEAD_SIZE)
                    dv_ref[at : at + HEAD_SIZE, :keys] += jnp.dot(
                        d_turned[half], prob.astype(jnp.bfloat16), preferred_element_type=jnp.float32
                    )
                    dk_ref[at : at + HEAD_SIZE, :keys] += jnp.dot(
                        query_turned[half], d_scores, preferred_element_type=jnp.float32
                    )
                    total += jnp.dot(d_scores, key, preferred_element_type=jnp.float32)
                total = total * 0.125
                total = total * cos - partner_lanes(total) * sin
                out_ref[start:keys, 128 * g : 128 * g + 128] = total.astype(jnp.bfloat16)

    @pl.when(step == blocks - 1)
    def _():
        d_key = dk_ref[...].T
        d_key = d_key * cos_ref[...] - partner_lanes(d_key) * sin_ref[...]
        out_ref[:, 384:512] = d_key.astype(jnp.bfloat16)
        out_ref[:, 512:640] = dv_ref[...].T.astype(jnp.bfloat16)
        half = away_ref.shape[0]
        for first, grad_ref in ((0, away_ref), (half, home_ref)):
            grad_ref[...] = jnp.dot(
                turned_ref[first : first + half, :],
                out_ref[...],
                preferred_element_type=jnp.float32,
            ).astype(jnp.bfloat16)


def attend_backward(qkv, d_attended, logs, position, cos, sin, turned, pair):
    rows = qkv.shape[0]
    model = turned.shape[0]
    block = min(BLOCK_ROWS, rows)
    half = pl.BlockSpec((model // 2, 640), lambda i: (0, 0))
    return pl.pallas_call(
        backward_kernel,
        grid=(rows // block,),
        in_specs=[
            pl.BlockSpec((rows, 640), lambda i: (0, pair)),
            pl.BlockSpec((block, 384), lambda i: (i, pair)),
            pl.BlockSpec((1, block, 128), lambda i: (pair, i, 0)),
            pl.BlockSpec((block, 1), lambda i: (i, 0)),
            pl.BlockSpec((rows, 128), lambda i: (0, 0)),
            pl.BlockSpec((rows, 128), lambda i: (0, 0)),
            pl.BlockSpec((model, rows), lambda i: (0, 0), pipeline_mode=pl.Buffered(1)),
        ],
        out_specs=[pl.BlockSpec((rows, 640), lambda i: (0, 0)), half, half],
        out_shape=[
            jax.ShapeDtypeStruct((rows, 640), jnp.bfloat16),
            jax.ShapeDtypeStruct((model // 2, 640), jnp.bfloat16),
            jax.ShapeDtypeStruct((model // 2, 640), jnp.bfloat16),
        ],
        scratch_shapes=[
            pltpu.VMEM((4, rows, 128), jnp.bfloat16),
            pltpu.VMEM((4, rows, 128), jnp.bfloat16),
            pltpu.VMEM((128, rows), jnp.float32),
            pltpu.VMEM((128, rows), jnp.float32),
        ],
        compiler_params=pltpu.CompilerParams(vmem_limit_bytes=VMEM_BYTES),
        cost_estimate=pl.CostEstimate(
            flops=50 * rows * rows * 128,
            bytes_accessed=8 * rows * 640,
            transcendentals=6 * rows * rows,
        ),
    )(qkv, d_attended, logs, position, cos, sin, turned)


def turn_kernel(order_ref, rows_ref, out_ref, turned_ref):
    turned_ref[...] = rows_ref[...].astype(jnp.float32).T
    owners = order_ref.shape[0]
    share = turned_ref.shape[0] // owners
    parts = [
        turned_ref[pl.ds(pl.multiple_of(order_ref[p] * share, 8), share), :] for p in range(owners)
    ]
    out_ref[...] = jnp.concatenate(parts, axis=0).astype(jnp.bfloat16)


def turn_rows(rows, order):
    count, model = rows.shape
    block = min(BLOCK_ROWS, count)
    return pl.pallas_call(
        turn_kernel,
        grid_spec=pltpu.PrefetchScalarGridSpec(
            num_scalar_prefetch=1,
            grid=(count // block,),
            in_specs=[pl.BlockSpec((block, model), lambda i, order: (i, 0))],
            out_specs=pl.BlockSpec((model, block), lambda i, order: (0, i)),
            scratch_shapes=[pltpu.VMEM((model, block), jnp.float32)],
        ),
        out_shape=jax.ShapeDtypeStruct((model, count), jnp.bfloat16),
        compiler_params=pltpu.CompilerParams(vmem_limit_bytes=VMEM_BYTES),
        cost_estimate=pl.CostEstimate(
            flops=0, bytes_accessed=4 * count * model, transcendentals=0
        ),
    )(order, rows)


def mlp_kernel(reps, first, last, slot_ref, place_ref, mid_ref, d_ref, *refs):
    del slot_ref
    mid_hbm, d_hbm = refs[:2]
    befores = refs[2 : 3 if first else 4]
    refs = refs[2 + len(befores) :]
    weight_hbm, refs = (refs[:1], refs[1:]) if place_ref.shape[0] == 1 else (refs[:2], refs[2:])
    away_ref, home_ref, result_ref, back_ref = refs[:4]
    weight_ref, mid_turned_ref, d_turned_ref, d_pair_ref, hidden_ref, weight_sem, sem = refs[4:11]
    output_ref = result_ref
    if last:
        result_ref = refs[11]
    step = pl.program_id(0)
    count = mid_ref.shape[0]
    part = min(512, count)
    tile = hidden_ref.shape[1]
    half = away_ref.shape[1]

    wide = 3 * tile
    skip = weight_hbm[0].shape[2] - wide * (reps // 2)

    def load(i):
        if len(weight_hbm) == 1:
            pltpu.make_async_copy(
                weight_hbm[0].at[i], weight_ref.at[i], weight_sem.at[i]
            ).start()
            return
        ref, at = weight_hbm[2 * i // reps], i % (reps // 2)
        owners, share = ref.shape[:2]
        for a in range(owners):
            pltpu.make_async_copy(
                ref.at[place_ref[a], :, skip + wide * at : skip + wide * at + wide],
                weight_ref.at[i, share * a : share * a + share, :],
                weight_sem.at[i],
            ).start()

    sums = [pltpu.make_async_copy(befores[0], result_ref, sem.at[0])]
    if not first:
        sums.append(pltpu.make_async_copy(befores[1], back_ref, sem.at[1]))
    turned = [
        pltpu.make_async_copy(mid_hbm, mid_turned_ref, sem.at[2]),
        pltpu.make_async_copy(d_hbm, d_turned_ref, sem.at[3]),
    ]

    @pl.when(step == 0)
    def _():
        load(0)
        for copy in sums + turned:
            copy.start()
        for i in range(1, reps):
            load(i)
        if first:
            back_ref[...] = jnp.zeros_like(back_ref)

    for i in range(reps):

        @pl.when(step == i)
        def _(i=i):
            pltpu.make_async_copy(weight_ref.at[i], weight_ref.at[i], weight_sem.at[i]).wait()

    @pl.when(step == 0)
    def _():
        for copy in sums:
            copy.wait()

    @pl.loop(0, count // part)
    def _(t):
        rows = pl.ds(pl.multiple_of(t * part, part), part)
        pair_w = weight_ref[step, :, : 2 * tile]
        down_w = weight_ref[step, :, 2 * tile :]
        pair = jnp.dot(mid_ref[rows, :], pair_w, preferred_element_type=jnp.float32)
        d_hidden = jnp.dot(d_ref[rows, :], down_w, preferred_element_type=jnp.float32)
        gate, up = pair[:, :tile], pair[:, tile:]
        sig = jax.nn.sigmoid(gate)
        silu = gate * sig
        hidden = (silu * up).astype(jnp.bfloat16)
        hidden_ref[rows, :] = hidden
        d_gate = d_hidden * up * (sig * (1.0 + gate * (1.0 - sig)))
        d_pair_ref[rows, :tile] = d_gate.astype(jnp.bfloat16)
        d_pair_ref[rows, tile:] = (d_hidden * silu).astype(jnp.bfloat16)
        back_ref[rows, :] += across(d_pair_ref[rows, :], pair_w)
        result_ref[rows, :] += across(hidden, down_w)
        if last:

            @pl.when(step == reps - 1)
            def _():
                output_ref[rows, :] = result_ref[rows, :].astype(jnp.bfloat16)

    @pl.when(step == 0)
    def _():
        for copy in turned:
            copy.wait()

    for at, out_ref in ((0, away_ref), (half, home_ref)):
        pair = jnp.dot(
            mid_turned_ref[at : at + half, :], d_pair_ref[...], preferred_element_type=jnp.float32
        )
        out_ref[0] = pair[:, :tile].astype(jnp.bfloat16)
        out_ref[1] = pair[:, tile:].astype(jnp.bfloat16)
        out_ref[2] = jnp.dot(
            d_turned_ref[at : at + half, :], hidden_ref[...], preferred_element_type=jnp.float32
        ).astype(jnp.bfloat16)


def mlp_part(reps, slots, places, mid, d_out, mid_turned, d_turned, weights, result, back, last):
    count, model = mid.shape
    tile = (weights[0].shape[2] - (512 if len(weights) == 2 else 0)) // 3
    if len(weights) == 2:
        tile //= reps // 2
    units = tile * reps
    half = model // 2
    first = back is None
    befores = [result] if first else [result, back]

    def once(shape):
        return pl.BlockSpec(shape, lambda i, slots, places: (0, 0), pipeline_mode=pl.Buffered(1))

    anywhere = pl.BlockSpec(memory_space=pl.ANY)
    return pl.pallas_call(
        functools.partial(mlp_kernel, reps, first, last),
        grid_spec=pltpu.PrefetchScalarGridSpec(
            num_scalar_prefetch=2,
            grid=(reps,),
            in_specs=[once((count, model))] * 2 + [anywhere] * (2 + len(befores) + len(weights)),
            out_specs=[
                pl.BlockSpec((3, half, tile), lambda i, slots, places: (0, 0, slots[i])),
                pl.BlockSpec((3, half, tile), lambda i, slots, places: (0, 0, slots[i])),
                once((count, model)),
                once((count, model)),
            ],
            scratch_shapes=[
                pltpu.VMEM((reps, model, 3 * tile), jnp.bfloat16),
                pltpu.VMEM((model, count), jnp.bfloat16),
                pltpu.VMEM((model, count), jnp.bfloat16),
                pltpu.VMEM((count, 2 * tile), jnp.bfloat16),
                pltpu.VMEM((count, tile), jnp.bfloat16),
                pltpu.SemaphoreType.DMA((reps,)),
                pltpu.SemaphoreType.DMA((4,)),
            ]
            + ([pltpu.VMEM((count, model), jnp.float32)] if last else []),
        ),
        out_shape=[
            jax.ShapeDtypeStruct((3, half, units), jnp.bfloat16),
            jax.ShapeDtypeStruct((3, half, units), jnp.bfloat16),
            jax.ShapeDtypeStruct((count, model), jnp.bfloat16 if last else jnp.float32),
            jax.ShapeDtypeStruct((count, model), jnp.float32),
        ],
        compiler_params=pltpu.CompilerParams(vmem_limit_bytes=VMEM_BYTES),
        cost_estimate=pl.CostEstimate(
            flops=18 * count * model * units,
            bytes_accessed=2 * (4 * count * model + 6 * model * units) + 16 * count * model,
            transcendentals=count * units,
        ),
    )(slots, places, mid, d_out, mid_turned, d_turned, *befores, *weights)


def assemble(rows, mine, other, places, core, low, high):
    owners = mine[0].shape[0]
    widths = [m.shape[2] for m in mine]
    count = len(mine)

    def kernel(place_ref, core_ref, *refs):
        del place_ref
        out_ref = refs[-1]
        for own in range(2):

            @pl.when(core_ref[0] == own)
            def _(own=own):
                at = 0
                for i in range(count):
                    for half in range(2):
                        ref = refs[i] if half == own else refs[count + i]
                        first, last = max(low, at), min(high, at + widths[i])
                        if first < last:
                            out_ref[0, :, first - low : last - low] = ref[
                                0, :, first - at : last - at
                            ]
                        at += widths[i]

    def spec(width):
        return pl.BlockSpec((1, rows, width), lambda a, place, core: (place[a], 0, 0))

    out = pl.pallas_call(
        kernel,
        grid_spec=pltpu.PrefetchScalarGridSpec(
            num_scalar_prefetch=2,
            grid=(owners,),
            in_specs=[spec(w) for w in widths] * 2,
            out_specs=pl.BlockSpec((1, rows, high - low), lambda a, place, core: (a, 0, 0)),
        ),
        out_shape=jax.ShapeDtypeStruct((owners, rows, high - low), jnp.bfloat16),
        compiler_params=pltpu.CompilerParams(vmem_limit_bytes=VMEM_BYTES),
        cost_estimate=pl.CostEstimate(
            flops=0, bytes_accessed=8 * owners * rows * sum(widths), transcendentals=0
        ),
    )(places, core, *mine, *other)
    return out.reshape(owners * rows, high - low)


def left_rows(factor, rows):
    lane = lax.broadcasted_iota(jnp.int32, (rows.shape[0], 128), 1)
    columns = jnp.zeros((rows.shape[0], 128), jnp.float32)
    for r in range(8):
        column = jnp.sum(rows * factor[r : r + 1, :], axis=1, keepdims=True)
        columns = jnp.where(lane == r, column, columns)
    return columns.T[:8, :]


def exact_dot(left, right, contract):
    return lax.dot_general(
        left, right, (contract, ((), ())), precision=highest, preferred_element_type=jnp.float32
    )


def mix_kernel(layout, count, flag_ref, *refs):
    sums, refs = refs[: 3 * count], refs[3 * count :]
    errors, refs = refs[: len(layout)], refs[len(layout) :]
    factors, refs = refs[: len(layout)], refs[len(layout) :]
    mixed, left_ref = refs[: len(layout)], refs[len(layout)]
    stays = flag_ref[0] == 1
    for m, pieces in enumerate(layout):
        at = 0
        for which, first, last in pieces:
            away, home, moved = (
                sums[3 * which + k][..., first:last].astype(jnp.float32) for k in range(3)
            )
            width = last - first
            where = (..., slice(at, at + width))
            total = away + jnp.where(stays, home, moved)
            total = total.reshape(total.shape[-2:])
            error = errors[m][where]
            error = error.reshape(error.shape[-2:])
            mixed[m][where] = (total + error).reshape(mixed[m].shape[:-1] + (width,))
            at += width
        rows = mixed[m][...].reshape(mixed[m].shape[-2:])
        factor = factors[m][...].reshape(factors[m].shape[-2:])
        left_ref[8 * m : 8 * m + 8, :] = left_rows(factor, rows)


def mix_wide(flag, parts, error, factor):
    count, rows, third = parts[0][0].shape
    columns = third * len(parts)
    arrays = [a for part in parts for a in part]
    layout = [[(i, 0, third) for i in range(len(parts))]]
    return pl.pallas_call(
        functools.partial(mix_kernel, layout, len(parts)),
        grid_spec=pltpu.PrefetchScalarGridSpec(
            num_scalar_prefetch=1,
            grid=(count,),
            in_specs=[pl.BlockSpec((1, rows, third), lambda i, flag: (i, 0, 0))] * len(arrays)
            + [
                pl.BlockSpec((1, 1, rows, columns), lambda i, flag: (0, i, 0, 0)),
                pl.BlockSpec((1, 8, columns), lambda i, flag: (i, 0, 0)),
            ],
            out_specs=[
                pl.BlockSpec((1, rows, columns), lambda i, flag: (i, 0, 0)),
                pl.BlockSpec((8, rows), lambda i, flag: (i, 0)),
            ],
        ),
        out_shape=[
            jax.ShapeDtypeStruct((count, rows, columns), jnp.float32),
            jax.ShapeDtypeStruct((8 * count, rows), jnp.float32),
        ],
        compiler_params=pltpu.CompilerParams(vmem_limit_bytes=VMEM_BYTES),
        cost_estimate=pl.CostEstimate(
            flops=96 * count * rows * columns,
            bytes_accessed=14 * count * rows * columns,
            transcendentals=0,
        ),
    )(flag, *arrays, error, factor)


def in_vmem(count):
    return [pl.BlockSpec(memory_space=pltpu.VMEM)] * count


def mix_rest(flag, parts, layout, errors, factors):
    rows = errors[0].shape[0]
    arrays = [a for part in parts for a in part]
    return pl.pallas_call(
        functools.partial(mix_kernel, layout, len(parts)),
        in_specs=[pl.BlockSpec(memory_space=pltpu.SMEM)]
        + in_vmem(len(arrays) + len(errors) + len(factors)),
        out_specs=in_vmem(len(errors) + 1),
        out_shape=[jax.ShapeDtypeStruct(e.shape, jnp.float32) for e in errors]
        + [jax.ShapeDtypeStruct((8 * len(errors), rows), jnp.float32)],
        compiler_params=pltpu.CompilerParams(vmem_limit_bytes=VMEM_BYTES),
        cost_estimate=pl.CostEstimate(
            flops=96 * sum(e.size for e in errors),
            bytes_accessed=14 * sum(e.size for e in errors),
            transcendentals=0,
        ),
    )(flag, *arrays, *errors, *factors)


def contract_all(left, mixed, width, extra=None):
    def kernel(*refs):
        left_ref, out_ref = refs[0], refs[-1]
        out_ref[...] = jnp.zeros_like(out_ref)
        at, m = 0, 0
        for ref in refs[1 : 1 + len(mixed)]:
            for k in range(ref.shape[0] if len(ref.shape) == 3 else 1):
                rows = ref[k] if len(ref.shape) == 3 else ref[...]
                own = left_ref[8 * m : 8 * m + 8, :]
                out_ref[:, at : at + rows.shape[1]] = exact_dot(own, rows, ((1,), (0,)))
                at += rows.shape[1]
                m += 1
        for k in range(m):
            own = left_ref[8 * k : 8 * k + 8, :]
            out_ref[:, at : at + 8] = exact_dot(own, own, ((1,), (1,)))
            at += 128
        if extra is not None:
            out_ref[: extra.shape[0], at : at + extra.shape[1]] = refs[-2][...]

    more = [] if extra is None else [extra]
    return pl.pallas_call(
        kernel,
        in_specs=in_vmem(1 + len(mixed) + len(more)),
        out_specs=pl.BlockSpec(memory_space=pltpu.VMEM),
        out_shape=jax.ShapeDtypeStruct((8, width), jnp.float32),
        compiler_params=pltpu.CompilerParams(vmem_limit_bytes=VMEM_BYTES),
        cost_estimate=pl.CostEstimate(
            flops=96 * sum(m.size for m in mixed),
            bytes_accessed=4 * sum(m.size for m in mixed),
            transcendentals=0,
        ),
    )(left, *mixed, *more)


def eliminate(gram, rights):
    row = lax.broadcasted_iota(jnp.int32, (8, 1), 0)
    for j in range(8):
        scale = 1.0 / jnp.sqrt(gram[j : j + 1, j : j + 1])
        below = jnp.where(row > j, gram[:, j : j + 1] * scale, 0.0)
        done = []
        for right in [gram] + list(rights):
            top = right[j : j + 1, :] * scale
            done.append(jnp.where(row == j, top, right - below * top))
        gram, rights = done[0], done[1:]
    return rights


def finish_matrix(reps, rate, row, gram, left, mixed, moment, master, outs):
    new_ref, moment_new_ref, error_ref, factor_ref = outs
    factor, basis = eliminate(gram[:, :8] * (1.0 / reps), [row, left])
    factor = factor * (1.0 / reps)
    factor_ref[...] = factor
    turned = basis.T
    columns = factor.shape[1]
    for first in range(0, columns, 256):
        span = slice(first, min(first + 256, columns))
        approx = turned[:, 0:1] * factor[0:1, span]
        for r in range(1, 8):
            approx += turned[:, r : r + 1] * factor[r : r + 1, span]
        moment_new = decay_rate * moment[:, span] + approx
        moment_new_ref[:, span] = moment_new
        new_ref[:, span] = master[:, span] - rate * moment_new
        error_ref[:, span] = mixed[:, span] - approx


def finish_wide(reps, packed, gram_at, left, mixed, moment, master):
    count, rows, columns = mixed.shape

    def kernel(row_ref, gram_ref, left_ref, mixed_ref, moment_ref, master_ref, *outs):
        new_ref, moment_new_ref, error_ref, factor_ref = outs
        finish_matrix(
            reps,
            rate_wide,
            row_ref[...],
            gram_ref[...],
            left_ref[...],
            mixed_ref.at[0],
            moment_ref.at[0],
            master_ref.at[0],
            (new_ref.at[0], moment_new_ref.at[0], error_ref.at[0, 0], factor_ref.at[0]),
        )

    whole = pl.BlockSpec((1, rows, columns), lambda i: (i, 0, 0))
    shape = jax.ShapeDtypeStruct((count, rows, columns), jnp.float32)
    return pl.pallas_call(
        kernel,
        grid=(count,),
        in_specs=[
            pl.BlockSpec((8, columns), lambda i: (0, i)),
            pl.BlockSpec((8, 128), lambda i: (0, gram_at // 128 + i)),
            pl.BlockSpec((8, rows), lambda i: (i, 0)),
            whole,
            whole,
            whole,
        ],
        out_specs=[
            whole,
            whole,
            pl.BlockSpec((1, 1, rows, columns), lambda i: (0, i, 0, 0)),
            pl.BlockSpec((1, 8, columns), lambda i: (i, 0, 0)),
        ],
        out_shape=[
            shape,
            shape,
            jax.ShapeDtypeStruct((1, count, rows, columns), jnp.float32),
            jax.ShapeDtypeStruct((count, 8, columns), jnp.float32),
        ],
        compiler_params=pltpu.CompilerParams(vmem_limit_bytes=VMEM_BYTES),
        cost_estimate=light(
            flops=96 * count * rows * columns,
            bytes_accessed=24 * count * rows * columns,
            transcendentals=0,
        ),
    )(packed, packed, left, mixed, moment, master)


def finish_rest(reps, packs, lefts, mixed, where, states):
    groups = []
    at = 0
    for moment, _, rate in states:
        groups.append((at, moment.shape[0], rate))
        at += moment.shape[0]

    def kernel(*refs):
        pack_refs, refs = refs[: len(packs)], refs[len(packs) :]
        left_refs, refs = refs[: len(lefts)], refs[len(lefts) :]
        mixed_refs, refs = refs[: len(mixed)], refs[len(mixed) :]
        state_refs, outs = refs[: 2 * len(states)], refs[2 * len(states) :]
        for g, (first, count, rate) in enumerate(groups):
            new_ref, moment_new_ref, error_ref, factor_ref = outs[4 * g : 4 * g + 4]
            for k in range(count):
                pack, row_at, gram_at, left_at = where[first + k]
                rows = mixed_refs[first + k]
                finish_matrix(
                    reps,
                    rate,
                    pack_refs[pack][:, row_at : row_at + rows.shape[1]],
                    pack_refs[pack][:, gram_at : gram_at + 128],
                    left_refs[pack][left_at : left_at + 8, :],
                    rows,
                    state_refs[2 * g].at[k],
                    state_refs[2 * g + 1].at[k],
                    (new_ref.at[k], moment_new_ref.at[k], error_ref.at[0, k], factor_ref.at[k]),
                )

    shapes = []
    for moment, _, _ in states:
        count, rows, columns = moment.shape
        shapes += [
            jax.ShapeDtypeStruct(moment.shape, jnp.float32),
            jax.ShapeDtypeStruct(moment.shape, jnp.float32),
            jax.ShapeDtypeStruct((1,) + moment.shape, jnp.float32),
            jax.ShapeDtypeStruct((count, 8, columns), jnp.float32),
        ]
    arrays = [a for state in states for a in state[:2]]
    return pl.pallas_call(
        kernel,
        in_specs=in_vmem(len(packs) + len(lefts) + len(mixed) + len(arrays)),
        out_specs=in_vmem(len(shapes)),
        out_shape=shapes,
        compiler_params=pltpu.CompilerParams(vmem_limit_bytes=VMEM_BYTES),
        cost_estimate=light(
            flops=96 * sum(m.size for m in mixed),
            bytes_accessed=24 * sum(m.size for m in mixed),
            transcendentals=0,
        ),
    )(*packs, *lefts, *mixed, *arrays)


def pack_wide(master, picks, groups, tile):
    count, rows, _ = master.shape
    number = picks.shape[0]

    def kernel(pick_ref, *refs):
        del pick_ref
        for group, out_ref in zip(groups, refs[number:]):
            at = 0
            for pick in group:
                for i in range(count):
                    out_ref[:, at : at + tile] = refs[pick][i].astype(jnp.bfloat16)
                    at += tile

    def spec(n):
        return pl.BlockSpec((count, rows, tile), lambda i, picks: (0, 0, picks[n]))

    shapes = [
        jax.ShapeDtypeStruct((rows, count * tile * len(group)), jnp.bfloat16) for group in groups
    ]
    return pl.pallas_call(
        kernel,
        grid_spec=pltpu.PrefetchScalarGridSpec(
            num_scalar_prefetch=1,
            grid=(1,),
            in_specs=[spec(n) for n in range(number)],
            out_specs=[pl.BlockSpec(s.shape, lambda i, picks: (0, 0)) for s in shapes],
        ),
        out_shape=shapes,
        compiler_params=pltpu.CompilerParams(vmem_limit_bytes=VMEM_BYTES),
        cost_estimate=pl.CostEstimate(
            flops=0, bytes_accessed=6 * number * count * rows * tile, transcendentals=0
        ),
    )(picks, *[master] * number)


def split_sum(home, got):
    shape = home.shape
    rows, columns = shape[-2:]
    lead = home.size // (rows * columns)
    half = rows // 2

    def kernel(home_ref, got_ref, away_ref, kept_ref):
        total = home_ref[0].astype(jnp.float32) + got_ref[0].astype(jnp.float32)
        away_ref[0] = total[:half].astype(jnp.bfloat16)
        kept_ref[0] = total[half:].astype(jnp.bfloat16)

    whole = pl.BlockSpec((1, rows, columns), lambda i: (i, 0, 0))
    part = pl.BlockSpec((1, half, columns), lambda i: (i, 0, 0))
    out = jax.ShapeDtypeStruct((lead, half, columns), jnp.bfloat16)
    away, kept = pl.pallas_call(
        kernel,
        grid=(lead,),
        in_specs=[whole, whole],
        out_specs=[part, part],
        out_shape=[out, out],
        compiler_params=pltpu.CompilerParams(vmem_limit_bytes=VMEM_BYTES),
        cost_estimate=pl.CostEstimate(
            flops=home.size, bytes_accessed=6 * home.size, transcendentals=0
        ),
    )(home.reshape(lead, rows, columns), got.reshape(lead, rows, columns))
    tail = (half, columns)
    return away.reshape(shape[:-2] + tail), kept.reshape(shape[:-2] + tail)


def out_kernel(owners, place_ref, core_ref, order_ref, att_ref, x_ref, gain_ref, *refs):
    halves, refs = refs[:4], refs[4:]
    residual_ref, mid_ref, mid_turned_ref, w_ref, turned_ref, sem = refs
    share = w_ref.shape[0] // owners

    @pl.when(pl.program_id(0) == 0)
    def _():
        for own in range(2):

            @pl.when(core_ref[0] == own)
            def _(own=own):
                spans = (
                    (halves[0 if own == 1 else 1], 896, 0, 128),
                    (halves[2 if own == 0 else 3], 0, 128, 512),
                    (halves[2 if own == 1 else 3], 0, 640, 512),
                )
                for ref, first, at, width in spans:
                    for a in range(owners):
                        pltpu.make_async_copy(
                            ref.at[place_ref[a], :share, first : first + width],
                            w_ref.at[share * a : share * a + share, at : at + width],
                            sem.at[0],
                        ).start()

        pltpu.make_async_copy(w_ref, w_ref, sem.at[0]).wait()

    residual = x_ref[...].astype(jnp.float32) + across(att_ref[...], w_ref[...])
    residual_ref[...] = residual
    scale = lax.rsqrt(jnp.mean(residual * residual, axis=-1, keepdims=True) + eps_norm)
    mid = (residual * scale * gain_ref[...]).astype(jnp.bfloat16)
    mid_ref[...] = mid
    turned_ref[...] = mid.astype(jnp.float32).T
    parts = [
        turned_ref[pl.ds(pl.multiple_of(order_ref[p] * share, 8), share), :] for p in range(owners)
    ]
    mid_turned_ref[...] = jnp.concatenate(parts, axis=0).astype(jnp.bfloat16)


def project_out(places, core, order, attended, x, gain, halves):
    count, model = x.shape
    owners = order.shape[0]
    block = min(BLOCK_ROWS, count)
    rows = pl.BlockSpec((block, model), lambda i, *_: (i, 0))
    return pl.pallas_call(
        functools.partial(out_kernel, owners),
        grid_spec=pltpu.PrefetchScalarGridSpec(
            num_scalar_prefetch=3,
            grid=(count // block,),
            in_specs=[rows, rows, pl.BlockSpec((1, model), lambda i, *_: (0, 0))]
            + [pl.BlockSpec(memory_space=pl.ANY)] * 4,
            out_specs=[
                rows,
                rows,
                pl.BlockSpec((model, block), lambda i, *_: (0, i)),
                pl.BlockSpec((model, model), lambda i, *_: (0, 0)),
            ],
            scratch_shapes=[
                pltpu.VMEM((model, block), jnp.float32),
                pltpu.SemaphoreType.DMA((1,)),
            ],
        ),
        out_shape=[
            jax.ShapeDtypeStruct((count, model), jnp.float32),
            jax.ShapeDtypeStruct((count, model), jnp.bfloat16),
            jax.ShapeDtypeStruct((model, count), jnp.bfloat16),
            jax.ShapeDtypeStruct((model, model), jnp.bfloat16),
        ],
        compiler_params=pltpu.CompilerParams(vmem_limit_bytes=VMEM_BYTES),
        cost_estimate=pl.CostEstimate(
            flops=2 * count * model * model,
            bytes_accessed=12 * count * model + 4 * model * model,
            transcendentals=count,
        ),
    )(places, core, order, attended, x, gain, *halves)


class Grid:
    def __init__(self, mesh):
        self.reps = mesh.shape["rep"]
        self.shards = mesh.shape["shard"]
        self.core_bit = self.shards.bit_length() - 3
        stages = self.shards.bit_length() - 1
        self.order = [self.core_bit] + [b for b in range(stages) if b != self.core_bit]

    def swapped(self, rep, shard):
        bit = self.core_bit
        core = rep & 1
        turn = (shard >> bit) & 1
        return (rep - core + turn, shard - (turn << bit) + (core << bit))

    def flat(self, pair):
        return pair[0] * self.shards + pair[1]

    def every(self):
        return [(r, s) for r in range(self.reps) for s in range(self.shards)]

    def move(self, value, target):
        pairs = [(self.flat(p), self.flat(target(*p))) for p in self.every() if target(*p) != p]
        return lax.ppermute(value, ("rep", "shard"), pairs)

    def stays(self):
        return lax.axis_index("rep") % 2 == (lax.axis_index("shard") >> self.core_bit) % 2

    def swap_rows(self, value):
        return jnp.where(self.stays(), value, self.move(value, self.swapped))

    def partner(self, bit):
        def target(rep, shard):
            lr, ls = self.swapped(rep, shard)
            return self.swapped(lr, ls ^ (1 << bit))

        return target

    def last(self, bit):
        def target(rep, shard):
            lr, ls = self.swapped(rep, shard)
            return (lr, ls ^ (1 << bit))

        return target

    def flip_rep(self, bit):
        return lambda rep, shard: (rep ^ (1 << bit), shard)

    def flip_shard(self, bit):
        return lambda rep, shard: (rep, shard ^ (1 << bit))

    def doubling(self):
        return list(range(len(self.order)))[::-1]

    def places(self):
        out = [0] * self.shards
        for place in range(self.shards):
            distance = 0
            for k, bit in enumerate(self.doubling()):
                if (place >> k) & 1:
                    distance |= 1 << bit
            out[distance] = place
        return out

    def masks(self):
        count = len(self.order)
        out = []
        for place in range(self.shards):
            mask = 0
            for k, bit in enumerate(self.order):
                if not (place >> (count - 1 - k)) & 1:
                    mask |= 1 << bit
            out.append(mask)
        return out


def after(value, *others):
    return lax.optimization_barrier((value, others))[0]


def gather_pieces(grid, blocks):
    mine = []
    before = [None] * len(grid.order)
    for number, block in enumerate(blocks):
        held = block[None]
        for k, bit in enumerate(grid.doubling()):
            last = k == len(before) - 1
            if before[k] is not None:
                held = after(held, before[k])
            before[k] = grid.move(held, grid.flip_shard(bit))
            if not (last and number == len(blocks) - 1):
                held = jnp.concatenate([held, before[k]], axis=0)
        mine.append(held)
    return mine, before


class Sums:
    def __init__(self, grid, away, home):
        self.grid = grid
        self.stage = 0
        self.away, self.home = away, home
        self.send()

    def send(self):
        grid, bit = self.grid, self.grid.order[self.stage]
        if self.stage == len(grid.order) - 1:
            self.got = (grid.move(self.away, grid.last(bit)), grid.move(self.home, grid.swapped))
        else:
            self.got = grid.move(self.away, grid.partner(bit))

    def step(self, late, hold=False):
        self.got = after(self.got, late)
        self.away, self.home = split_sum(self.home, self.got)
        self.stage += 1
        if not hold:
            self.send()
        return (self.away, self.home)

    def join(self, other):
        self.away = jnp.concatenate([self.away, other.away], axis=-1)
        self.home = jnp.concatenate([self.home, other.home], axis=-1)
        self.send()

    def result(self, late):
        while self.stage < len(self.grid.order) - 1:
            self.step(late)
        return (self.got[0], self.home, self.got[1])


def butterfly(grid, value, moves):
    for move in moves:
        value = jax.tree.map(lambda v: v + grid.move(v, move), value)
    return value


def sum_all(grid, value, beside=None):
    rep = lax.axis_index("rep")
    bits = range(grid.reps.bit_length() - 1)
    pad = -value.shape[1] % (128 * grid.reps)
    columns = value.shape[1]
    value = jnp.pad(value, ((0, 0), (0, pad)))
    for bit in bits:
        half = value.shape[1] // 2
        upper = (rep >> bit) % 2 == 1
        low, high = value[:, :half], value[:, half:]
        got = grid.move(jnp.where(upper, low, high), grid.flip_rep(bit))
        value = jnp.where(upper, high, low) + got
    for bit in range(grid.shards.bit_length() - 1):
        value = value + grid.move(value, grid.flip_shard(bit))
    if beside is not None:
        value = after(value, beside)
    for bit in reversed(bits):
        got = grid.move(value, grid.flip_rep(bit))
        upper = (rep >> bit) % 2 == 1
        value = jnp.concatenate(
            [jnp.where(upper, got, value), jnp.where(upper, value, got)], axis=1
        )
    return value[:, :columns]


def shards(
    grid,
    tokens,
    cotangent,
    segments,
    positions,
    wide_master,
    square_master,
    key_value_master,
    wide_moment,
    square_moment,
    key_value_momentum,
    wide_error,
    square_error,
    key_value_error,
    wide_factor,
    square_factor,
    key_value_factor,
    norm_gains,
    gain_moment,
):
    reps, owners = grid.reps, grid.shards
    rep = lax.axis_index("rep")
    shard = lax.axis_index("shard")
    core = rep % 2
    turn = (shard >> grid.core_bit) % 2
    logical_shard = shard + (core - turn) * (1 << grid.core_bit)

    low_square = square_master.astype(jnp.bfloat16)
    low_narrow = key_value_master.astype(jnp.bfloat16)
    pieces = []
    for j in range(PAIRS):
        pieces.append(low_square[0, :, 384 * j : 384 * j + 384])
        pieces.append(low_narrow[0, :, 128 * j : 128 * j + 128])
        pieces.append(low_narrow[1, :, 128 * j : 128 * j + 128])
    low_attn = jnp.concatenate(pieces + [low_square[1]], axis=1)
    units = wide_master.shape[2] // 3

    position = grid.swap_rows(positions)[0]
    rows = low_attn.shape[0]
    tile = units // reps
    chained = 1 if rows % 16 == 0 else 0
    gain_row = norm_gains.astype(jnp.bfloat16).reshape(1, 2 * rows)
    gain_row = jnp.pad(gain_row, ((0, 15), (0, 1024 - 2 * rows)))
    first = lax.dynamic_slice_in_dim(low_attn, core * 1024, 1024, axis=1)
    first = jnp.concatenate([first, gain_row], axis=0)
    second = lax.dynamic_slice_in_dim(low_attn, 2048 + core * 512, 512, axis=1)
    picks = [core * (reps // 2) + i for i in range(reps // 2)] if chained else []
    groups = [tuple(range(len(picks)))] if chained else []
    for k in range(chained, 3):
        groups.append((len(picks),))
        picks.append(reps * k + rep)
    cuts = list(pack_wide(wide_master, jnp.stack(picks).astype(jnp.int32), groups, tile))
    if chained:
        second = jnp.concatenate([second, cuts[0]], axis=1)
    mine, gathering = gather_pieces(grid, [first, second])
    other = [grid.move(mine[0], grid.flip_rep(0))]
    places = jnp.array(grid.places(), jnp.int32)[jnp.arange(owners) ^ shard]
    cores = core[None]
    gain_w = mine[0][:, rows, : 2 * rows].reshape(owners, 2, rows)
    gain_w = jnp.take(gain_w, places, axis=0).transpose(1, 0, 2).reshape(2, -1).astype(jnp.float32)
    natural = jnp.arange(reps, dtype=jnp.int32)
    whole = jnp.zeros((1,), jnp.int32)
    moved_tokens = grid.move(after(tokens, gathering[1]), grid.swapped)
    tokens = jnp.where(grid.stays(), tokens, moved_tokens)[0]
    moved_out = grid.move(after(cotangent, moved_tokens), grid.swapped)
    model = gain_w.shape[1]
    columns = 640 * PAIRS
    qkv_w = assemble(rows, mine[:1], other[:1], places, cores, 0, columns)

    count = tokens.shape[0]
    hidden_in = tokens.astype(jnp.float32)
    gain_attn, gain_mlp = gain_w[0], gain_w[1]
    cos, sin = rotary_tables(position, HEAD_SIZE)
    cos = jnp.concatenate([cos] * 4, axis=1)
    sin = jnp.concatenate([-sin, sin] * 2, axis=1)
    place = position[:, None]
    order = jnp.array(grid.masks(), jnp.int32) ^ logical_shard

    qkv, turned_in = project_qkv(order, tokens, gain_attn[None], qkv_w, cos, sin)
    held, got = after((mine[1], gathering[-1]), qkv)
    mine[1] = jnp.concatenate([held, got], axis=0)
    qkv = after(qkv, mine[1])
    wide_parts = [None] * chained
    for k in range(chained, 3):
        part = after(cuts[k], mine[1])
        part = lax.all_gather(part, ("rep", "shard"), axis=0, tiled=True)
        wide_parts.append((natural, whole, [part.reshape(reps, owners * rows, 3 * tile)]))
    other.append(grid.move(mine[1], grid.flip_rep(0)))
    attended, logs = attend_forward(qkv, place)
    other[1] = after(other[1], attended)
    d_out = jnp.where(grid.stays(), cotangent, after(moved_out, attended))[0]
    if chained:
        slots = (natural + core * (reps // 2)) % reps
        wide_parts[0] = (slots, places, [mine[1], other[1]])
        residual, normed_mid, turned_mid, out_w = project_out(
            places,
            cores,
            order,
            attended,
            tokens,
            gain_mlp[None],
            [mine[0], other[0], mine[1], other[1]],
        )
    else:
        out_w = assemble(rows, mine, other, places, cores, columns, 3072)
        residual = hidden_in + jnp.einsum(
            "tn,dn->td", attended, out_w, preferred_element_type=jnp.float32
        )
        normed_mid = normed(residual, gain_mlp).astype(jnp.bfloat16)
        turned_mid = turn_rows(normed_mid, order)
    turned_out = turn_rows(d_out, order)

    half = model // 2

    def weight_grad(turned, right):
        return Sums(
            grid,
            jnp.dot(turned[:half], right, preferred_element_type=jnp.float32).astype(jnp.bfloat16),
            jnp.dot(turned[half:], right, preferred_element_type=jnp.float32).astype(jnp.bfloat16),
        )

    wide_sums = []
    result, d_mid = residual, None
    for k in range(3):
        slots, where, weights = wide_parts[k]
        away, home, result, d_mid = mlp_part(
            reps,
            slots,
            where,
            normed_mid,
            d_out,
            turned_mid,
            turned_out,
            weights,
            result,
            d_mid,
            k == 2,
        )
        wide_sums.append(Sums(grid, away, home))
        for earlier in wide_sums[max(0, k - 2) : k]:
            d_mid, result = after((d_mid, result), earlier.step(away))
    result = grid.swap_rows(result[None])

    _, mid_back = jax.vjp(normed, residual, gain_mlp)
    d_residual, grad_gain_mlp = mid_back(d_mid)
    d_residual = d_residual + d_out.astype(jnp.float32)
    d_branch = d_residual.astype(jnp.bfloat16)
    d_attended = jnp.einsum(
        "td,dn->tn", d_branch, out_w, preferred_element_type=jnp.float32
    ).astype(jnp.bfloat16)
    out_sums = weight_grad(turn_rows(d_branch, order), attended)

    d_attended = after(d_attended, wide_sums[2].step(out_sums.away), wide_sums[0].got)
    d_stacks, pair_sums = [], []
    hold = len(grid.order) == 3
    for j in range(PAIRS):
        d_stack, away, home = attend_backward(
            qkv, d_attended, logs, place, cos, sin, turned_in, j
        )
        d_stacks.append(d_stack)
        pair_sums.append(Sums(grid, away, home))
        if j == 0:
            done = (wide_sums[1].step(d_stack), out_sums.step(d_stack), result)
        elif j == 1:
            done = (
                wide_sums[2].step(d_stack),
                out_sums.step(d_stack),
                pair_sums[0].step(d_stack),
                wide_sums[1].got,
            )
        else:
            done = (pair_sums[0].step(d_stack, hold), pair_sums[1].step(d_stack), out_sums.got)
        d_attended = after(d_attended, done, pair_sums[j].away)
        d_stacks = after(d_stacks, done, pair_sums[j].away)
    def back(j):
        return jnp.einsum(
            "tn,dn->td",
            d_stacks[j],
            qkv_w[:, 640 * j : 640 * j + 640],
            preferred_element_type=jnp.float32,
        )

    flag = grid.stays().astype(jnp.int32)[None]
    d_first = back(0)
    d_stacks, wide_got = after(
        (d_stacks, wide_sums[2].got), pair_sums[2].step(d_first), pair_sums[1].step(d_first, hold)
    )
    wide_sums[2].got = wide_got
    d_second = d_first + back(1)
    spans = [(j, 0) for j in range(PAIRS)]
    late_sums = pair_sums
    if hold:
        pair_sums[0].join(pair_sums[1])
        spans = [(0, 0), (0, 640), (1, 0)]
        late_sums = [pair_sums[0], pair_sums[2]]
    mixed_wide, left_wide = mix_wide(
        flag, [part.result(d_first) for part in wide_sums], wide_error, wide_factor
    )
    mixed_out, left_out = mix_rest(
        flag,
        [out_sums.result(d_first)],
        [[(0, 0, model)]],
        [square_error[0, 1]],
        [square_factor[1]],
    )
    last_step = pair_sums[2].step(left_wide)
    rep_moves = [grid.flip_rep(b) for b in range(reps.bit_length() - 1)]
    unit = 128 * reps
    left_early = butterfly(grid, jnp.concatenate([left_wide, left_out], axis=0), rep_moves)
    left_early = after(left_early, last_step)
    gram_early = 9 * units + model
    width = -(-(gram_early + 512) // unit) * unit
    early = contract_all(left_early, [mixed_wide, mixed_out], width)
    narrow = 128 * PAIRS
    early = sum_all(grid, early)

    mixed_query, mixed_key, mixed_value, left_late = mix_rest(
        flag,
        [part.result(left_wide) for part in late_sums],
        [
            [(which, at + first, at + last) for which, at in spans]
            for first, last in ((0, 384), (384, 512), (512, 640))
        ],
        [square_error[0, 0], key_value_error[0, 0], key_value_error[0, 1]],
        [square_factor[0], key_value_factor[0], key_value_factor[1]],
    )
    d_stacks = after(d_stacks, left_late)
    d_normed_in = d_second + back(2)
    _, in_back = jax.vjp(normed, hidden_in, gain_attn)
    d_input, grad_gain_attn = in_back(d_normed_in)
    d_input = (d_input + d_residual).astype(jnp.bfloat16)
    d_input = grid.swap_rows(d_input[None])

    left_late = butterfly(grid, left_late, rep_moves)
    gram_late = columns
    gain_at = gram_late + 384
    width = -(-(gain_at + model) // unit) * unit
    gain_grad = jnp.stack([grad_gain_attn, grad_gain_mlp])
    mixed_late = [mixed_query, mixed_key, mixed_value]
    summed = contract_all(left_late, mixed_late, width, gain_grad)
    wide_new, wide_moment_new, wide_error_new, factor_wide = finish_wide(
        reps, early, gram_early, left_early, mixed_wide, wide_moment, wide_master
    )
    shard_moves = [grid.flip_shard(b) for b in range(owners.bit_length() - 1)]
    summed = butterfly(grid, summed, shard_moves[1:] + rep_moves[:1])
    summed = after(summed, wide_new)
    summed = butterfly(grid, summed, rep_moves[1:] + shard_moves[:1])
    (
        square_new,
        square_moment_new,
        square_error_new,
        factor_square,
        narrow_new,
        narrow_moment_new,
        narrow_error_new,
        factor_narrow,
    ) = finish_rest(
        reps,
        [summed, early],
        [left_late, left_early],
        [mixed_query, mixed_out, mixed_key, mixed_value],
        [
            (0, 0, gram_late, 0),
            (1, 9 * units, gram_early + 384, 24),
            (0, model, gram_late + 128, 8),
            (0, model + narrow, gram_late + 256, 16),
        ],
        [
            (square_moment, square_master, rate_square),
            (key_value_momentum, key_value_master, rate_narrow),
        ],
    )
    gain_total = lax.dynamic_slice_in_dim(
        summed[:2, gain_at : gain_at + model], shard * (model // owners), model // owners, axis=1
    )
    gain_moment_new = decay_rate * gain_moment + gain_total / reps
    gains_new = norm_gains - rate_gains * gain_moment_new
    return (
        result,
        d_input,
        wide_new,
        square_new,
        narrow_new,
        wide_moment_new,
        square_moment_new,
        narrow_moment_new,
        wide_error_new,
        square_error_new,
        narrow_error_new,
        factor_wide,
        factor_square,
        factor_narrow,
        gains_new,
        gain_moment_new,
    )


def solution(mesh):
    return jax.shard_map(
        functools.partial(shards, Grid(mesh)),
        mesh=mesh,
        in_specs=(
            P(("rep", "shard"), None, None),
            P(("rep", "shard"), None, None),
            P(("rep", "shard"), None),
            P(("rep", "shard"), None),
            P(None, "shard", None),
            P(None, "shard", None),
            P(None, "shard", None),
            P(None, "shard", None),
            P(None, "shard", None),
            P(None, "shard", None),
            P("rep", None, "shard", None),
            P("rep", None, "shard", None),
            P("rep", None, "shard", None),
            P(),
            P(),
            P(),
            P(None, "shard"),
            P(None, "shard"),
        ),
        out_specs=(
            P(("rep", "shard"), None, None),
            P(("rep", "shard"), None, None),
            P(None, "shard", None),
            P(None, "shard", None),
            P(None, "shard", None),
            P(None, "shard", None),
            P(None, "shard", None),
            P(None, "shard", None),
            P("rep", None, "shard", None),
            P("rep", None, "shard", None),
            P("rep", None, "shard", None),
            P(),
            P(),
            P(),
            P(None, "shard"),
            P(None, "shard"),
        ),
        check_vma=False,
    )
```

```python
import functools

import jax
import jax.numpy as jnp
from jax import lax
from jax.experimental import pallas as pl
from jax.experimental.pallas import tpu as pltpu
from jax.sharding import PartitionSpec as P

QUERY_HEADS = 18
KEY_VALUE_HEADS = 6
HEAD_SIZE = 64
PAIRS = KEY_VALUE_HEADS // 2


eps_norm = 1e-05
theta_base = 10000.0
decay_rate = 0.9
rate_wide = 0.03
rate_square = 0.1
rate_narrow = 0.02
rate_gains = 0.01
mask_fill = -1e30
highest = lax.Precision.HIGHEST


def normed(value_heads, gain):
    return (
        value_heads
        * lax.rsqrt(jnp.mean(value_heads * value_heads, axis=-1, keepdims=True) + eps_norm)
        * gain
    )


def rotary_tables(position, width):
    halfway = width // 2
    inverse = theta_base ** (-2.0 * jnp.arange(halfway, dtype=jnp.float32) / width)
    angles = position.astype(jnp.float32)[:, None] * inverse[None, :]
    return (jnp.cos(angles), jnp.sin(angles))


BLOCK_ROWS = 256
VMEM_BYTES = 56 * 1024 * 1024


def light(flops, bytes_accessed, transcendentals):
    return pl.CostEstimate(
        flops=flops // 8, bytes_accessed=bytes_accessed // 8, transcendentals=transcendentals // 8
    )


def partner_lanes(values):
    lane = lax.broadcasted_iota(jnp.int32, values.shape, 1)
    return jnp.where(
        lane % HEAD_SIZE < HEAD_SIZE // 2,
        pltpu.roll(values, 128 - HEAD_SIZE // 2, 1),
        pltpu.roll(values, HEAD_SIZE // 2, 1),
    )


def project_kernel(
    order_ref, x_ref, gain_ref, w_ref, cos_ref, sin_ref, out_ref, turned_ref, scratch_ref
):
    x = x_ref[...].astype(jnp.float32)
    scale = lax.rsqrt(jnp.mean(x * x, axis=-1, keepdims=True) + eps_norm)
    low = (x * scale * gain_ref[...]).astype(jnp.bfloat16)
    scratch_ref[...] = low.astype(jnp.float32).T
    share = scratch_ref.shape[0] // order_ref.shape[0]
    parts = [
        scratch_ref[pl.ds(pl.multiple_of(order_ref[p] * share, 8), share), :]
        for p in range(order_ref.shape[0])
    ]
    turned_ref[...] = jnp.concatenate(parts, axis=0).astype(jnp.bfloat16)
    cos, sin = cos_ref[...], sin_ref[...]
    for first in range(0, out_ref.shape[1], 640):
        got = jnp.dot(low, w_ref[:, first : first + 640], preferred_element_type=jnp.float32)
        for at in range(0, 640, 128):
            piece = got[:, at : at + 128]
            if at < 512:
                piece = piece * cos + partner_lanes(piece) * sin
            out_ref[:, first + at : first + at + 128] = piece.astype(jnp.bfloat16)


def project_qkv(order, x, gain, weights, cos, sin):
    rows, width = x.shape
    columns = weights.shape[1]
    block = min(BLOCK_ROWS, rows)
    return pl.pallas_call(
        project_kernel,
        grid_spec=pltpu.PrefetchScalarGridSpec(
            num_scalar_prefetch=1,
            grid=(rows // block,),
            in_specs=[
                pl.BlockSpec((block, width), lambda i, order: (i, 0)),
                pl.BlockSpec((1, width), lambda i, order: (0, 0)),
                pl.BlockSpec((width, columns), lambda i, order: (0, 0)),
                pl.BlockSpec((block, 128), lambda i, order: (i, 0)),
                pl.BlockSpec((block, 128), lambda i, order: (i, 0)),
            ],
            out_specs=[
                pl.BlockSpec((block, columns), lambda i, order: (i, 0)),
                pl.BlockSpec((width, block), lambda i, order: (0, i)),
            ],
            scratch_shapes=[pltpu.VMEM((width, block), jnp.float32)],
        ),
        out_shape=[
            jax.ShapeDtypeStruct((rows, columns), jnp.bfloat16),
            jax.ShapeDtypeStruct((width, rows), jnp.bfloat16),
        ],
        compiler_params=pltpu.CompilerParams(vmem_limit_bytes=VMEM_BYTES),
        cost_estimate=pl.CostEstimate(
            flops=2 * rows * width * columns,
            bytes_accessed=2 * (rows * width * 2 + rows * columns + width * columns),
            transcendentals=0,
        ),
    )(order, x, gain, weights, cos, sin)


def spread_heads(pair, spread_ref):
    wide = pair.astype(jnp.float32)
    turned = pltpu.roll(wide, HEAD_SIZE, 1)
    low_half = lax.broadcasted_iota(jnp.int32, wide.shape, 1) < HEAD_SIZE
    zero = jnp.zeros_like(wide)
    spread_ref[0] = jnp.where(low_half, wide, zero).astype(jnp.bfloat16)
    spread_ref[1] = jnp.where(low_half, zero, turned).astype(jnp.bfloat16)
    spread_ref[2] = jnp.where(low_half, turned, zero).astype(jnp.bfloat16)
    spread_ref[3] = jnp.where(low_half, zero, wide).astype(jnp.bfloat16)


def mask_bias(position, start, keys):
    rows = position.shape[0]
    row = lax.broadcasted_iota(jnp.int32, (rows, keys), 0) + start
    column = lax.broadcasted_iota(jnp.int32, (rows, keys), 1)
    allowed = (column <= row) & (column >= row - position)
    return jnp.where(allowed, 0.0, mask_fill)


def across(left, right):
    return lax.dot_general(
        left, right, (((1,), (1,)), ((), ())), preferred_element_type=jnp.float32
    )


def forward_kernel(qkv_ref, pos_ref, out_ref, log_ref, key_ref, value_ref):
    step = pl.program_id(1)
    block = out_ref.shape[0]

    @pl.when(step == 0)
    def _():
        spread_heads(qkv_ref[:, 384:512], key_ref)
        spread_heads(qkv_ref[:, 512:640], value_ref)

    for place in range(qkv_ref.shape[0] // block):

        @pl.when(step == place)
        def _(place=place):
            start = place * block
            keys = start + block
            bias = mask_bias(pos_ref[...], start, keys)
            lane = lax.broadcasted_iota(jnp.int32, (block, 128), 1)
            logs = jnp.zeros((block, 128), jnp.float32)
            for g in range(3):
                query = qkv_ref[start:keys, 128 * g : 128 * g + 128] * 0.125
                total = jnp.zeros((block, 128), jnp.float32)
                for e in range(2):
                    head = 2 * g + e
                    which = 2 * (head // 3) + e
                    scores = across(query, key_ref[which, :keys, :]) + bias
                    top = jnp.max(scores, axis=-1, keepdims=True)
                    raised = jnp.exp(scores - top)
                    row_total = jnp.sum(raised, axis=-1, keepdims=True)
                    low = (raised * (1.0 / row_total)).astype(jnp.bfloat16)
                    total += jnp.dot(
                        low, value_ref[which, :keys, :], preferred_element_type=jnp.float32
                    )
                    logs = jnp.where(lane == head, top + jnp.log(row_total), logs)
                out_ref[:, 128 * g : 128 * g + 128] = total.astype(jnp.bfloat16)
            log_ref[0] = logs


def attend_forward(qkv, position):
    rows = qkv.shape[0]
    pairs = qkv.shape[1] // 640
    block = min(BLOCK_ROWS, rows)
    return pl.pallas_call(
        forward_kernel,
        grid=(pairs, rows // block),
        in_specs=[
            pl.BlockSpec((rows, 640), lambda j, i: (0, j)),
            pl.BlockSpec((block, 1), lambda j, i: (i, 0)),
        ],
        out_specs=[
            pl.BlockSpec((block, 384), lambda j, i: (i, j)),
            pl.BlockSpec((1, block, 128), lambda j, i: (j, i, 0)),
        ],
        out_shape=[
            jax.ShapeDtypeStruct((rows, 384 * pairs), jnp.bfloat16),
            jax.ShapeDtypeStruct((pairs, rows, 128), jnp.float32),
        ],
        scratch_shapes=[
            pltpu.VMEM((4, rows, 128), jnp.bfloat16),
            pltpu.VMEM((4, rows, 128), jnp.bfloat16),
        ],
        compiler_params=pltpu.CompilerParams(vmem_limit_bytes=VMEM_BYTES),
        cost_estimate=pl.CostEstimate(
            flops=20 * pairs * rows * rows * 128,
            bytes_accessed=8 * rows * 640 * pairs,
            transcendentals=6 * pairs * rows * rows,
        ),
    )(qkv, position)


def backward_kernel(
    qkv_ref,
    d_ref,
    log_ref,
    pos_ref,
    cos_ref,
    sin_ref,
    turned_ref,
    out_ref,
    away_ref,
    home_ref,
    key_ref,
    value_ref,
    dk_ref,
    dv_ref,
):
    step = pl.program_id(0)
    block = d_ref.shape[0]
    blocks = qkv_ref.shape[0] // block

    @pl.when(step == 0)
    def _():
        spread_heads(qkv_ref[:, 384:512], key_ref)
        spread_heads(qkv_ref[:, 512:640], value_ref)
        dk_ref[...] = jnp.zeros_like(dk_ref)
        dv_ref[...] = jnp.zeros_like(dv_ref)

    for place in range(blocks):

        @pl.when(step == place)
        def _(place=place):
            start = place * block
            keys = start + block
            bias = mask_bias(pos_ref[...], start, keys)
            logs = log_ref[0]
            cos, sin = cos_ref[start:keys, :], sin_ref[start:keys, :]
            for g in range(3):
                query = qkv_ref[start:keys, 128 * g : 128 * g + 128] * 0.125
                d_out = d_ref[:, 128 * g : 128 * g + 128]
                query_turned = query.astype(jnp.float32).T.astype(jnp.bfloat16)
                d_turned = d_out.astype(jnp.float32).T.astype(jnp.bfloat16)
                total = jnp.zeros((block, 128), jnp.float32)
                for e in range(2):
                    head = 2 * g + e
                    which = 2 * (head // 3) + e
                    at = HEAD_SIZE * (head // 3)
                    key = key_ref[which, :keys, :]
                    scores = across(query, key) + bias
                    prob = jnp.exp(scores - logs[:, head : head + 1])
                    d_prob = across(d_out, value_ref[which, :keys, :])
                    delta = jnp.sum(prob * d_prob, axis=-1, keepdims=True)
                    d_scores = (prob * (d_prob - delta)).astype(jnp.bfloat16)
                    half = slice(HEAD_SIZE * e, HEAD_SIZE * e + HEAD_SIZE)
                    dv_ref[at : at + HEAD_SIZE, :keys] += jnp.dot(
                        d_turned[half], prob.astype(jnp.bfloat16), preferred_element_type=jnp.float32
                    )
                    dk_ref[at : at + HEAD_SIZE, :keys] += jnp.dot(
                        query_turned[half], d_scores, preferred_element_type=jnp.float32
                    )
                    total += jnp.dot(d_scores, key, preferred_element_type=jnp.float32)
                total = total * 0.125
                total = total * cos - partner_lanes(total) * sin
                out_ref[start:keys, 128 * g : 128 * g + 128] = total.astype(jnp.bfloat16)

    @pl.when(step == blocks - 1)
    def _():
        d_key = dk_ref[...].T
        d_key = d_key * cos_ref[...] - partner_lanes(d_key) * sin_ref[...]
        out_ref[:, 384:512] = d_key.astype(jnp.bfloat16)
        out_ref[:, 512:640] = dv_ref[...].T.astype(jnp.bfloat16)
        half = away_ref.shape[0]
        for first, grad_ref in ((0, away_ref), (half, home_ref)):
            grad_ref[...] = jnp.dot(
                turned_ref[first : first + half, :],
                out_ref[...],
                preferred_element_type=jnp.float32,
            ).astype(jnp.bfloat16)


def attend_backward(qkv, d_attended, logs, position, cos, sin, turned, pair):
    rows = qkv.shape[0]
    model = turned.shape[0]
    block = min(BLOCK_ROWS, rows)
    half = pl.BlockSpec((model // 2, 640), lambda i: (0, 0))
    return pl.pallas_call(
        backward_kernel,
        grid=(rows // block,),
        in_specs=[
            pl.BlockSpec((rows, 640), lambda i: (0, pair)),
            pl.BlockSpec((block, 384), lambda i: (i, pair)),
            pl.BlockSpec((1, block, 128), lambda i: (pair, i, 0)),
            pl.BlockSpec((block, 1), lambda i: (i, 0)),
            pl.BlockSpec((rows, 128), lambda i: (0, 0)),
            pl.BlockSpec((rows, 128), lambda i: (0, 0)),
            pl.BlockSpec((model, rows), lambda i: (0, 0), pipeline_mode=pl.Buffered(1)),
        ],
        out_specs=[pl.BlockSpec((rows, 640), lambda i: (0, 0)), half, half],
        out_shape=[
            jax.ShapeDtypeStruct((rows, 640), jnp.bfloat16),
            jax.ShapeDtypeStruct((model // 2, 640), jnp.bfloat16),
            jax.ShapeDtypeStruct((model // 2, 640), jnp.bfloat16),
        ],
        scratch_shapes=[
            pltpu.VMEM((4, rows, 128), jnp.bfloat16),
            pltpu.VMEM((4, rows, 128), jnp.bfloat16),
            pltpu.VMEM((128, rows), jnp.float32),
            pltpu.VMEM((128, rows), jnp.float32),
        ],
        compiler_params=pltpu.CompilerParams(vmem_limit_bytes=VMEM_BYTES),
        cost_estimate=pl.CostEstimate(
            flops=50 * rows * rows * 128,
            bytes_accessed=8 * rows * 640,
            transcendentals=6 * rows * rows,
        ),
    )(qkv, d_attended, logs, position, cos, sin, turned)


def turn_kernel(order_ref, rows_ref, out_ref, turned_ref):
    turned_ref[...] = rows_ref[...].astype(jnp.float32).T
    owners = order_ref.shape[0]
    share = turned_ref.shape[0] // owners
    parts = [
        turned_ref[pl.ds(pl.multiple_of(order_ref[p] * share, 8), share), :] for p in range(owners)
    ]
    out_ref[...] = jnp.concatenate(parts, axis=0).astype(jnp.bfloat16)


def turn_rows(rows, order):
    count, model = rows.shape
    block = min(BLOCK_ROWS, count)
    return pl.pallas_call(
        turn_kernel,
        grid_spec=pltpu.PrefetchScalarGridSpec(
            num_scalar_prefetch=1,
            grid=(count // block,),
            in_specs=[pl.BlockSpec((block, model), lambda i, order: (i, 0))],
            out_specs=pl.BlockSpec((model, block), lambda i, order: (0, i)),
            scratch_shapes=[pltpu.VMEM((model, block), jnp.float32)],
        ),
        out_shape=jax.ShapeDtypeStruct((model, count), jnp.bfloat16),
        compiler_params=pltpu.CompilerParams(vmem_limit_bytes=VMEM_BYTES),
        cost_estimate=pl.CostEstimate(
            flops=0, bytes_accessed=4 * count * model, transcendentals=0
        ),
    )(order, rows)


def mlp_kernel(reps, first, last, slot_ref, place_ref, mid_ref, d_ref, *refs):
    del slot_ref
    mid_hbm, d_hbm = refs[:2]
    befores = refs[2 : 3 if first else 4]
    refs = refs[2 + len(befores) :]
    weight_hbm, refs = (refs[:1], refs[1:]) if place_ref.shape[0] == 1 else (refs[:2], refs[2:])
    away_ref, home_ref, result_ref, back_ref = refs[:4]
    weight_ref, mid_turned_ref, d_turned_ref, d_pair_ref, hidden_ref, weight_sem, sem = refs[4:11]
    output_ref = result_ref
    if last:
        result_ref = refs[11]
    step = pl.program_id(0)
    count = mid_ref.shape[0]
    part = min(512, count)
    tile = hidden_ref.shape[1]
    half = away_ref.shape[1]

    wide = 3 * tile
    skip = weight_hbm[0].shape[2] - wide * (reps // 2)

    def load(i):
        if len(weight_hbm) == 1:
            pltpu.make_async_copy(
                weight_hbm[0].at[i], weight_ref.at[i], weight_sem.at[i]
            ).start()
            return
        ref, at = weight_hbm[2 * i // reps], i % (reps // 2)
        owners, share = ref.shape[:2]
        for a in range(owners):
            pltpu.make_async_copy(
                ref.at[place_ref[a], :, skip + wide * at : skip + wide * at + wide],
                weight_ref.at[i, share * a : share * a + share, :],
                weight_sem.at[i],
            ).start()

    sums = [pltpu.make_async_copy(befores[0], result_ref, sem.at[0])]
    if not first:
        sums.append(pltpu.make_async_copy(befores[1], back_ref, sem.at[1]))
    turned = [
        pltpu.make_async_copy(mid_hbm, mid_turned_ref, sem.at[2]),
        pltpu.make_async_copy(d_hbm, d_turned_ref, sem.at[3]),
    ]

    @pl.when(step == 0)
    def _():
        load(0)
        for copy in sums + turned:
            copy.start()
        for i in range(1, reps):
            load(i)
        if first:
            back_ref[...] = jnp.zeros_like(back_ref)

    for i in range(reps):

        @pl.when(step == i)
        def _(i=i):
            pltpu.make_async_copy(weight_ref.at[i], weight_ref.at[i], weight_sem.at[i]).wait()

    @pl.when(step == 0)
    def _():
        for copy in sums:
            copy.wait()

    @pl.loop(0, count // part)
    def _(t):
        rows = pl.ds(pl.multiple_of(t * part, part), part)
        pair_w = weight_ref[step, :, : 2 * tile]
        down_w = weight_ref[step, :, 2 * tile :]
        pair = jnp.dot(mid_ref[rows, :], pair_w, preferred_element_type=jnp.float32)
        d_hidden = jnp.dot(d_ref[rows, :], down_w, preferred_element_type=jnp.float32)
        gate, up = pair[:, :tile], pair[:, tile:]
        sig = jax.nn.sigmoid(gate)
        silu = gate * sig
        hidden = (silu * up).astype(jnp.bfloat16)
        hidden_ref[rows, :] = hidden
        d_gate = d_hidden * up * (sig * (1.0 + gate * (1.0 - sig)))
        d_pair_ref[rows, :tile] = d_gate.astype(jnp.bfloat16)
        d_pair_ref[rows, tile:] = (d_hidden * silu).astype(jnp.bfloat16)
        back_ref[rows, :] += across(d_pair_ref[rows, :], pair_w)
        result_ref[rows, :] += across(hidden, down_w)
        if last:

            @pl.when(step == reps - 1)
            def _():
                output_ref[rows, :] = result_ref[rows, :].astype(jnp.bfloat16)

    @pl.when(step == 0)
    def _():
        for copy in turned:
            copy.wait()

    for at, out_ref in ((0, away_ref), (half, home_ref)):
        pair = jnp.dot(
            mid_turned_ref[at : at + half, :], d_pair_ref[...], preferred_element_type=jnp.float32
        )
        out_ref[0] = pair[:, :tile].astype(jnp.bfloat16)
        out_ref[1] = pair[:, tile:].astype(jnp.bfloat16)
        out_ref[2] = jnp.dot(
            d_turned_ref[at : at + half, :], hidden_ref[...], preferred_element_type=jnp.float32
        ).astype(jnp.bfloat16)


def mlp_part(reps, slots, places, mid, d_out, mid_turned, d_turned, weights, result, back, last):
    count, model = mid.shape
    tile = (weights[0].shape[2] - (512 if len(weights) == 2 else 0)) // 3
    if len(weights) == 2:
        tile //= reps // 2
    units = tile * reps
    half = model // 2
    first = back is None
    befores = [result] if first else [result, back]

    def once(shape):
        return pl.BlockSpec(shape, lambda i, slots, places: (0, 0), pipeline_mode=pl.Buffered(1))

    anywhere = pl.BlockSpec(memory_space=pl.ANY)
    return pl.pallas_call(
        functools.partial(mlp_kernel, reps, first, last),
        grid_spec=pltpu.PrefetchScalarGridSpec(
            num_scalar_prefetch=2,
            grid=(reps,),
            in_specs=[once((count, model))] * 2 + [anywhere] * (2 + len(befores) + len(weights)),
            out_specs=[
                pl.BlockSpec((3, half, tile), lambda i, slots, places: (0, 0, slots[i])),
                pl.BlockSpec((3, half, tile), lambda i, slots, places: (0, 0, slots[i])),
                once((count, model)),
                once((count, model)),
            ],
            scratch_shapes=[
                pltpu.VMEM((reps, model, 3 * tile), jnp.bfloat16),
                pltpu.VMEM((model, count), jnp.bfloat16),
                pltpu.VMEM((model, count), jnp.bfloat16),
                pltpu.VMEM((count, 2 * tile), jnp.bfloat16),
                pltpu.VMEM((count, tile), jnp.bfloat16),
                pltpu.SemaphoreType.DMA((reps,)),
                pltpu.SemaphoreType.DMA((4,)),
            ]
            + ([pltpu.VMEM((count, model), jnp.float32)] if last else []),
        ),
        out_shape=[
            jax.ShapeDtypeStruct((3, half, units), jnp.bfloat16),
            jax.ShapeDtypeStruct((3, half, units), jnp.bfloat16),
            jax.ShapeDtypeStruct((count, model), jnp.bfloat16 if last else jnp.float32),
            jax.ShapeDtypeStruct((count, model), jnp.float32),
        ],
        compiler_params=pltpu.CompilerParams(vmem_limit_bytes=VMEM_BYTES),
        cost_estimate=pl.CostEstimate(
            flops=18 * count * model * units,
            bytes_accessed=2 * (4 * count * model + 6 * model * units) + 16 * count * model,
            transcendentals=count * units,
        ),
    )(slots, places, mid, d_out, mid_turned, d_turned, *befores, *weights)


def assemble(rows, mine, other, places, core, low, high):
    owners = mine[0].shape[0]
    widths = [m.shape[2] for m in mine]
    count = len(mine)

    def kernel(place_ref, core_ref, *refs):
        del place_ref
        out_ref = refs[-1]
        for own in range(2):

            @pl.when(core_ref[0] == own)
            def _(own=own):
                at = 0
                for i in range(count):
                    for half in range(2):
                        ref = refs[i] if half == own else refs[count + i]
                        first, last = max(low, at), min(high, at + widths[i])
                        if first < last:
                            out_ref[0, :, first - low : last - low] = ref[
                                0, :, first - at : last - at
                            ]
                        at += widths[i]

    def spec(width):
        return pl.BlockSpec((1, rows, width), lambda a, place, core: (place[a], 0, 0))

    out = pl.pallas_call(
        kernel,
        grid_spec=pltpu.PrefetchScalarGridSpec(
            num_scalar_prefetch=2,
            grid=(owners,),
            in_specs=[spec(w) for w in widths] * 2,
            out_specs=pl.BlockSpec((1, rows, high - low), lambda a, place, core: (a, 0, 0)),
        ),
        out_shape=jax.ShapeDtypeStruct((owners, rows, high - low), jnp.bfloat16),
        compiler_params=pltpu.CompilerParams(vmem_limit_bytes=VMEM_BYTES),
        cost_estimate=pl.CostEstimate(
            flops=0, bytes_accessed=8 * owners * rows * sum(widths), transcendentals=0
        ),
    )(places, core, *mine, *other)
    return out.reshape(owners * rows, high - low)


def left_rows(factor, rows):
    lane = lax.broadcasted_iota(jnp.int32, (rows.shape[0], 128), 1)
    columns = jnp.zeros((rows.shape[0], 128), jnp.float32)
    for r in range(8):
        column = jnp.sum(rows * factor[r : r + 1, :], axis=1, keepdims=True)
        columns = jnp.where(lane == r, column, columns)
    return columns.T[:8, :]


def exact_dot(left, right, contract):
    return lax.dot_general(
        left, right, (contract, ((), ())), precision=highest, preferred_element_type=jnp.float32
    )


def mix_kernel(layout, count, flag_ref, *refs):
    sums, refs = refs[: 3 * count], refs[3 * count :]
    errors, refs = refs[: len(layout)], refs[len(layout) :]
    factors, refs = refs[: len(layout)], refs[len(layout) :]
    mixed, left_ref = refs[: len(layout)], refs[len(layout)]
    stays = flag_ref[0] == 1
    for m, pieces in enumerate(layout):
        at = 0
        for which, first, last in pieces:
            away, home, moved = (
                sums[3 * which + k][..., first:last].astype(jnp.float32) for k in range(3)
            )
            width = last - first
            where = (..., slice(at, at + width))
            total = away + jnp.where(stays, home, moved)
            total = total.reshape(total.shape[-2:])
            error = errors[m][where]
            error = error.reshape(error.shape[-2:])
            mixed[m][where] = (total + error).reshape(mixed[m].shape[:-1] + (width,))
            at += width
        rows = mixed[m][...].reshape(mixed[m].shape[-2:])
        factor = factors[m][...].reshape(factors[m].shape[-2:])
        left_ref[8 * m : 8 * m + 8, :] = left_rows(factor, rows)


def mix_wide(flag, parts, error, factor):
    count, rows, third = parts[0][0].shape
    columns = third * len(parts)
    arrays = [a for part in parts for a in part]
    layout = [[(i, 0, third) for i in range(len(parts))]]
    return pl.pallas_call(
        functools.partial(mix_kernel, layout, len(parts)),
        grid_spec=pltpu.PrefetchScalarGridSpec(
            num_scalar_prefetch=1,
            grid=(count,),
            in_specs=[pl.BlockSpec((1, rows, third), lambda i, flag: (i, 0, 0))] * len(arrays)
            + [
                pl.BlockSpec((1, 1, rows, columns), lambda i, flag: (0, i, 0, 0)),
                pl.BlockSpec((1, 8, columns), lambda i, flag: (i, 0, 0)),
            ],
            out_specs=[
                pl.BlockSpec((1, rows, columns), lambda i, flag: (i, 0, 0)),
                pl.BlockSpec((8, rows), lambda i, flag: (i, 0)),
            ],
        ),
        out_shape=[
            jax.ShapeDtypeStruct((count, rows, columns), jnp.float32),
            jax.ShapeDtypeStruct((8 * count, rows), jnp.float32),
        ],
        compiler_params=pltpu.CompilerParams(vmem_limit_bytes=VMEM_BYTES),
        cost_estimate=pl.CostEstimate(
            flops=96 * count * rows * columns,
            bytes_accessed=14 * count * rows * columns,
            transcendentals=0,
        ),
    )(flag, *arrays, error, factor)


def in_vmem(count):
    return [pl.BlockSpec(memory_space=pltpu.VMEM)] * count


def mix_rest(flag, parts, layout, errors, factors):
    rows = errors[0].shape[0]
    arrays = [a for part in parts for a in part]
    return pl.pallas_call(
        functools.partial(mix_kernel, layout, len(parts)),
        in_specs=[pl.BlockSpec(memory_space=pltpu.SMEM)]
        + in_vmem(len(arrays) + len(errors) + len(factors)),
        out_specs=in_vmem(len(errors) + 1),
        out_shape=[jax.ShapeDtypeStruct(e.shape, jnp.float32) for e in errors]
        + [jax.ShapeDtypeStruct((8 * len(errors), rows), jnp.float32)],
        compiler_params=pltpu.CompilerParams(vmem_limit_bytes=VMEM_BYTES),
        cost_estimate=pl.CostEstimate(
            flops=96 * sum(e.size for e in errors),
            bytes_accessed=14 * sum(e.size for e in errors),
            transcendentals=0,
        ),
    )(flag, *arrays, *errors, *factors)


def contract_all(left, mixed, width, extra=None):
    def kernel(*refs):
        left_ref, out_ref = refs[0], refs[-1]
        out_ref[...] = jnp.zeros_like(out_ref)
        at, m = 0, 0
        for ref in refs[1 : 1 + len(mixed)]:
            for k in range(ref.shape[0] if len(ref.shape) == 3 else 1):
                rows = ref[k] if len(ref.shape) == 3 else ref[...]
                own = left_ref[8 * m : 8 * m + 8, :]
                out_ref[:, at : at + rows.shape[1]] = exact_dot(own, rows, ((1,), (0,)))
                at += rows.shape[1]
                m += 1
        for k in range(m):
            own = left_ref[8 * k : 8 * k + 8, :]
            out_ref[:, at : at + 8] = exact_dot(own, own, ((1,), (1,)))
            at += 128
        if extra is not None:
            out_ref[: extra.shape[0], at : at + extra.shape[1]] = refs[-2][...]

    more = [] if extra is None else [extra]
    return pl.pallas_call(
        kernel,
        in_specs=in_vmem(1 + len(mixed) + len(more)),
        out_specs=pl.BlockSpec(memory_space=pltpu.VMEM),
        out_shape=jax.ShapeDtypeStruct((8, width), jnp.float32),
        compiler_params=pltpu.CompilerParams(vmem_limit_bytes=VMEM_BYTES),
        cost_estimate=pl.CostEstimate(
            flops=96 * sum(m.size for m in mixed),
            bytes_accessed=4 * sum(m.size for m in mixed),
            transcendentals=0,
        ),
    )(left, *mixed, *more)


def eliminate(gram, rights):
    row = lax.broadcasted_iota(jnp.int32, (8, 1), 0)
    for j in range(8):
        scale = 1.0 / jnp.sqrt(gram[j : j + 1, j : j + 1])
        below = jnp.where(row > j, gram[:, j : j + 1] * scale, 0.0)
        done = []
        for right in [gram] + list(rights):
            top = right[j : j + 1, :] * scale
            done.append(jnp.where(row == j, top, right - below * top))
        gram, rights = done[0], done[1:]
    return rights


def finish_matrix(reps, rate, row, gram, left, mixed, moment, master, outs):
    new_ref, moment_new_ref, error_ref, factor_ref = outs
    factor, basis = eliminate(gram[:, :8] * (1.0 / reps), [row, left])
    factor = factor * (1.0 / reps)
    factor_ref[...] = factor
    turned = basis.T
    columns = factor.shape[1]
    for first in range(0, columns, 256):
        span = slice(first, min(first + 256, columns))
        approx = turned[:, 0:1] * factor[0:1, span]
        for r in range(1, 8):
            approx += turned[:, r : r + 1] * factor[r : r + 1, span]
        moment_new = decay_rate * moment[:, span] + approx
        moment_new_ref[:, span] = moment_new
        new_ref[:, span] = master[:, span] - rate * moment_new
        error_ref[:, span] = mixed[:, span] - approx


def finish_wide(reps, packed, gram_at, left, mixed, moment, master):
    count, rows, columns = mixed.shape

    def kernel(row_ref, gram_ref, left_ref, mixed_ref, moment_ref, master_ref, *outs):
        new_ref, moment_new_ref, error_ref, factor_ref = outs
        finish_matrix(
            reps,
            rate_wide,
            row_ref[...],
            gram_ref[...],
            left_ref[...],
            mixed_ref.at[0],
            moment_ref.at[0],
            master_ref.at[0],
            (new_ref.at[0], moment_new_ref.at[0], error_ref.at[0, 0], factor_ref.at[0]),
        )

    whole = pl.BlockSpec((1, rows, columns), lambda i: (i, 0, 0))
    shape = jax.ShapeDtypeStruct((count, rows, columns), jnp.float32)
    return pl.pallas_call(
        kernel,
        grid=(count,),
        in_specs=[
            pl.BlockSpec((8, columns), lambda i: (0, i)),
            pl.BlockSpec((8, 128), lambda i: (0, gram_at // 128 + i)),
            pl.BlockSpec((8, rows), lambda i: (i, 0)),
            whole,
            whole,
            whole,
        ],
        out_specs=[
            whole,
            whole,
            pl.BlockSpec((1, 1, rows, columns), lambda i: (0, i, 0, 0)),
            pl.BlockSpec((1, 8, columns), lambda i: (i, 0, 0)),
        ],
        out_shape=[
            shape,
            shape,
            jax.ShapeDtypeStruct((1, count, rows, columns), jnp.float32),
            jax.ShapeDtypeStruct((count, 8, columns), jnp.float32),
        ],
        compiler_params=pltpu.CompilerParams(vmem_limit_bytes=VMEM_BYTES),
        cost_estimate=light(
            flops=96 * count * rows * columns,
            bytes_accessed=24 * count * rows * columns,
            transcendentals=0,
        ),
    )(packed, packed, left, mixed, moment, master)


def finish_rest(reps, packs, lefts, mixed, where, states):
    groups = []
    at = 0
    for moment, _, rate in states:
        groups.append((at, moment.shape[0], rate))
        at += moment.shape[0]

    def kernel(*refs):
        pack_refs, refs = refs[: len(packs)], refs[len(packs) :]
        left_refs, refs = refs[: len(lefts)], refs[len(lefts) :]
        mixed_refs, refs = refs[: len(mixed)], refs[len(mixed) :]
        state_refs, outs = refs[: 2 * len(states)], refs[2 * len(states) :]
        for g, (first, count, rate) in enumerate(groups):
            new_ref, moment_new_ref, error_ref, factor_ref = outs[4 * g : 4 * g + 4]
            for k in range(count):
                pack, row_at, gram_at, left_at = where[first + k]
                rows = mixed_refs[first + k]
                finish_matrix(
                    reps,
                    rate,
                    pack_refs[pack][:, row_at : row_at + rows.shape[1]],
                    pack_refs[pack][:, gram_at : gram_at + 128],
                    left_refs[pack][left_at : left_at + 8, :],
                    rows,
                    state_refs[2 * g].at[k],
                    state_refs[2 * g + 1].at[k],
                    (new_ref.at[k], moment_new_ref.at[k], error_ref.at[0, k], factor_ref.at[k]),
                )

    shapes = []
    for moment, _, _ in states:
        count, rows, columns = moment.shape
        shapes += [
            jax.ShapeDtypeStruct(moment.shape, jnp.float32),
            jax.ShapeDtypeStruct(moment.shape, jnp.float32),
            jax.ShapeDtypeStruct((1,) + moment.shape, jnp.float32),
            jax.ShapeDtypeStruct((count, 8, columns), jnp.float32),
        ]
    arrays = [a for state in states for a in state[:2]]
    return pl.pallas_call(
        kernel,
        in_specs=in_vmem(len(packs) + len(lefts) + len(mixed) + len(arrays)),
        out_specs=in_vmem(len(shapes)),
        out_shape=shapes,
        compiler_params=pltpu.CompilerParams(vmem_limit_bytes=VMEM_BYTES),
        cost_estimate=light(
            flops=96 * sum(m.size for m in mixed),
            bytes_accessed=24 * sum(m.size for m in mixed),
            transcendentals=0,
        ),
    )(*packs, *lefts, *mixed, *arrays)


def pack_wide(master, picks, groups, tile):
    count, rows, _ = master.shape
    number = picks.shape[0]

    def kernel(pick_ref, *refs):
        del pick_ref
        for group, out_ref in zip(groups, refs[number:]):
            at = 0
            for pick in group:
                for i in range(count):
                    out_ref[:, at : at + tile] = refs[pick][i].astype(jnp.bfloat16)
                    at += tile

    def spec(n):
        return pl.BlockSpec((count, rows, tile), lambda i, picks: (0, 0, picks[n]))

    shapes = [
        jax.ShapeDtypeStruct((rows, count * tile * len(group)), jnp.bfloat16) for group in groups
    ]
    return pl.pallas_call(
        kernel,
        grid_spec=pltpu.PrefetchScalarGridSpec(
            num_scalar_prefetch=1,
            grid=(1,),
            in_specs=[spec(n) for n in range(number)],
            out_specs=[pl.BlockSpec(s.shape, lambda i, picks: (0, 0)) for s in shapes],
        ),
        out_shape=shapes,
        compiler_params=pltpu.CompilerParams(vmem_limit_bytes=VMEM_BYTES),
        cost_estimate=pl.CostEstimate(
            flops=0, bytes_accessed=6 * number * count * rows * tile, transcendentals=0
        ),
    )(picks, *[master] * number)


def split_sum(home, got):
    shape = home.shape
    rows, columns = shape[-2:]
    lead = home.size // (rows * columns)
    half = rows // 2

    def kernel(home_ref, got_ref, away_ref, kept_ref):
        total = home_ref[0].astype(jnp.float32) + got_ref[0].astype(jnp.float32)
        away_ref[0] = total[:half].astype(jnp.bfloat16)
        kept_ref[0] = total[half:].astype(jnp.bfloat16)

    whole = pl.BlockSpec((1, rows, columns), lambda i: (i, 0, 0))
    part = pl.BlockSpec((1, half, columns), lambda i: (i, 0, 0))
    out = jax.ShapeDtypeStruct((lead, half, columns), jnp.bfloat16)
    away, kept = pl.pallas_call(
        kernel,
        grid=(lead,),
        in_specs=[whole, whole],
        out_specs=[part, part],
        out_shape=[out, out],
        compiler_params=pltpu.CompilerParams(vmem_limit_bytes=VMEM_BYTES),
        cost_estimate=pl.CostEstimate(
            flops=home.size, bytes_accessed=6 * home.size, transcendentals=0
        ),
    )(home.reshape(lead, rows, columns), got.reshape(lead, rows, columns))
    tail = (half, columns)
    return away.reshape(shape[:-2] + tail), kept.reshape(shape[:-2] + tail)


def out_kernel(owners, place_ref, core_ref, order_ref, att_ref, x_ref, gain_ref, *refs):
    halves, refs = refs[:4], refs[4:]
    residual_ref, mid_ref, mid_turned_ref, w_ref, turned_ref, sem = refs
    share = w_ref.shape[0] // owners

    @pl.when(pl.program_id(0) == 0)
    def _():
        for own in range(2):

            @pl.when(core_ref[0] == own)
            def _(own=own):
                spans = (
                    (halves[0 if own == 1 else 1], 896, 0, 128),
                    (halves[2 if own == 0 else 3], 0, 128, 512),
                    (halves[2 if own == 1 else 3], 0, 640, 512),
                )
                for ref, first, at, width in spans:
                    for a in range(owners):
                        pltpu.make_async_copy(
                            ref.at[place_ref[a], :share, first : first + width],
                            w_ref.at[share * a : share * a + share, at : at + width],
                            sem.at[0],
                        ).start()

        pltpu.make_async_copy(w_ref, w_ref, sem.at[0]).wait()

    residual = x_ref[...].astype(jnp.float32) + across(att_ref[...], w_ref[...])
    residual_ref[...] = residual
    scale = lax.rsqrt(jnp.mean(residual * residual, axis=-1, keepdims=True) + eps_norm)
    mid = (residual * scale * gain_ref[...]).astype(jnp.bfloat16)
    mid_ref[...] = mid
    turned_ref[...] = mid.astype(jnp.float32).T
    parts = [
        turned_ref[pl.ds(pl.multiple_of(order_ref[p] * share, 8), share), :] for p in range(owners)
    ]
    mid_turned_ref[...] = jnp.concatenate(parts, axis=0).astype(jnp.bfloat16)


def project_out(places, core, order, attended, x, gain, halves):
    count, model = x.shape
    owners = order.shape[0]
    block = min(BLOCK_ROWS, count)
    rows = pl.BlockSpec((block, model), lambda i, *_: (i, 0))
    return pl.pallas_call(
        functools.partial(out_kernel, owners),
        grid_spec=pltpu.PrefetchScalarGridSpec(
            num_scalar_prefetch=3,
            grid=(count // block,),
            in_specs=[rows, rows, pl.BlockSpec((1, model), lambda i, *_: (0, 0))]
            + [pl.BlockSpec(memory_space=pl.ANY)] * 4,
            out_specs=[
                rows,
                rows,
                pl.BlockSpec((model, block), lambda i, *_: (0, i)),
                pl.BlockSpec((model, model), lambda i, *_: (0, 0)),
            ],
            scratch_shapes=[
                pltpu.VMEM((model, block), jnp.float32),
                pltpu.SemaphoreType.DMA((1,)),
            ],
        ),
        out_shape=[
            jax.ShapeDtypeStruct((count, model), jnp.float32),
            jax.ShapeDtypeStruct((count, model), jnp.bfloat16),
            jax.ShapeDtypeStruct((model, count), jnp.bfloat16),
            jax.ShapeDtypeStruct((model, model), jnp.bfloat16),
        ],
        compiler_params=pltpu.CompilerParams(vmem_limit_bytes=VMEM_BYTES),
        cost_estimate=pl.CostEstimate(
            flops=2 * count * model * model,
            bytes_accessed=12 * count * model + 4 * model * model,
            transcendentals=count,
        ),
    )(places, core, order, attended, x, gain, *halves)


class Grid:
    def __init__(self, mesh):
        self.reps = mesh.shape["rep"]
        self.shards = mesh.shape["shard"]
        self.core_bit = self.shards.bit_length() - 3
        stages = self.shards.bit_length() - 1
        self.order = [self.core_bit] + [b for b in range(stages) if b != self.core_bit]

    def swapped(self, rep, shard):
        bit = self.core_bit
        core = rep & 1
        turn = (shard >> bit) & 1
        return (rep - core + turn, shard - (turn << bit) + (core << bit))

    def flat(self, pair):
        return pair[0] * self.shards + pair[1]

    def every(self):
        return [(r, s) for r in range(self.reps) for s in range(self.shards)]

    def move(self, value, target):
        pairs = [(self.flat(p), self.flat(target(*p))) for p in self.every() if target(*p) != p]
        return lax.ppermute(value, ("rep", "shard"), pairs)

    def stays(self):
        return lax.axis_index("rep") % 2 == (lax.axis_index("shard") >> self.core_bit) % 2

    def swap_rows(self, value):
        return jnp.where(self.stays(), value, self.move(value, self.swapped))

    def partner(self, bit):
        def target(rep, shard):
            lr, ls = self.swapped(rep, shard)
            return self.swapped(lr, ls ^ (1 << bit))

        return target

    def last(self, bit):
        def target(rep, shard):
            lr, ls = self.swapped(rep, shard)
            return (lr, ls ^ (1 << bit))

        return target

    def flip_rep(self, bit):
        return lambda rep, shard: (rep ^ (1 << bit), shard)

    def flip_shard(self, bit):
        return lambda rep, shard: (rep, shard ^ (1 << bit))

    def doubling(self):
        return list(range(len(self.order)))[::-1]

    def places(self):
        out = [0] * self.shards
        for place in range(self.shards):
            distance = 0
            for k, bit in enumerate(self.doubling()):
                if (place >> k) & 1:
                    distance |= 1 << bit
            out[distance] = place
        return out

    def masks(self):
        count = len(self.order)
        out = []
        for place in range(self.shards):
            mask = 0
            for k, bit in enumerate(self.order):
                if not (place >> (count - 1 - k)) & 1:
                    mask |= 1 << bit
            out.append(mask)
        return out


def after(value, *others):
    return lax.optimization_barrier((value, others))[0]


def gather_pieces(grid, blocks):
    mine = []
    before = [None] * len(grid.order)
    for number, block in enumerate(blocks):
        held = block[None]
        for k, bit in enumerate(grid.doubling()):
            last = k == len(before) - 1
            if before[k] is not None:
                held = after(held, before[k])
            before[k] = grid.move(held, grid.flip_shard(bit))
            if not (last and number == len(blocks) - 1):
                held = jnp.concatenate([held, before[k]], axis=0)
        mine.append(held)
    return mine, before


class Sums:
    def __init__(self, grid, away, home):
        self.grid = grid
        self.stage = 0
        self.away, self.home = away, home
        self.send()

    def send(self):
        grid, bit = self.grid, self.grid.order[self.stage]
        if self.stage == len(grid.order) - 1:
            self.got = (grid.move(self.away, grid.last(bit)), grid.move(self.home, grid.swapped))
        else:
            self.got = grid.move(self.away, grid.partner(bit))

    def step(self, late, hold=False):
        self.got = after(self.got, late)
        self.away, self.home = split_sum(self.home, self.got)
        self.stage += 1
        if not hold:
            self.send()
        return (self.away, self.home)

    def join(self, other):
        self.away = jnp.concatenate([self.away, other.away], axis=-1)
        self.home = jnp.concatenate([self.home, other.home], axis=-1)
        self.send()

    def result(self, late):
        while self.stage < len(self.grid.order) - 1:
            self.step(late)
        return (self.got[0], self.home, self.got[1])


def butterfly(grid, value, moves):
    for move in moves:
        value = jax.tree.map(lambda v: v + grid.move(v, move), value)
    return value


def sum_all(grid, value, beside=None):
    rep = lax.axis_index("rep")
    bits = range(grid.reps.bit_length() - 1)
    pad = -value.shape[1] % (128 * grid.reps)
    columns = value.shape[1]
    value = jnp.pad(value, ((0, 0), (0, pad)))
    for bit in bits:
        half = value.shape[1] // 2
        upper = (rep >> bit) % 2 == 1
        low, high = value[:, :half], value[:, half:]
        got = grid.move(jnp.where(upper, low, high), grid.flip_rep(bit))
        value = jnp.where(upper, high, low) + got
    for bit in range(grid.shards.bit_length() - 1):
        value = value + grid.move(value, grid.flip_shard(bit))
    if beside is not None:
        value = after(value, beside)
    for bit in reversed(bits):
        got = grid.move(value, grid.flip_rep(bit))
        upper = (rep >> bit) % 2 == 1
        value = jnp.concatenate(
            [jnp.where(upper, got, value), jnp.where(upper, value, got)], axis=1
        )
    return value[:, :columns]


def shards(
    grid,
    tokens,
    cotangent,
    segments,
    positions,
    wide_master,
    square_master,
    key_value_master,
    wide_moment,
    square_moment,
    key_value_momentum,
    wide_error,
    square_error,
    key_value_error,
    wide_factor,
    square_factor,
    key_value_factor,
    norm_gains,
    gain_moment,
):
    reps, owners = grid.reps, grid.shards
    rep = lax.axis_index("rep")
    shard = lax.axis_index("shard")
    core = rep % 2
    turn = (shard >> grid.core_bit) % 2
    logical_shard = shard + (core - turn) * (1 << grid.core_bit)

    low_square = square_master.astype(jnp.bfloat16)
    low_narrow = key_value_master.astype(jnp.bfloat16)
    pieces = []
    for j in range(PAIRS):
        pieces.append(low_square[0, :, 384 * j : 384 * j + 384])
        pieces.append(low_narrow[0, :, 128 * j : 128 * j + 128])
        pieces.append(low_narrow[1, :, 128 * j : 128 * j + 128])
    low_attn = jnp.concatenate(pieces + [low_square[1]], axis=1)
    units = wide_master.shape[2] // 3

    position = grid.swap_rows(positions)[0]
    rows = low_attn.shape[0]
    tile = units // reps
    chained = 1 if rows % 16 == 0 else 0
    gain_row = norm_gains.astype(jnp.bfloat16).reshape(1, 2 * rows)
    gain_row = jnp.pad(gain_row, ((0, 15), (0, 1024 - 2 * rows)))
    first = lax.dynamic_slice_in_dim(low_attn, core * 1024, 1024, axis=1)
    first = jnp.concatenate([first, gain_row], axis=0)
    second = lax.dynamic_slice_in_dim(low_attn, 2048 + core * 512, 512, axis=1)
    picks = [core * (reps // 2) + i for i in range(reps // 2)] if chained else []
    groups = [tuple(range(len(picks)))] if chained else []
    for k in range(chained, 3):
        groups.append((len(picks),))
        picks.append(reps * k + rep)
    cuts = list(pack_wide(wide_master, jnp.stack(picks).astype(jnp.int32), groups, tile))
    if chained:
        second = jnp.concatenate([second, cuts[0]], axis=1)
    mine, gathering = gather_pieces(grid, [first, second])
    other = [grid.move(mine[0], grid.flip_rep(0))]
    places = jnp.array(grid.places(), jnp.int32)[jnp.arange(owners) ^ shard]
    cores = core[None]
    gain_w = mine[0][:, rows, : 2 * rows].reshape(owners, 2, rows)
    gain_w = jnp.take(gain_w, places, axis=0).transpose(1, 0, 2).reshape(2, -1).astype(jnp.float32)
    natural = jnp.arange(reps, dtype=jnp.int32)
    whole = jnp.zeros((1,), jnp.int32)
    moved_tokens = grid.move(after(tokens, gathering[1]), grid.swapped)
    tokens = jnp.where(grid.stays(), tokens, moved_tokens)[0]
    moved_out = grid.move(after(cotangent, moved_tokens), grid.swapped)
    model = gain_w.shape[1]
    columns = 640 * PAIRS
    qkv_w = assemble(rows, mine[:1], other[:1], places, cores, 0, columns)

    count = tokens.shape[0]
    hidden_in = tokens.astype(jnp.float32)
    gain_attn, gain_mlp = gain_w[0], gain_w[1]
    cos, sin = rotary_tables(position, HEAD_SIZE)
    cos = jnp.concatenate([cos] * 4, axis=1)
    sin = jnp.concatenate([-sin, sin] * 2, axis=1)
    place = position[:, None]
    order = jnp.array(grid.masks(), jnp.int32) ^ logical_shard

    qkv, turned_in = project_qkv(order, tokens, gain_attn[None], qkv_w, cos, sin)
    held, got = after((mine[1], gathering[-1]), qkv)
    mine[1] = jnp.concatenate([held, got], axis=0)
    qkv = after(qkv, mine[1])
    wide_parts = [None] * chained
    for k in range(chained, 3):
        part = after(cuts[k], mine[1])
        part = lax.all_gather(part, ("rep", "shard"), axis=0, tiled=True)
        wide_parts.append((natural, whole, [part.reshape(reps, owners * rows, 3 * tile)]))
    other.append(grid.move(mine[1], grid.flip_rep(0)))
    attended, logs = attend_forward(qkv, place)
    other[1] = after(other[1], attended)
    d_out = jnp.where(grid.stays(), cotangent, after(moved_out, attended))[0]
    if chained:
        slots = (natural + core * (reps // 2)) % reps
        wide_parts[0] = (slots, places, [mine[1], other[1]])
        residual, normed_mid, turned_mid, out_w = project_out(
            places,
            cores,
            order,
            attended,
            tokens,
            gain_mlp[None],
            [mine[0], other[0], mine[1], other[1]],
        )
    else:
        out_w = assemble(rows, mine, other, places, cores, columns, 3072)
        residual = hidden_in + jnp.einsum(
            "tn,dn->td", attended, out_w, preferred_element_type=jnp.float32
        )
        normed_mid = normed(residual, gain_mlp).astype(jnp.bfloat16)
        turned_mid = turn_rows(normed_mid, order)
    turned_out = turn_rows(d_out, order)

    half = model // 2

    def weight_grad(turned, right):
        return Sums(
            grid,
            jnp.dot(turned[:half], right, preferred_element_type=jnp.float32).astype(jnp.bfloat16),
            jnp.dot(turned[half:], right, preferred_element_type=jnp.float32).astype(jnp.bfloat16),
        )

    wide_sums = []
    result, d_mid = residual, None
    for k in range(3):
        slots, where, weights = wide_parts[k]
        away, home, result, d_mid = mlp_part(
            reps,
            slots,
            where,
            normed_mid,
            d_out,
            turned_mid,
            turned_out,
            weights,
            result,
            d_mid,
            k == 2,
        )
        wide_sums.append(Sums(grid, away, home))
        for earlier in wide_sums[max(0, k - 2) : k]:
            d_mid, result = after((d_mid, result), earlier.step(away))
    result = grid.swap_rows(result[None])

    _, mid_back = jax.vjp(normed, residual, gain_mlp)
    d_residual, grad_gain_mlp = mid_back(d_mid)
    d_residual = d_residual + d_out.astype(jnp.float32)
    d_branch = d_residual.astype(jnp.bfloat16)
    d_attended = jnp.einsum(
        "td,dn->tn", d_branch, out_w, preferred_element_type=jnp.float32
    ).astype(jnp.bfloat16)
    out_sums = weight_grad(turn_rows(d_branch, order), attended)

    d_attended = after(d_attended, wide_sums[2].step(out_sums.away), wide_sums[0].got)
    d_stacks, pair_sums = [], []
    hold = len(grid.order) == 3
    for j in range(PAIRS):
        d_stack, away, home = attend_backward(
            qkv, d_attended, logs, place, cos, sin, turned_in, j
        )
        d_stacks.append(d_stack)
        pair_sums.append(Sums(grid, away, home))
        if j == 0:
            done = (wide_sums[1].step(d_stack), out_sums.step(d_stack), result)
        elif j == 1:
            done = (
                wide_sums[2].step(d_stack),
                out_sums.step(d_stack),
                pair_sums[0].step(d_stack),
                wide_sums[1].got,
            )
        else:
            done = (pair_sums[0].step(d_stack, hold), pair_sums[1].step(d_stack), out_sums.got)
        d_attended = after(d_attended, done, pair_sums[j].away)
        d_stacks = after(d_stacks, done, pair_sums[j].away)
    def back(j):
        return jnp.einsum(
            "tn,dn->td",
            d_stacks[j],
            qkv_w[:, 640 * j : 640 * j + 640],
            preferred_element_type=jnp.float32,
        )

    flag = grid.stays().astype(jnp.int32)[None]
    d_first = back(0) + back(1)
    d_stacks, wide_got = after(
        (d_stacks, wide_sums[2].got), pair_sums[2].step(d_first), pair_sums[1].step(d_first, hold)
    )
    wide_sums[2].got = wide_got
    spans = [(j, 0) for j in range(PAIRS)]
    late_sums = pair_sums
    if hold:
        pair_sums[0].join(pair_sums[1])
        spans = [(0, 0), (0, 640), (1, 0)]
        late_sums = [pair_sums[0], pair_sums[2]]
    mixed_wide, left_wide = mix_wide(
        flag, [part.result(d_first) for part in wide_sums], wide_error, wide_factor
    )
    mixed_out, left_out = mix_rest(
        flag,
        [out_sums.result(d_first)],
        [[(0, 0, model)]],
        [square_error[0, 1]],
        [square_factor[1]],
    )
    last_step = pair_sums[2].step(left_wide)
    d_stacks = after(d_stacks, last_step, left_out)
    d_normed_in = d_first + back(2)
    rep_moves = [grid.flip_rep(b) for b in range(reps.bit_length() - 1)]
    unit = 128 * reps
    left_early = butterfly(grid, jnp.concatenate([left_wide, left_out], axis=0), rep_moves)
    left_early = after(left_early, last_step)
    gram_early = 9 * units + model
    width = -(-(gram_early + 512) // unit) * unit
    early = contract_all(left_early, [mixed_wide, mixed_out], width)
    d_normed_in = after(d_normed_in, early)
    _, in_back = jax.vjp(normed, hidden_in, gain_attn)
    d_input, grad_gain_attn = in_back(d_normed_in)
    d_input = (d_input + d_residual).astype(jnp.bfloat16)
    early = sum_all(grid, early)
    late = d_input
    d_input = grid.swap_rows(d_input[None])
    narrow = 128 * PAIRS

    mixed_query, mixed_key, mixed_value, left_late = mix_rest(
        flag,
        [part.result(late) for part in late_sums],
        [
            [(which, at + first, at + last) for which, at in spans]
            for first, last in ((0, 384), (384, 512), (512, 640))
        ],
        [square_error[0, 0], key_value_error[0, 0], key_value_error[0, 1]],
        [square_factor[0], key_value_factor[0], key_value_factor[1]],
    )
    left_late = butterfly(grid, left_late, rep_moves)
    gram_late = columns
    gain_at = gram_late + 384
    width = -(-(gain_at + model) // unit) * unit
    gain_grad = jnp.stack([grad_gain_attn, grad_gain_mlp])
    mixed_late = [mixed_query, mixed_key, mixed_value]
    left_late = after(left_late, late)
    summed = contract_all(left_late, mixed_late, width, gain_grad)
    wide_new, wide_moment_new, wide_error_new, factor_wide = finish_wide(
        reps, early, gram_early, left_early, mixed_wide, wide_moment, wide_master
    )
    shard_moves = [grid.flip_shard(b) for b in range(owners.bit_length() - 1)]
    summed = butterfly(grid, summed, shard_moves[1:] + rep_moves[:1])
    summed = after(summed, wide_new)
    summed = butterfly(grid, summed, rep_moves[1:] + shard_moves[:1])
    (
        square_new,
        square_moment_new,
        square_error_new,
        factor_square,
        narrow_new,
        narrow_moment_new,
        narrow_error_new,
        factor_narrow,
    ) = finish_rest(
        reps,
        [summed, early],
        [left_late, left_early],
        [mixed_query, mixed_out, mixed_key, mixed_value],
        [
            (0, 0, gram_late, 0),
            (1, 9 * units, gram_early + 384, 24),
            (0, model, gram_late + 128, 8),
            (0, model + narrow, gram_late + 256, 16),
        ],
        [
            (square_moment, square_master, rate_square),
            (key_value_momentum, key_value_master, rate_narrow),
        ],
    )
    gain_total = lax.dynamic_slice_in_dim(
        summed[:2, gain_at : gain_at + model], shard * (model // owners), model // owners, axis=1
    )
    gain_moment_new = decay_rate * gain_moment + gain_total / reps
    gains_new = norm_gains - rate_gains * gain_moment_new
    return (
        result,
        d_input,
        wide_new,
        square_new,
        narrow_new,
        wide_moment_new,
        square_moment_new,
        narrow_moment_new,
        wide_error_new,
        square_error_new,
        narrow_error_new,
        factor_wide,
        factor_square,
        factor_narrow,
        gains_new,
        gain_moment_new,
    )


def solution(mesh):
    return jax.shard_map(
        functools.partial(shards, Grid(mesh)),
        mesh=mesh,
        in_specs=(
            P(("rep", "shard"), None, None),
            P(("rep", "shard"), None, None),
            P(("rep", "shard"), None),
            P(("rep", "shard"), None),
            P(None, "shard", None),
            P(None, "shard", None),
            P(None, "shard", None),
            P(None, "shard", None),
            P(None, "shard", None),
            P(None, "shard", None),
            P("rep", None, "shard", None),
            P("rep", None, "shard", None),
            P("rep", None, "shard", None),
            P(),
            P(),
            P(),
            P(None, "shard"),
            P(None, "shard"),
        ),
        out_specs=(
            P(("rep", "shard"), None, None),
            P(("rep", "shard"), None, None),
            P(None, "shard", None),
            P(None, "shard", None),
            P(None, "shard", None),
            P(None, "shard", None),
            P(None, "shard", None),
            P(None, "shard", None),
            P("rep", None, "shard", None),
            P("rep", None, "shard", None),
            P("rep", None, "shard", None),
            P(),
            P(),
            P(),
            P(None, "shard"),
            P(None, "shard"),
        ),
        check_vma=False,
    )
```
